32 devices in a mesh: dp: 8 (over z, core), tensor: 4 (over y, x).
Axes of the slice: x: 2, y: 2, z: 4, core: 2. Of those that a mesh axis runs over, the one named last changes fastest.
Arguments:
- hidden_in: bfloat16 [8192, 2048], P('dp'), may hold values from -6 to 6
- self_out: bfloat16 [8192, 2048], P('dp'), may hold values from -6 to 6
- out_grad: bfloat16 [8192, 2048], P('dp'), may hold values from -6 to 6
- lengths: int32 [8], P('dp'), may hold values from 256 to 1024, as said below
- w_query: bfloat16 [2048, 2048], P('dp', 'tensor'), may hold values from -0.125 to 0.125
- w_key: bfloat16 [2048, 2048], P('dp', 'tensor'), may hold values from -0.125 to 0.125
- w_value: bfloat16 [2048, 2048], P('dp', 'tensor'), may hold values from -0.125 to 0.125
- w_output: bfloat16 [2048, 2048], P('tensor', 'dp'), may hold values from -0.5 to 0.5
- w_gate: bfloat16 [2048, 5504], P('dp', 'tensor'), may hold values from -0.125 to 0.125
- w_up: bfloat16 [2048, 5504], P('dp', 'tensor'), may hold values from -0.125 to 0.125
- w_down: bfloat16 [5504, 2048], P('tensor', 'dp'), may hold values from -0.078125 to 0.078125
- attn_gain: bfloat16 [2048], P('dp'), may hold values from 0.099609375 to 1.8984375
- ffn_gain: bfloat16 [2048], P('dp'), may hold values from 0.099609375 to 1.8984375
- kv_gain: bfloat16 [2048], P('dp'), may hold values from 0.099609375 to 1.8984375
Outputs:
- layer_out: bfloat16 [8192, 2048], P('dp')
- input_grad: float32 [8192, 2048], P('dp')
- self_grad: float32 [8192, 2048], P('dp')
- grad_query: float32 [2048, 2048], P('dp', 'tensor')
- grad_key: float32 [2048, 2048], P('dp', 'tensor')
- grad_value: float32 [2048, 2048], P('dp', 'tensor')
- grad_output: float32 [2048, 2048], P('tensor', 'dp')
- grad_gate: float32 [2048, 5504], P('dp', 'tensor')
- grad_up: float32 [2048, 5504], P('dp', 'tensor')
- grad_down: float32 [5504, 2048], P('tensor', 'dp')
- grad_attn_gain: float32 [2048], P('dp')
- grad_ffn_gain: float32 [2048], P('dp')
- grad_kv_gain: float32 [2048], P('dp')
The draws below stay inside these ranges and needn't reach their ends.
Inputs may be any that keep to these rules, and one draw needn't show every extreme that they name: `lengths`: each sequence has 256 to 1024 live tokens; in every draw one sequence is exactly 1024 long.
All inputs are finite; a program needn't handle non-finite values.
Results may differ from the reference program's by a relative error of at most 0.023.
Values may be sent and summed in bfloat16 or wider, within the bound.
No kernel may reach another device: no remote copies, remote signals or barrier semaphores. Data moves between devices by JAX's collectives and lax.ppermute only.
A program may use at most 256 MiB of HBM per device.

```python
import jax
import jax.numpy as jnp
from jax import lax

D = 2048
H = 16
HD = 128
FF = 5504
SLOT = 1024
SEQS = 8
TOKENS = 8192
QBLOCK = 512


def draw_lengths(key, part):
    key = jax.random.fold_in(key, 7)
    draw_key, pick_key = jax.random.split(key)
    drawn = jax.random.randint(draw_key, (SEQS,), SLOT // 4, SLOT + 1)
    chosen = jax.random.randint(pick_key, (), 0, SEQS)
    return jnp.where(jnp.arange(SEQS) == chosen, SLOT, drawn).astype(jnp.int32)


def steps_of(rng, dims, cuts, low, largest):
    level = 1.0
    for axis_at, blocks in cuts:
        draws = jax.random.uniform(jax.random.fold_in(jax.random.fold_in(rng, 6), axis_at), (blocks,), jnp.float32, low / len(cuts), largest / len(cuts))
        level = level * jnp.repeat(jnp.exp(draws), dims[axis_at] // blocks).reshape((-1,) + (1,) * (len(dims) - 1 - axis_at))
    return level


def scatter_about(key, dims, scale, bound, pieces=(), kind=jnp.bfloat16):
    factor_of = steps_of(key, dims, pieces, -0.22, 0.18) if pieces else 1.0
    values = jax.random.normal(key, dims, jnp.float32) * scale * factor_of
    return jnp.minimum(jnp.maximum(values, -bound), bound).astype(kind)


def setup_inputs(seed: int = 0) -> dict:
    keys = jax.random.split(jax.random.key(seed), 15)
    return {
        "hidden_in": scatter_about(keys[0], (TOKENS, D), 1.0, 6.0, ((0, 8),)),
        "self_out": scatter_about(keys[1], (TOKENS, D), 1.0, 6.0, ((0, 8),)),
        "out_grad": scatter_about(keys[2], (TOKENS, D), 1.0, 6.0, ((0, 8),)),
        "lengths": draw_lengths(jax.random.fold_in(keys[14], 71), 0),
        "w_query": scatter_about(keys[4], (D, D), D ** -0.5, 0.125, ((0, 8), (1, 4))),
        "w_key": scatter_about(keys[5], (D, D), D ** -0.5, 0.125, ((0, 8), (1, 4))),
        "w_value": scatter_about(keys[6], (D, D), D ** -0.5, 0.125, ((0, 8), (1, 4))),
        "w_output": scatter_about(keys[7], (D, D), (D // 16) ** -0.5, 0.5, ((0, 4), (1, 8))),
        "w_gate": scatter_about(keys[8], (D, FF), D ** -0.5, 0.125, ((0, 8), (1, 4))),
        "w_up": scatter_about(keys[9], (D, FF), D ** -0.5, 0.125, ((0, 8), (1, 4))),
        "w_down": scatter_about(keys[10], (FF, D), FF ** -0.5, 0.078125, ((0, 4), (1, 8))),
        "attn_gain": jnp.clip(1.0 + 0.18 * jax.random.normal(keys[11], (D,), jnp.float32), 0.099609375, 1.8984375).astype(jnp.bfloat16),
        "ffn_gain": jnp.clip(1.0 + 0.18 * jax.random.normal(keys[12], (D,), jnp.float32), 0.099609375, 1.8984375).astype(jnp.bfloat16),
        "kv_gain": jnp.clip(1.0 + 0.18 * jax.random.normal(keys[13], (D,), jnp.float32), 0.099609375, 1.8984375).astype(jnp.bfloat16),
    }


@jax.custom_vjp
def low(v):
    return lax.optimization_barrier(v.astype(jnp.bfloat16)).astype(jnp.float32)

@jax.custom_vjp
def low_back(v):
    return v

def low_keep(v):
    return (low(v), None)

def low_pass(kept, grad):
    return (grad,)

def back_keep(v):
    return (v, None)

def back_low(kept, grad):
    return (low(grad),)
low.defvjp(low_keep, low_pass)
low_back.defvjp(back_keep, back_low)
epsilon = 1e-06
highest = lax.Precision.HIGHEST

def matmul(left, right):
    return jnp.dot(left, right, precision=highest)

def scale_norm(values, gain):
    return values * lax.rsqrt(lax.optimization_barrier(jnp.mean(values * values, axis=-1, keepdims=True)) + epsilon) * gain

def rotary_tables():
    position = jnp.arange(SLOT, dtype=jnp.float32)
    freqs = jnp.exp(-jnp.log(10000.0) * jnp.arange(HD // 2, dtype=jnp.float32) * 2.0 / HD)
    angle = position[:, None] * freqs[None, :]
    return (jnp.cos(angle)[:, None, :], jnp.sin(angle)[:, None, :])

def rotate(values, cosine, sine):
    middle = values.shape[-1] // 2
    front = values[..., :middle]
    behind = values[..., middle:]
    return jnp.concatenate([front * cosine - behind * sine, front * sine + behind * cosine], axis=-1)

def block_attend(start, queries, keys_rot, values_in, valid):
    rows = lax.dynamic_slice_in_dim(queries, start, QBLOCK, 0)
    scores = jnp.einsum('qhd,khd->hqk', rows, keys_rot, precision=highest) * HD ** (-0.5)
    scores = low_back(scores)
    places = start + jnp.arange(QBLOCK, dtype=jnp.int32)
    allowed = (jnp.arange(SLOT, dtype=jnp.int32)[None, :] <= places[:, None]) & valid[None, :]
    scores = jnp.where(allowed[None], scores, -1e+30)
    weights = low(jax.nn.softmax(scores, axis=-1))
    return jnp.einsum('hqk,khd->qhd', weights, values_in, precision=highest)

def layer(params, hidden, selfout, valid):
    w_query, w_key, w_value, w_output, w_gate, w_up, w_down, attn_gain, ffn_gain, kv_gain = params
    normed = low(scale_norm(hidden, attn_gain))
    kv_normed = low(scale_norm(selfout, kv_gain))
    cosine, sine = rotary_tables()
    queries = low(rotate(low_back(matmul(normed, w_query)).reshape(SLOT, H, HD), cosine, sine))
    keys_rot = low(rotate(low_back(matmul(kv_normed, w_key)).reshape(SLOT, H, HD), cosine, sine))
    values_in = low(low_back(matmul(kv_normed, w_value))).reshape(SLOT, H, HD)
    checked = jax.checkpoint(block_attend)
    starts = jnp.arange(SLOT // QBLOCK, dtype=jnp.int32) * QBLOCK
    blocks = lax.map(lambda start: checked(start, queries, keys_rot, values_in, valid), starts)
    attended = low(low_back(blocks.reshape(SLOT, D)))
    mid = hidden + low_back(matmul(attended, w_output))
    ffn_in = low(scale_norm(mid, ffn_gain))
    gate_pre = low_back(matmul(ffn_in, w_gate))
    up_pre = low_back(matmul(ffn_in, w_up))
    activated = low(jax.nn.silu(gate_pre) * up_pre)
    return mid + low_back(matmul(activated, w_down))

def reference(hidden_in, self_out, out_grad, lengths, w_query, w_key, w_value, w_output, w_gate, w_up, w_down, attn_gain, ffn_gain, kv_gain):
    params = tuple((weight.astype(jnp.float32) for weight in (w_query, w_key, w_value, w_output, w_gate, w_up, w_down, attn_gain, ffn_gain, kv_gain)))
    sequences = (hidden_in.astype(jnp.float32).reshape(SEQS, SLOT, D), self_out.astype(jnp.float32).reshape(SEQS, SLOT, D), out_grad.astype(jnp.float32).reshape(SEQS, SLOT, D), lengths)

    def one_sequence(totals, entry):
        hidden, selfout, cotangent, length = entry
        valid = jnp.arange(SLOT, dtype=jnp.int32) < length
        result, pullback = jax.vjp(lambda weights, left, right: layer(weights, left, right, valid), params, hidden, selfout)
        pulled = pullback(cotangent * valid[:, None].astype(jnp.float32))
        totals = jax.tree.map(jnp.add, totals, pulled[0])
        return (totals, (result, pulled[1], pulled[2]))
    zeros = tuple((jnp.zeros_like(weight) for weight in params))
    grads, (results, input_grads, self_grads) = lax.scan(one_sequence, zeros, sequences)
    return (results.reshape(TOKENS, D).astype(jnp.bfloat16), input_grads.reshape(TOKENS, D), self_grads.reshape(TOKENS, D), grads[0], grads[1], grads[2], grads[3], grads[4], grads[5], grads[6], grads[7], grads[8], grads[9])
```

```python
import jax
import jax.numpy as jnp
from jax import lax
from jax.sharding import PartitionSpec as P

HD = 128
QBLOCK = 512
BF = jnp.bfloat16
F32 = jnp.float32


epsilon = 1e-06


def plain_dot(left, right):
    return jnp.dot(left, right, preferred_element_type=jnp.float32)


def first_dims(left, right):
    return lax.dot_general(
        left, right, (((0,), (0,)), ((), ())), preferred_element_type=jnp.float32
    )


def last_dims(left, right):
    return lax.dot_general(
        left, right, (((1,), (1,)), ((), ())), preferred_element_type=jnp.float32
    )


def rms_scale(values, gain):
    inverse = lax.rsqrt(jnp.mean(values * values, axis=-1, keepdims=True) + epsilon)
    return (inverse, values * inverse * gain)


def norm_back(grad, values, inverse, gain):
    scaled = grad * gain
    inner = jnp.mean(scaled * values, axis=-1, keepdims=True)
    return (
        inverse * scaled - values * inverse**3 * inner,
        jnp.sum(grad * values * inverse, axis=0),
    )


def rotary_tables(length, head_size):
    position = jnp.arange(length, dtype=jnp.float32)
    freqs = jnp.exp(
        -jnp.log(10000.0) * jnp.arange(head_size // 2, dtype=jnp.float32) * 2.0 / head_size
    )
    angle = position[:, None] * freqs[None, :]
    return (jnp.cos(angle)[:, None, :], jnp.sin(angle)[:, None, :])


def rotate(values, cosine, sine):
    middle = values.shape[-1] // 2
    front = values[..., :middle]
    behind = values[..., middle:]
    return jnp.concatenate(
        [front * cosine - behind * sine, front * sine + behind * cosine], axis=-1
    )


def block_scores(start, queries, keys_rot, valid):
    length = keys_rot.shape[0]
    rows = lax.dynamic_slice_in_dim(queries, start, QBLOCK, 0)
    scores = jnp.einsum(
        "qhd,khd->hqk", rows, keys_rot, preferred_element_type=jnp.float32
    ) * queries.shape[2] ** (-0.5)
    places = start + jnp.arange(QBLOCK, dtype=jnp.int32)
    allowed = (jnp.arange(length, dtype=jnp.int32)[None, :] <= places[:, None]) & valid[None, :]
    return (rows, jnp.where(allowed[None], scores, -1e30), allowed)


def attend_forward(queries, keys_rot, values_in, valid):
    length, heads, size = queries.shape
    starts = jnp.arange(length // QBLOCK, dtype=jnp.int32) * QBLOCK

    def one_block(start):
        rows, scores, allowed = block_scores(start, queries, keys_rot, valid)
        largest = jnp.max(scores, axis=-1, keepdims=True)
        expo = jnp.exp(scores - largest)
        totals = jnp.sum(expo, axis=-1, keepdims=True)
        probs = (expo / totals).astype(jnp.bfloat16)
        result = jnp.einsum("hqk,khd->qhd", probs, values_in, preferred_element_type=jnp.float32)
        return (result, (largest + jnp.log(totals))[..., 0])

    results, log_sums = lax.map(one_block, starts)
    return (results.reshape(length, heads, size), log_sums)


def attend_backward(queries, keys_rot, values_in, valid, log_sums, grad_attended):
    length, heads, size = queries.shape
    scale = size ** (-0.5)
    starts = jnp.arange(length // QBLOCK, dtype=jnp.int32) * QBLOCK

    def one_block(carry, entry):
        start, block_sums = entry
        rows, scores, allowed = block_scores(start, queries, keys_rot, valid)
        grad_rows = lax.dynamic_slice_in_dim(grad_attended, start, QBLOCK, 0)
        probs = jnp.where(allowed[None], jnp.exp(scores - block_sums[:, :, None]), 0.0)
        grad_probs = jnp.einsum(
            "qhd,khd->hqk", grad_rows, values_in, preferred_element_type=jnp.float32
        )
        inner = jnp.sum(probs * grad_probs, axis=-1, keepdims=True)
        grad_scores = (probs * (grad_probs - inner)).astype(jnp.bfloat16)
        query_grad = (
            jnp.einsum("hqk,khd->qhd", grad_scores, keys_rot, preferred_element_type=jnp.float32)
            * scale
        )
        key_grad = (
            carry[0]
            + jnp.einsum("hqk,qhd->khd", grad_scores, rows, preferred_element_type=jnp.float32)
            * scale
        )
        value_grad = carry[1] + jnp.einsum(
            "hqk,qhd->khd",
            probs.astype(jnp.bfloat16),
            grad_rows,
            preferred_element_type=jnp.float32,
        )
        return ((key_grad, value_grad), query_grad)

    empty = jnp.zeros(keys_rot.shape, jnp.float32)
    (key_grad, value_grad), query_grad = lax.scan(one_block, (empty, empty), (starts, log_sums))
    return (query_grad.reshape(length, heads, size), key_grad, value_grad)


def swap(array, bit, size):
    return lax.ppermute(array, "tensor", [(t, t ^ bit) for t in range(size)])


def bit_orders(size):
    bits = [1 << step for step in range(size.bit_length() - 1)]
    return (bits, bits[1:] + bits[:1])


def relative(array, me, size):
    part = array.shape[0] // size
    return jnp.stack(
        [lax.dynamic_slice_in_dim(array, (me ^ step) * part, part, 0) for step in range(size)]
    )


def absolute(blocks, me):
    parts = [
        lax.dynamic_index_in_dim(blocks, me ^ step, 0, keepdims=False)
        for step in range(blocks.shape[0])
    ]
    return jnp.concatenate(parts, axis=0)


def scatter_sum(blocks):
    size = blocks.shape[0]
    half = blocks.shape[2] // 2
    sums = []
    for group, order in enumerate(bit_orders(size)):
        held = {
            place: blocks[place, :, group * half : (group + 1) * half].astype(F32)
            for place in range(size)
        }
        for bit in order:
            sent = [place for place in held if place & bit]
            got = swap(jnp.stack([held[place].astype(BF) for place in sent]), bit, size)
            held = {
                place ^ bit: held[place ^ bit] + got[at].astype(F32)
                for at, place in enumerate(sent)
            }
        sums.append(held[0])
    return jnp.concatenate(sums, axis=1)


def gather_rows(own, size):
    half = own.shape[1] // 2
    parts = []
    for group, order in enumerate(bit_orders(size)):
        held = {0: own[:, group * half : (group + 1) * half]}
        for bit in order[::-1]:
            places = list(held)
            got = swap(jnp.stack([held[place] for place in places]), bit, size)
            for at, place in enumerate(places):
                held[place ^ bit] = got[at]
        parts.append(held)
    return jnp.stack(
        [jnp.concatenate([held[place] for held in parts], axis=1) for place in range(size)]
    )


def local(
    hidden_in,
    self_out,
    out_grad,
    lengths,
    w_query,
    w_key,
    w_value,
    w_output,
    w_gate,
    w_up,
    w_down,
    attn_gain,
    ffn_gain,
    kv_gain,
):
    me = lax.axis_index("tensor")
    size = lax.axis_size("tensor")
    dp_size = lax.axis_size("dp")
    gains = lax.all_gather(jnp.stack([attn_gain, ffn_gain, kv_gain]), "dp", axis=1, tiled=True)
    gains = gains.astype(F32)
    attn_scale, ffn_scale, kv_scale = gains[0], gains[1], gains[2]
    wide = w_query.shape[1]
    qkv = lax.all_gather(
        jnp.concatenate([w_query, w_key, w_value], axis=1), "dp", axis=0, tiled=True
    )
    f_query, f_key, f_value = qkv[:, :wide], qkv[:, wide : 2 * wide], qkv[:, 2 * wide :]
    f_output = lax.all_gather(w_output, "dp", axis=1, tiled=True)
    f_gate = lax.all_gather(w_gate, "dp", axis=0, tiled=True)
    f_up = lax.all_gather(w_up, "dp", axis=0, tiled=True)
    f_down = lax.all_gather(w_down, "dp", axis=1, tiled=True)

    hidden = hidden_in.astype(F32)
    selfout = self_out.astype(F32)
    length, width = hidden.shape
    quarter = length // size
    valid = jnp.arange(length, dtype=jnp.int32) < lengths[0]
    heads_here = wide // HD
    x_inverse, x_normed = rms_scale(hidden, attn_scale)
    normed = x_normed.astype(BF)
    s_inverse, s_normed = rms_scale(selfout, kv_scale)
    kv_normed = s_normed.astype(BF)
    cosine, sine = rotary_tables(length, HD)
    queries = rotate(
        plain_dot(normed, f_query).reshape(length, heads_here, HD), cosine, sine
    ).astype(BF)
    keys_rot = rotate(
        plain_dot(kv_normed, f_key).reshape(length, heads_here, HD), cosine, sine
    ).astype(BF)
    values_in = plain_dot(kv_normed, f_value).astype(BF).reshape(length, heads_here, HD)
    attended, log_sums = attend_forward(queries, keys_rot, values_in, valid)
    attended_low = relative(attended.reshape(length, -1).astype(BF), me, size).reshape(length, -1)

    def own_rows(array):
        return lax.dynamic_slice_in_dim(array, me * quarter, quarter, 0)

    hidden_own = own_rows(hidden_in).astype(F32)
    self_own = own_rows(self_out).astype(F32)
    mid_sum = scatter_sum(plain_dot(attended_low, f_output).reshape(size, quarter, width))
    mid = hidden_own + mid_sum
    m_inverse, m_normed = rms_scale(mid, ffn_scale)
    ffn_in = gather_rows(m_normed.astype(BF), size).reshape(length, width)

    grad_y_low = relative(jnp.where(valid[:, None], out_grad, jnp.zeros((), BF)), me, size)
    grad_y = grad_y_low[0].astype(F32)
    grad_y_low = grad_y_low.reshape(length, width)

    gate_pre = plain_dot(ffn_in, f_gate)
    up_pre = plain_dot(ffn_in, f_up)
    sigma = jax.nn.sigmoid(gate_pre)
    activated = (gate_pre * sigma * up_pre).astype(BF)
    grad_down = first_dims(activated, grad_y_low)
    sum_down = lax.psum_scatter(grad_down.astype(BF), "dp", scatter_dimension=1, tiled=True)
    grad_act = last_dims(grad_y_low, f_down)
    grad_gate_pre = (grad_act * up_pre * sigma * (1.0 + gate_pre * (1.0 - sigma))).astype(BF)
    grad_up_pre = (grad_act * gate_pre * sigma).astype(BF)
    back_sum = scatter_sum(
        (last_dims(grad_gate_pre, f_gate) + last_dims(grad_up_pre, f_up)).reshape(
            size, quarter, width
        )
    )
    grad_gate = first_dims(ffn_in, grad_gate_pre)
    sum_gate = lax.psum_scatter(grad_gate.astype(BF), "dp", scatter_dimension=0, tiled=True)
    grad_up = first_dims(ffn_in, grad_up_pre)
    sum_up = lax.psum_scatter(grad_up.astype(BF), "dp", scatter_dimension=0, tiled=True)

    mid_part, grad_ffn_gain = norm_back(back_sum, mid, m_inverse, ffn_scale)
    grad_mid = grad_y + mid_part
    grad_mid_low = gather_rows(grad_mid.astype(BF), size).reshape(length, width)

    out_sum = scatter_sum(plain_dot(activated, f_down).reshape(size, quarter, width))
    layer_out = absolute(gather_rows((mid + out_sum).astype(BF), size), me)

    grad_output = first_dims(attended_low, grad_mid_low)
    sum_output = lax.psum_scatter(grad_output.astype(BF), "dp", scatter_dimension=1, tiled=True)
    grad_attended = absolute(
        last_dims(grad_mid_low, f_output).astype(BF).reshape(size, quarter, -1), me
    ).reshape(length, heads_here, HD)
    query_grad, key_grad, value_grad = attend_backward(
        queries, keys_rot, values_in, valid, log_sums, grad_attended
    )
    grad_q_pre = rotate(query_grad, cosine, -sine).reshape(length, -1).astype(BF)
    grad_k_pre = rotate(key_grad, cosine, -sine).reshape(length, -1).astype(BF)
    grad_v_pre = value_grad.reshape(length, -1).astype(BF)
    rel_q = relative(grad_q_pre, me, size).reshape(length, -1)
    rel_k = relative(grad_k_pre, me, size).reshape(length, -1)
    rel_v = relative(grad_v_pre, me, size).reshape(length, -1)
    grad_normed = scatter_sum(last_dims(rel_q, f_query).reshape(size, quarter, width))
    grad_kv_normed = scatter_sum(
        (last_dims(rel_k, f_key) + last_dims(rel_v, f_value)).reshape(size, quarter, width)
    )
    grad_qkv = jnp.concatenate(
        [
            first_dims(normed, grad_q_pre).astype(BF),
            first_dims(kv_normed, grad_k_pre).astype(BF),
            first_dims(kv_normed, grad_v_pre).astype(BF),
        ],
        axis=1,
    )
    sum_qkv = lax.psum_scatter(grad_qkv, "dp", scatter_dimension=0, tiled=True).astype(F32)
    x_part, grad_attn_gain = norm_back(grad_normed, hidden_own, own_rows(x_inverse), attn_scale)
    s_part, grad_kv_gain = norm_back(grad_kv_normed, self_own, own_rows(s_inverse), kv_scale)
    input_grad = absolute(gather_rows((grad_mid + x_part).astype(BF), size), me).astype(F32)
    self_grad = absolute(gather_rows(s_part.astype(BF), size), me).astype(F32)

    gain_grads = jnp.stack([grad_attn_gain, grad_ffn_gain, grad_kv_gain])
    for bit in bit_orders(size)[0]:
        gain_grads = gain_grads + swap(gain_grads, bit, size)
    place = lax.axis_index("dp")
    piece = width // dp_size

    def gain_piece(step):
        return lax.dynamic_slice_in_dim(gain_grads, ((place + step) % dp_size) * piece, piece, 1)

    total = gain_piece(0)
    for step in range(1, dp_size):
        total = total + lax.ppermute(
            gain_piece(step), "dp", [(i, (i + step) % dp_size) for i in range(dp_size)]
        )
    return (
        layer_out,
        input_grad,
        self_grad,
        sum_qkv[:, :wide],
        sum_qkv[:, wide : 2 * wide],
        sum_qkv[:, 2 * wide :],
        sum_output.astype(F32),
        sum_gate.astype(F32),
        sum_up.astype(F32),
        sum_down.astype(F32),
        total[0],
        total[1],
        total[2],
    )


def solution(mesh):
    placed = (
        P("dp", None),
        P("dp", None),
        P("dp", None),
        P("dp"),
        P("dp", "tensor"),
        P("dp", "tensor"),
        P("dp", "tensor"),
        P("tensor", "dp"),
        P("dp", "tensor"),
        P("dp", "tensor"),
        P("tensor", "dp"),
        P("dp"),
        P("dp"),
        P("dp"),
    )
    return jax.shard_map(
        local,
        mesh=mesh,
        in_specs=placed,
        out_specs=(
            P("dp", None),
            P("dp", None),
            P("dp", None),
            P("dp", "tensor"),
            P("dp", "tensor"),
            P("dp", "tensor"),
            P("tensor", "dp"),
            P("dp", "tensor"),
            P("dp", "tensor"),
            P("tensor", "dp"),
            P("dp"),
            P("dp"),
            P("dp"),
        ),
        check_vma=False,
    )
```

```python
import functools

import jax
import jax.numpy as jnp
from jax import lax
from jax.experimental import pallas as pl
from jax.experimental.pallas import tpu as pltpu
from jax.sharding import PartitionSpec as P

HD = 128
QROWS = 256
BF = jnp.bfloat16
F32 = jnp.float32
epsilon = 1e-06
VMEM_LIMIT = 60 * 1024 * 1024


def plain_dot(left, right):
    return jnp.dot(left, right, preferred_element_type=jnp.float32)


def last_dims(left, right):
    return lax.dot_general(
        left, right, (((1,), (1,)), ((), ())), preferred_element_type=jnp.float32
    )


def round_up(number, unit):
    return (number + unit - 1) // unit * unit


def head_group(wide):
    return 2 * HD if wide % (2 * HD) == 0 else HD


def limits():
    return pltpu.CompilerParams(vmem_limit_bytes=VMEM_LIMIT)


def turn(values, cosine, sine):
    return values * cosine + pltpu.roll(values, HD // 2, 1) * sine


def forward_kernel(
    size,
    place_ref,
    normed_ref,
    kv_ref,
    wq_ref,
    wk_ref,
    wv_ref,
    cos_ref,
    sin_ref,
    q_ref,
    k_ref,
    v_ref,
    out_ref,
    flip_ref,
):
    me, live = place_ref[0], place_ref[1]
    length = normed_ref.shape[0]
    group = wq_ref.shape[1]
    part = length // size
    cosine, sine = cos_ref[...], sin_ref[...]
    q_pre = plain_dot(normed_ref[...], wq_ref[...])
    for at in range(0, group, HD):
        q_ref[:, at : at + HD] = turn(q_pre[:, at : at + HD], cosine, sine).astype(BF)
    k_pre = plain_dot(kv_ref[...], wk_ref[...])
    for at in range(0, group, HD):
        k_ref[:, at : at + HD] = turn(k_pre[:, at : at + HD], cosine, sine).astype(BF)
    v_ref[...] = plain_dot(kv_ref[...], wv_ref[...]).astype(BF)
    for at in range(0, group, HD):
        for start in range(0, length, QROWS):
            stop = start + QROWS
            scores = last_dims(q_ref[start:stop, at : at + HD], k_ref[:stop, at : at + HD])
            scores = scores * HD ** (-0.5)
            rows = start + lax.broadcasted_iota(jnp.int32, (QROWS, 1), 0)
            bound = jnp.minimum(rows, live - 1)
            columns = lax.broadcasted_iota(jnp.int32, (QROWS, stop), 1)
            scores = jnp.where(columns <= bound, scores, -1e30)
            largest = jnp.max(scores, axis=1, keepdims=True)
            expo = jnp.exp(scores - largest)
            probs = (expo / jnp.sum(expo, axis=1, keepdims=True)).astype(BF)
            result = plain_dot(probs, v_ref[:stop, at : at + HD])
            flipped = result.T.astype(BF)
            result = result.astype(BF)
            step = min(part, QROWS)
            for piece in range(0, QROWS, step):
                block = (start + piece) // part
                row = pl.multiple_of((block ^ me) * part, part) + (start + piece) % part
                rows_at = pl.ds(pl.multiple_of(row, 128), step)
                out_ref[rows_at, at : at + HD] = result[piece : piece + step]
                flip_ref[at : at + HD, rows_at] = flipped[:, piece : piece + step]


def attend_forward(place, normed, kv_normed, weights, cosine, sine, size):
    length, width = normed.shape
    wide = weights.shape[1] // 4
    group = head_group(wide)
    groups = wide // group
    whole = pl.BlockSpec((length, width), lambda g: (0, 0))
    table = pl.BlockSpec((length, HD), lambda g: (0, 0))
    heads = pl.BlockSpec((length, group), lambda g: (0, g))
    out = jax.ShapeDtypeStruct((length, wide), BF)
    return pl.pallas_call(
        functools.partial(forward_kernel, size),
        grid=(groups,),
        in_specs=[
            pl.BlockSpec(memory_space=pltpu.SMEM),
            whole,
            whole,
            pl.BlockSpec((width, group), lambda g: (0, g)),
            pl.BlockSpec((width, group), lambda g: (0, g + groups)),
            pl.BlockSpec((width, group), lambda g: (0, g + 2 * groups)),
            table,
            table,
        ],
        out_specs=[heads] * 4 + [pl.BlockSpec((group, length), lambda g: (g, 0))],
        out_shape=[out] * 4 + [jax.ShapeDtypeStruct((wide, length), BF)],
        compiler_params=limits(),
        cost_estimate=pl.CostEstimate(
            flops=6 * length * width * wide + 3 * length * length * wide,
            bytes_accessed=4 * length * width + 6 * width * wide + 8 * length * wide,
            transcendentals=length * length * wide // HD,
        ),
    )(place, normed, kv_normed, weights, weights, weights, cosine, sine)


def backward_kernel(
    size,
    place_ref,
    grad_ref,
    wo_ref,
    q_ref,
    k_ref,
    v_ref,
    cos_ref,
    sin_ref,
    rq_ref,
    rk_ref,
    rv_ref,
    flip_ref,
    ga_ref,
    kt_ref,
    sum_k,
    sum_v,
):
    me, live = place_ref[0], place_ref[1]
    length = grad_ref.shape[0]
    group = wo_ref.shape[1]
    part = length // size
    scale = HD ** (-0.5)
    cosine, sine = cos_ref[...], -sin_ref[...]

    def home(row):
        block = row // part
        return pl.multiple_of(pl.multiple_of((block ^ me) * part, part) + row % part, 128)

    for block in range(size):
        ga_ref[pl.ds(home(block * part), part), :] = plain_dot(
            grad_ref[block * part : (block + 1) * part, :], wo_ref[...]
        ).astype(BF)
    step = min(part, QROWS)
    for at in range(0, group, HD):
        kt_ref[...] = k_ref[:, at : at + HD].T
        for start in reversed(range(0, length, QROWS)):
            stop = start + QROWS
            queries = q_ref[start:stop, at : at + HD]
            grads = ga_ref[start:stop, at : at + HD]
            scores = last_dims(k_ref[:stop, at : at + HD], queries) * scale
            columns = start + lax.broadcasted_iota(jnp.int32, (1, QROWS), 1)
            bound = jnp.minimum(columns, live - 1)
            rows = lax.broadcasted_iota(jnp.int32, (stop, QROWS), 0)
            scores = jnp.where(rows <= bound, scores, -1e30)
            largest = jnp.max(scores, axis=0, keepdims=True)
            expo = jnp.exp(scores - largest)
            probs = expo * (1.0 / jnp.sum(expo, axis=0, keepdims=True))
            grad_probs = last_dims(v_ref[:stop, at : at + HD], grads)
            inner = jnp.sum(probs * grad_probs, axis=0, keepdims=True)
            grad_scores = (probs * (grad_probs - inner)).astype(BF)
            add_k = plain_dot(grad_scores, queries)
            add_v = plain_dot(probs.astype(BF), grads)
            if stop == length:
                sum_k[...] = add_k
                sum_v[...] = add_v
            else:
                sum_k[:stop] += add_k
                sum_v[:stop] += add_v
            grad_q = plain_dot(kt_ref[:, :stop], grad_scores).T * scale
            grad_q = turn(grad_q, cosine[start:stop], sine[start:stop])
            flip_ref[0, at : at + HD, start:stop] = grad_q.T.astype(BF)
            grad_q = grad_q.astype(BF)
            for piece in range(0, QROWS, step):
                rq_ref[pl.ds(home(start + piece), step), at : at + HD] = grad_q[
                    piece : piece + step
                ]
        grad_k = turn(sum_k[...] * scale, cosine, sine)
        grad_v = sum_v[...]
        flip_ref[1, at : at + HD, :] = grad_k.T.astype(BF)
        flip_ref[2, at : at + HD, :] = grad_v.T.astype(BF)
        grad_k, grad_v = grad_k.astype(BF), grad_v.astype(BF)
        for block in range(size):
            rows = slice(block * part, (block + 1) * part)
            rk_ref[pl.ds(home(block * part), part), at : at + HD] = grad_k[rows]
            rv_ref[pl.ds(home(block * part), part), at : at + HD] = grad_v[rows]


def attend_backward(place, grad_mid_low, weights, queries, keys, values, cosine, sine, size):
    length, width = grad_mid_low.shape
    wide = queries.shape[1]
    group = head_group(wide)
    groups = wide // group
    table = pl.BlockSpec((length, HD), lambda g: (0, 0))
    heads = pl.BlockSpec((length, group), lambda g: (0, g))
    out = jax.ShapeDtypeStruct((length, wide), BF)
    return pl.pallas_call(
        functools.partial(backward_kernel, size),
        grid=(groups,),
        in_specs=[
            pl.BlockSpec(memory_space=pltpu.SMEM),
            pl.BlockSpec((length, width), lambda g: (0, 0)),
            pl.BlockSpec((width, group), lambda g: (0, g + 3 * groups)),
            heads,
            heads,
            heads,
            table,
            table,
        ],
        out_specs=[heads] * 3 + [pl.BlockSpec((3, group, length), lambda g: (0, g, 0))],
        out_shape=[out] * 3 + [jax.ShapeDtypeStruct((3, wide, length), BF)],
        scratch_shapes=[
            pltpu.VMEM((length, group), BF),
            pltpu.VMEM((HD, length), BF),
            pltpu.VMEM((length, HD), F32),
            pltpu.VMEM((length, HD), F32),
        ],
        compiler_params=limits(),
        cost_estimate=pl.CostEstimate(
            flops=2 * length * width * wide + 10 * length * length * wide,
            bytes_accessed=2 * length * width + 2 * width * wide + 18 * length * wide,
            transcendentals=length * length * wide // HD,
        ),
    )(place, grad_mid_low, weights, queries, keys, values, cosine, sine)


def feed_kernel(x_ref, g_ref, wg_ref, wu_ref, wd_ref, act_ref, gate_ref, up_ref, flip_ref):
    gate = plain_dot(x_ref[...], wg_ref[...])
    up = plain_dot(x_ref[...], wu_ref[...])
    grad = plain_dot(g_ref[...], wd_ref[...])
    sigma = 1.0 / (1.0 + jnp.exp(-gate))
    silu = gate * sigma
    act = silu * up
    grad_up = grad * silu
    grad_gate = grad * up * (sigma + silu * (1.0 - sigma))
    act_ref[...] = act.astype(BF)
    up_ref[...] = grad_up.astype(BF)
    gate_ref[...] = grad_gate.astype(BF)
    flip_ref[0] = grad_gate.T.astype(BF)
    flip_ref[1] = grad_up.T.astype(BF)
    flip_ref[2] = act.T.astype(BF)


def feed_forward(ffn_in, grad_low, weights):
    length, width = ffn_in.shape
    units = weights.shape[1] // 3
    step = 256 if units % 256 == 0 else 128
    steps = units // step
    whole = pl.BlockSpec((length, width), lambda f: (0, 0))
    out = pl.BlockSpec((length, step), lambda f: (0, f))
    return pl.pallas_call(
        feed_kernel,
        grid=(steps,),
        in_specs=[
            whole,
            whole,
            pl.BlockSpec((width, step), lambda f: (0, f)),
            pl.BlockSpec((width, step), lambda f: (0, f + steps)),
            pl.BlockSpec((width, step), lambda f: (0, f + 2 * steps)),
        ],
        out_specs=[out] * 3 + [pl.BlockSpec((3, step, length), lambda f: (0, f, 0))],
        out_shape=[jax.ShapeDtypeStruct((length, units), BF)] * 3
        + [jax.ShapeDtypeStruct((3, units, length), BF)],
        compiler_params=limits(),
        cost_estimate=pl.CostEstimate(
            flops=6 * length * width * units,
            bytes_accessed=4 * length * width + 6 * width * units + 12 * length * units,
            transcendentals=2 * length * units,
        ),
    )(ffn_in, grad_low, weights, weights, weights)


def products_kernel(counts, *refs):
    step = pl.program_id(0)
    lefts, rights, out_ref = refs[: len(counts)], refs[len(counts) : -1], refs[-1]
    first = 0
    for (steps, right), left in zip(counts, lefts):

        @pl.when((step >= first) & (step < first + steps))
        def _(left=left, right=right):
            out_ref[...] = plain_dot(left[...], rights[right][...]).astype(BF)

        first += steps


def products(terms, rights):
    length, width = rights[0].shape
    step = 256 if all(left.shape[1] % 256 == 0 for left, _, _ in terms) else 128
    counts = tuple((left.shape[1] // step, at) for left, _, at in terms)
    total = sum(steps for steps, _ in counts)
    left_specs = []
    first = 0
    for (steps, _), (_, lead, _) in zip(counts, terms):

        def block(i, first=first, last=steps - 1, lead=lead):
            return (lead, lax.max(lax.min(i - first, last), 0), 0)

        left_specs.append(pl.BlockSpec((None, step, length), block))
        first += steps
    return pl.pallas_call(
        functools.partial(products_kernel, counts),
        grid=(total,),
        in_specs=left_specs + [pl.BlockSpec((length, width), lambda i: (0, 0))] * len(rights),
        out_specs=pl.BlockSpec((step, width), lambda i: (i, 0)),
        out_shape=jax.ShapeDtypeStruct((total * step, width), BF),
        compiler_params=limits(),
        cost_estimate=pl.CostEstimate(
            flops=2 * total * step * length * width,
            bytes_accessed=2 * (total * step * (length + width) + len(rights) * length * width),
            transcendentals=0,
        ),
    )(*[left for left, _, _ in terms], *rights)


def rows_kernel(count, *refs):
    out_ref = refs[-1]
    total = None
    for left, right in zip(refs[:count], refs[count:-1]):
        rows = left[...].reshape(-1, left.shape[-1])
        part = last_dims(rows, right[...])
        total = part if total is None else total + part
    out_ref[...] = total.astype(BF).reshape(out_ref.shape)


def row_products(terms, bit, side, half, width):
    columns = width // 2
    step = 512 if columns % 512 == 0 else columns
    left_specs, right_specs, lefts, rights = [], [], [], []
    flops = nbytes = 0
    for left, right, at in terms:
        rows, depth = left.shape[0] // 4, left.shape[1]
        lefts.append(left.reshape(2, 2, rows, depth))
        if bit == 1:
            left_specs.append(pl.BlockSpec((2, 1, rows, depth), lambda j: (0, side, 0, 0)))
        else:
            left_specs.append(pl.BlockSpec((1, 2, rows, depth), lambda j: (side, 0, 0, 0)))
        right_specs.append(
            pl.BlockSpec(
                (step, depth), lambda j, at=at: (half * (columns // step) + j, at)
            )
        )
        rights.append(right)
        flops += 4 * rows * depth * columns
        nbytes += 2 * depth * (2 * rows + columns)
    return pl.pallas_call(
        functools.partial(rows_kernel, len(terms)),
        grid=(columns // step,),
        in_specs=left_specs + right_specs,
        out_specs=pl.BlockSpec((2, rows, step), lambda j: (0, 0, j)),
        out_shape=jax.ShapeDtypeStruct((2, rows, columns), BF),
        compiler_params=limits(),
        cost_estimate=pl.CostEstimate(
            flops=flops, bytes_accessed=nbytes + 4 * rows * columns, transcendentals=0
        ),
    )(*lefts, *rights)


def rms_scale(values, gain):
    inverse = lax.rsqrt(jnp.mean(values * values, axis=-1, keepdims=True) + epsilon)
    return (inverse, values * inverse * gain)


def norm_back(grad, values, inverse, gain):
    scaled = grad * gain
    inner = jnp.mean(scaled * values, axis=-1, keepdims=True)
    return (
        inverse * scaled - values * inverse**3 * inner,
        jnp.sum(grad * values * inverse, axis=0),
    )


def rotary_tables(length):
    position = jnp.arange(length, dtype=jnp.float32)
    freqs = jnp.exp(-jnp.log(10000.0) * jnp.arange(HD // 2, dtype=jnp.float32) * 2.0 / HD)
    angle = position[:, None] * freqs[None, :]
    cosine, sine = jnp.cos(angle), jnp.sin(angle)
    return (jnp.concatenate([cosine, cosine], 1), jnp.concatenate([-sine, sine], 1))


def after(value, *earlier):
    return lax.optimization_barrier((value, *earlier))[0]


def swap(array, bit, size):
    return lax.ppermute(array, "tensor", [(t, t ^ bit) for t in range(size)])


def bit_orders(size):
    bits = [1 << step for step in range(size.bit_length() - 1)]
    return (bits, bits[1:] + bits[:1])


def relative(array, me, size):
    part = array.shape[0] // size
    return jnp.stack(
        [lax.dynamic_slice_in_dim(array, (me ^ step) * part, part, 0) for step in range(size)]
    )


def absolute(blocks, me):
    parts = [
        lax.dynamic_index_in_dim(blocks, me ^ step, 0, keepdims=False)
        for step in range(blocks.shape[0])
    ]
    return jnp.concatenate(parts, axis=0)


def scatter_sum(blocks):
    size = blocks.shape[0]
    half = blocks.shape[2] // 2
    sums = []
    for group, order in enumerate(bit_orders(size)):
        held = {
            place: blocks[place, :, group * half : (group + 1) * half].astype(F32)
            for place in range(size)
        }
        for bit in order:
            sent = [place for place in held if place & bit]
            got = swap(jnp.stack([held[place].astype(BF) for place in sent]), bit, size)
            held = {
                place ^ bit: held[place ^ bit] + got[at].astype(F32)
                for at, place in enumerate(sent)
            }
        sums.append(held[0])
    return jnp.concatenate(sums, axis=1)


def gather_rows(own, size):
    half = own.shape[1] // 2
    parts = []
    for group, order in enumerate(bit_orders(size)):
        held = {0: own[:, group * half : (group + 1) * half]}
        for bit in order[::-1]:
            places = list(held)
            got = swap(jnp.stack([held[place] for place in places]), bit, size)
            for at, place in enumerate(places):
                held[place ^ bit] = got[at]
        parts.append(held)
    return jnp.stack(
        [jnp.concatenate([held[place] for held in parts], axis=1) for place in range(size)]
    )


def product_scatter(terms, size, width):
    if size != 4:
        total = 0.0
        for left, right, at in terms:
            depth = left.shape[1]
            total = total + last_dims(left, right[:, at * depth : (at + 1) * depth])
        return scatter_sum(total.reshape(size, -1, width))
    sent = [row_products(terms, 1 + half, 1, half, width) for half in range(2)]
    got = [swap(sent[half], 1 + half, size).astype(F32) for half in range(2)]
    lefts = after([left for left, _, _ in terms], *sent)
    terms = [(left, right, at) for left, (_, right, at) in zip(lefts, terms)]
    kept = [row_products(terms, 1 + half, 0, half, width).astype(F32) for half in range(2)]
    more = [
        swap((kept[half][1] + got[half][1]).astype(BF), 2 - half, size).astype(F32)
        for half in range(2)
    ]
    return jnp.concatenate([kept[half][0] + got[half][0] + more[half] for half in range(2)], axis=1)


def local(
    hidden_in,
    self_out,
    out_grad,
    lengths,
    w_query,
    w_key,
    w_value,
    w_output,
    w_gate,
    w_up,
    w_down,
    attn_gain,
    ffn_gain,
    kv_gain,
):
    me = lax.axis_index("tensor")
    size = lax.axis_size("tensor")
    dp_size = lax.axis_size("dp")
    length, width = hidden_in.shape
    quarter = length // size
    wide, units = w_query.shape[1], w_gate.shape[1]
    early = round_up(units // 2, 128)
    late = round_up(units - early, 128)

    def columns(array, start, count):
        kept = array[:, start : start + count]
        return jnp.pad(kept, ((0, 0), (0, count - kept.shape[1])))

    w_flip = w_down.T
    mine = [jnp.concatenate([w_query, w_key, w_value, w_output.T], axis=1)]
    for start, count in ((0, early), (early, late)):
        mine.append(
            jnp.concatenate([columns(w, start, count) for w in (w_gate, w_up, w_flip)], axis=1)
        )
    w_heads, w_early, w_late = [lax.all_gather(w, "dp", axis=0, tiled=True) for w in mine]
    gains = lax.all_gather(jnp.stack([attn_gain, ffn_gain, kv_gain]), "dp", axis=1, tiled=True)
    gains = gains.astype(F32)
    attn_scale, ffn_scale, kv_scale = gains[0], gains[1], gains[2]

    place = jnp.stack([me, lengths[0]])
    valid = jnp.arange(length, dtype=jnp.int32) < lengths[0]
    cosine, sine = rotary_tables(length)
    hidden = hidden_in.astype(F32)
    selfout = self_out.astype(F32)
    x_inverse, x_normed = rms_scale(hidden, attn_scale)
    normed = x_normed.astype(BF)
    s_inverse, s_normed = rms_scale(selfout, kv_scale)
    kv_normed = s_normed.astype(BF)

    def own_rows(array):
        return lax.dynamic_slice_in_dim(array, me * quarter, quarter, 0)

    hidden_own = own_rows(hidden_in).astype(F32)
    self_own = own_rows(self_out).astype(F32)
    grad_y_low = relative(jnp.where(valid[:, None], out_grad, jnp.zeros((), BF)), me, size)
    grad_y = grad_y_low[0].astype(F32)
    grad_y_low = grad_y_low.reshape(length, width)

    queries, keys, values, attended_low, attended_flip = attend_forward(
        place, normed, kv_normed, w_heads, cosine, sine, size
    )
    mid_sum = product_scatter([(attended_low, w_heads, 3)], size, width)
    mid = hidden_own + mid_sum
    m_inverse, m_normed = rms_scale(mid, ffn_scale)
    ffn_in = gather_rows(m_normed.astype(BF), size).reshape(length, width)

    act_early, gate_early, up_early, flip_early = feed_forward(ffn_in, grad_y_low, w_early)

    def unit_grads(flip):
        return products([(flip, 0, 0), (flip, 1, 0), (flip, 2, 1)], [ffn_in, grad_y_low])

    grads_early = unit_grads(flip_early)
    sum_early = lax.psum_scatter(grads_early, "dp", scatter_dimension=1, tiled=True)
    act_late, gate_late, up_late, flip_late = feed_forward(
        after(ffn_in, grads_early), grad_y_low, w_late
    )
    back_sum = product_scatter(
        [
            (gate_early, w_early, 0),
            (up_early, w_early, 1),
            (gate_late, w_late, 0),
            (up_late, w_late, 1),
        ],
        size,
        width,
    )
    grads_late = unit_grads(flip_late)
    sum_late = lax.psum_scatter(grads_late, "dp", scatter_dimension=1, tiled=True)

    mid_part, grad_ffn_gain = norm_back(back_sum, mid, m_inverse, ffn_scale)
    grad_mid = grad_y + mid_part
    grad_mid_low = gather_rows(grad_mid.astype(BF), size).reshape(length, width)

    out_sum = product_scatter([(act_early, w_early, 2), (act_late, w_late, 2)], size, width)
    layer_out = absolute(gather_rows((mid + out_sum).astype(BF), size), me)

    rel_q, rel_k, rel_v, flip_heads = attend_backward(
        place, grad_mid_low, w_heads, queries, keys, values, cosine, sine, size
    )
    grad_kv_normed = product_scatter([(rel_k, w_heads, 1), (rel_v, w_heads, 2)], size, width)
    grad_normed = product_scatter([(rel_q, w_heads, 0)], size, width)
    grads_heads = products(
        [(flip_heads, 0, 0), (flip_heads, 1, 1), (flip_heads, 2, 1), (attended_flip[None], 0, 2)],
        [normed, kv_normed, after(grad_mid_low, sum_early)],
    )
    sum_heads = lax.psum_scatter(grads_heads, "dp", scatter_dimension=1, tiled=True).astype(F32)
    x_part, grad_attn_gain = norm_back(grad_normed, hidden_own, own_rows(x_inverse), attn_scale)
    s_part, grad_kv_gain = norm_back(grad_kv_normed, self_own, own_rows(s_inverse), kv_scale)
    self_grad = absolute(gather_rows(s_part.astype(BF), size), me).astype(F32)
    input_grad = absolute(gather_rows((grad_mid + x_part).astype(BF), size), me).astype(F32)

    gain_grads = jnp.stack([grad_attn_gain, grad_ffn_gain, grad_kv_gain])
    for bit in bit_orders(size)[0]:
        gain_grads = gain_grads + swap(gain_grads, bit, size)
    place = lax.axis_index("dp")
    piece = width // dp_size

    def gain_piece(step):
        return lax.dynamic_slice_in_dim(gain_grads, ((place + step) % dp_size) * piece, piece, 1)

    total = gain_piece(0)
    for step in range(1, dp_size):
        total = total + lax.ppermute(
            gain_piece(step), "dp", [(i, (i + step) % dp_size) for i in range(dp_size)]
        )
    def unit_sums(at):
        early_rows = sum_early[at * early : (at + 1) * early]
        late_rows = sum_late[at * late : at * late + units - early]
        return jnp.concatenate([early_rows, late_rows], axis=0).astype(F32)

    return (
        layer_out,
        input_grad,
        self_grad,
        sum_heads[:wide].T,
        sum_heads[wide : 2 * wide].T,
        sum_heads[2 * wide : 3 * wide].T,
        sum_heads[3 * wide :],
        unit_sums(0).T,
        unit_sums(1).T,
        unit_sums(2),
        total[0],
        total[1],
        total[2],
    )


def solution(mesh):
    placed = (
        P("dp", None),
        P("dp", None),
        P("dp", None),
        P("dp"),
        P("dp", "tensor"),
        P("dp", "tensor"),
        P("dp", "tensor"),
        P("tensor", "dp"),
        P("dp", "tensor"),
        P("dp", "tensor"),
        P("tensor", "dp"),
        P("dp"),
        P("dp"),
        P("dp"),
    )
    return jax.shard_map(
        local,
        mesh=mesh,
        in_specs=placed,
        out_specs=(
            P("dp", None),
            P("dp", None),
            P("dp", None),
            P("dp", "tensor"),
            P("dp", "tensor"),
            P("dp", "tensor"),
            P("tensor", "dp"),
            P("dp", "tensor"),
            P("dp", "tensor"),
            P("tensor", "dp"),
            P("dp"),
            P("dp"),
            P("dp"),
        ),
        check_vma=False,
    )
```

```python
import functools

import jax
import jax.numpy as jnp
from jax import lax
from jax.experimental import pallas as pl
from jax.experimental.pallas import tpu as pltpu
from jax.sharding import PartitionSpec as P

HD = 128
QROWS = 256
BF = jnp.bfloat16
F32 = jnp.float32
epsilon = 1e-06
VMEM_LIMIT = 60 * 1024 * 1024
WEIGHT = 1


def plain_dot(left, right):
    return jnp.dot(left, right, preferred_element_type=jnp.float32)


def last_dims(left, right):
    return lax.dot_general(
        left, right, (((1,), (1,)), ((), ())), preferred_element_type=jnp.float32
    )


def round_up(number, unit):
    return (number + unit - 1) // unit * unit


def head_group(wide):
    return 2 * HD if wide % (2 * HD) == 0 else HD


def limits():
    return pltpu.CompilerParams(vmem_limit_bytes=VMEM_LIMIT)


def estimate(flops, bytes_accessed, transcendentals):
    return pl.CostEstimate(
        flops=flops // WEIGHT,
        bytes_accessed=bytes_accessed // WEIGHT,
        transcendentals=transcendentals // WEIGHT,
    )


def turn(values, cosine, sine):
    return values * cosine + pltpu.roll(values, HD // 2, 1) * sine


def forward_kernel(
    size,
    place_ref,
    normed_ref,
    kv_ref,
    wq_ref,
    wk_ref,
    wv_ref,
    cos_ref,
    sin_ref,
    q_ref,
    k_ref,
    v_ref,
    out_ref,
    flip_ref,
):
    me, live = place_ref[0], place_ref[1]
    length = normed_ref.shape[0]
    group = wq_ref.shape[1]
    part = length // size
    cosine, sine = cos_ref[...], sin_ref[...]
    q_pre = plain_dot(normed_ref[...], wq_ref[...])
    for at in range(0, group, HD):
        q_ref[:, at : at + HD] = turn(q_pre[:, at : at + HD], cosine, sine).astype(BF)
    k_pre = plain_dot(kv_ref[...], wk_ref[...])
    for at in range(0, group, HD):
        k_ref[:, at : at + HD] = turn(k_pre[:, at : at + HD], cosine, sine).astype(BF)
    v_ref[...] = plain_dot(kv_ref[...], wv_ref[...]).astype(BF)
    for at in range(0, group, HD):
        for start in range(0, length, QROWS):
            stop = start + QROWS
            scores = last_dims(q_ref[start:stop, at : at + HD], k_ref[:stop, at : at + HD])
            scores = scores * HD ** (-0.5)
            rows = start + lax.broadcasted_iota(jnp.int32, (QROWS, 1), 0)
            bound = jnp.minimum(rows, live - 1)
            columns = lax.broadcasted_iota(jnp.int32, (QROWS, stop), 1)
            scores = jnp.where(columns <= bound, scores, -1e30)
            largest = jnp.max(scores, axis=1, keepdims=True)
            expo = jnp.exp(scores - largest)
            probs = (expo / jnp.sum(expo, axis=1, keepdims=True)).astype(BF)
            result = plain_dot(probs, v_ref[:stop, at : at + HD])
            flipped = result.T.astype(BF)
            result = result.astype(BF)
            step = min(part, QROWS)
            for piece in range(0, QROWS, step):
                block = (start + piece) // part
                row = pl.multiple_of((block ^ me) * part, part) + (start + piece) % part
                rows_at = pl.ds(pl.multiple_of(row, 128), step)
                out_ref[rows_at, at : at + HD] = result[piece : piece + step]
                flip_ref[at : at + HD, rows_at] = flipped[:, piece : piece + step]


def attend_forward(place, normed, kv_normed, weights, cosine, sine, size):
    length, width = normed.shape
    wide = weights.shape[1] // 4
    group = head_group(wide)
    groups = wide // group
    whole = pl.BlockSpec((length, width), lambda g: (0, 0))
    table = pl.BlockSpec((length, HD), lambda g: (0, 0))
    heads = pl.BlockSpec((length, group), lambda g: (0, g))
    out = jax.ShapeDtypeStruct((length, wide), BF)
    return pl.pallas_call(
        functools.partial(forward_kernel, size),
        grid=(groups,),
        in_specs=[
            pl.BlockSpec(memory_space=pltpu.SMEM),
            whole,
            whole,
            pl.BlockSpec((width, group), lambda g: (0, g)),
            pl.BlockSpec((width, group), lambda g: (0, g + groups)),
            pl.BlockSpec((width, group), lambda g: (0, g + 2 * groups)),
            table,
            table,
        ],
        out_specs=[heads] * 4 + [pl.BlockSpec((group, length), lambda g: (g, 0))],
        out_shape=[out] * 4 + [jax.ShapeDtypeStruct((wide, length), BF)],
        compiler_params=limits(),
        cost_estimate=estimate(
            flops=6 * length * width * wide + 3 * length * length * wide,
            bytes_accessed=4 * length * width + 6 * width * wide + 8 * length * wide,
            transcendentals=length * length * wide // HD,
        ),
    )(place, normed, kv_normed, weights, weights, weights, cosine, sine)


def backward_kernel(
    size,
    place_ref,
    grad_ref,
    wo_ref,
    q_ref,
    k_ref,
    v_ref,
    cos_ref,
    sin_ref,
    gq_ref,
    rk_ref,
    rv_ref,
    flip_ref,
    ga_ref,
    kt_ref,
    sum_k,
    sum_v,
):
    me, live = place_ref[0], place_ref[1]
    length = grad_ref.shape[0]
    group = wo_ref.shape[1]
    part = length // size
    scale = HD ** (-0.5)
    cosine, sine = cos_ref[...], -sin_ref[...]

    def home(row):
        block = row // part
        return pl.multiple_of(pl.multiple_of((block ^ me) * part, part) + row % part, 128)

    for block in range(size):
        ga_ref[pl.ds(home(block * part), part), :] = plain_dot(
            grad_ref[block * part : (block + 1) * part, :], wo_ref[...]
        ).astype(BF)
    for at in range(0, group, HD):
        kt_ref[...] = k_ref[:, at : at + HD].T
        for start in reversed(range(0, length, QROWS)):
            stop = start + QROWS
            queries = q_ref[start:stop, at : at + HD]
            grads = ga_ref[start:stop, at : at + HD]
            scores = last_dims(k_ref[:stop, at : at + HD], queries) * scale
            columns = start + lax.broadcasted_iota(jnp.int32, (1, QROWS), 1)
            bound = jnp.minimum(columns, live - 1)
            rows = lax.broadcasted_iota(jnp.int32, (stop, QROWS), 0)
            scores = jnp.where(rows <= bound, scores, -1e30)
            largest = jnp.max(scores, axis=0, keepdims=True)
            expo = jnp.exp(scores - largest)
            probs = expo * (1.0 / jnp.sum(expo, axis=0, keepdims=True))
            grad_probs = last_dims(v_ref[:stop, at : at + HD], grads)
            inner = jnp.sum(probs * grad_probs, axis=0, keepdims=True)
            grad_scores = (probs * (grad_probs - inner)).astype(BF)
            add_k = plain_dot(grad_scores, queries)
            add_v = plain_dot(probs.astype(BF), grads)
            if stop == length:
                sum_k[...] = add_k
                sum_v[...] = add_v
            else:
                sum_k[:stop] += add_k
                sum_v[:stop] += add_v
            grad_q = plain_dot(kt_ref[:, :stop], grad_scores).T * scale
            grad_q = turn(grad_q, cosine[start:stop], sine[start:stop])
            flip_ref[0, at : at + HD, start:stop] = grad_q.T.astype(BF)
            gq_ref[start:stop, at : at + HD] = grad_q.astype(BF)
        grad_k = turn(sum_k[...] * scale, cosine, sine)
        grad_v = sum_v[...]
        flip_ref[1, at : at + HD, :] = grad_k.T.astype(BF)
        flip_ref[2, at : at + HD, :] = grad_v.T.astype(BF)
        grad_k, grad_v = grad_k.astype(BF), grad_v.astype(BF)
        for block in range(size):
            rows = slice(block * part, (block + 1) * part)
            rk_ref[pl.ds(home(block * part), part), at : at + HD] = grad_k[rows]
            rv_ref[pl.ds(home(block * part), part), at : at + HD] = grad_v[rows]


def attend_backward(place, grad_mid_low, weights, queries, keys, values, cosine, sine, size, at):
    length, width = grad_mid_low.shape
    wide = queries.shape[1]
    group = head_group(wide)
    groups = wide // group
    table = pl.BlockSpec((length, HD), lambda g: (0, 0))
    heads = pl.BlockSpec((length, group), lambda g: (0, at))
    outs = pl.BlockSpec((length, group), lambda g: (0, 0))
    out = jax.ShapeDtypeStruct((length, group), BF)
    return pl.pallas_call(
        functools.partial(backward_kernel, size),
        grid=(1,),
        in_specs=[
            pl.BlockSpec(memory_space=pltpu.SMEM),
            pl.BlockSpec((length, width), lambda g: (0, 0)),
            pl.BlockSpec((width, group), lambda g: (0, at + 3 * groups)),
            heads,
            heads,
            heads,
            table,
            table,
        ],
        out_specs=[outs] * 3 + [pl.BlockSpec((3, group, length), lambda g: (0, 0, 0))],
        out_shape=[out] * 3 + [jax.ShapeDtypeStruct((3, group, length), BF)],
        scratch_shapes=[
            pltpu.VMEM((length, group), BF),
            pltpu.VMEM((HD, length), BF),
            pltpu.VMEM((length, HD), F32),
            pltpu.VMEM((length, HD), F32),
        ],
        compiler_params=limits(),
        cost_estimate=estimate(
            flops=2 * length * width * group + 10 * length * length * group,
            bytes_accessed=2 * length * width + 2 * width * group + 18 * length * group,
            transcendentals=length * length * group // HD,
        ),
    )(place, grad_mid_low, weights, queries, keys, values, cosine, sine)


def feed_kernel(x_ref, g_ref, wg_ref, wu_ref, wd_ref, act_ref, gate_ref, up_ref, flip_ref):
    gate = plain_dot(x_ref[...], wg_ref[...])
    up = plain_dot(x_ref[...], wu_ref[...])
    grad = plain_dot(g_ref[...], wd_ref[...])
    sigma = 1.0 / (1.0 + jnp.exp(-gate))
    silu = gate * sigma
    act = silu * up
    grad_up = grad * silu
    grad_gate = grad * up * (sigma + silu * (1.0 - sigma))
    act_ref[...] = act.astype(BF)
    up_ref[...] = grad_up.astype(BF)
    gate_ref[...] = grad_gate.astype(BF)
    flip_ref[0] = grad_gate.T.astype(BF)
    flip_ref[1] = grad_up.T.astype(BF)
    flip_ref[2] = act.T.astype(BF)


def feed_forward(ffn_in, grad_low, weights):
    length, width = ffn_in.shape
    units = weights.shape[1] // 3
    step = 256 if units % 256 == 0 else units if units <= 512 else 128
    steps = units // step
    whole = pl.BlockSpec((length, width), lambda f: (0, 0))
    out = pl.BlockSpec((length, step), lambda f: (0, f))
    return pl.pallas_call(
        feed_kernel,
        grid=(steps,),
        in_specs=[
            whole,
            whole,
            pl.BlockSpec((width, step), lambda f: (0, f)),
            pl.BlockSpec((width, step), lambda f: (0, f + steps)),
            pl.BlockSpec((width, step), lambda f: (0, f + 2 * steps)),
        ],
        out_specs=[out] * 3 + [pl.BlockSpec((3, step, length), lambda f: (0, f, 0))],
        out_shape=[jax.ShapeDtypeStruct((length, units), BF)] * 3
        + [jax.ShapeDtypeStruct((3, units, length), BF)],
        compiler_params=limits(),
        cost_estimate=estimate(
            flops=6 * length * width * units,
            bytes_accessed=4 * length * width + 6 * width * units + 12 * length * units,
            transcendentals=2 * length * units,
        ),
    )(ffn_in, grad_low, weights, weights, weights)


def products_kernel(counts, *refs):
    step = pl.program_id(0)
    lefts, rights, out_ref = refs[: len(counts)], refs[len(counts) : -1], refs[-1]
    first = 0
    for (steps, right), left in zip(counts, lefts):

        @pl.when((step >= first) & (step < first + steps))
        def _(left=left, right=right):
            out_ref[...] = plain_dot(left[...], rights[right][...]).astype(BF)

        first += steps


def products(terms, rights):
    length, width = rights[0].shape
    step = 256 if all(left.shape[1] % 256 == 0 for left, _, _ in terms) else 128
    counts = tuple((left.shape[1] // step, at) for left, _, at in terms)
    total = sum(steps for steps, _ in counts)
    left_specs = []
    first = 0
    for (steps, _), (_, lead, _) in zip(counts, terms):

        def block(i, first=first, last=steps - 1, lead=lead):
            return (lead, lax.max(lax.min(i - first, last), 0), 0)

        left_specs.append(pl.BlockSpec((None, step, length), block))
        first += steps
    return pl.pallas_call(
        functools.partial(products_kernel, counts),
        grid=(total,),
        in_specs=left_specs + [pl.BlockSpec((length, width), lambda i: (0, 0))] * len(rights),
        out_specs=pl.BlockSpec((step, width), lambda i: (i, 0)),
        out_shape=jax.ShapeDtypeStruct((total * step, width), BF),
        compiler_params=limits(),
        cost_estimate=estimate(
            flops=2 * total * step * length * width,
            bytes_accessed=2 * (total * step * (length + width) + len(rights) * length * width),
            transcendentals=0,
        ),
    )(*[left for left, _, _ in terms], *rights)


def rows_kernel(count, side, steps, *refs):
    lefts, rights, outs = refs[:count], refs[count:-2], refs[-2:]
    for half in range(2):

        @pl.when(pl.program_id(0) // steps == half)
        def _(half=half):
            for piece in range(2):
                row = 2 * piece + side if half == 0 else 2 * side + piece
                total = None
                for left, right in zip(lefts, rights):
                    part = last_dims(left[row], right[...])
                    total = part if total is None else total + part
                outs[half][piece] = total.astype(BF)


def row_products(terms, side, width):
    columns = width // 2
    step = 512 if columns % 512 == 0 else columns
    steps = columns // step
    left_specs, right_specs, lefts, rights = [], [], [], []
    flops = nbytes = 0
    for left, right, at in terms:
        rows, depth = left.shape[0] // 4, left.shape[1]
        lefts.append(left.reshape(4, rows, depth))
        left_specs.append(pl.BlockSpec((4, rows, depth), lambda j: (0, 0, 0)))
        right_specs.append(pl.BlockSpec((step, depth), lambda j, at=at: (j, at)))
        rights.append(right)
        flops += 8 * rows * depth * columns
        nbytes += 4 * depth * (2 * rows + columns)
    return pl.pallas_call(
        functools.partial(rows_kernel, len(terms), side, steps),
        grid=(2 * steps,),
        in_specs=left_specs + right_specs,
        out_specs=[
            pl.BlockSpec((2, rows, step), lambda j: (0, 0, lax.min(j, steps - 1))),
            pl.BlockSpec((2, rows, step), lambda j: (0, 0, lax.max(j - steps, 0))),
        ],
        out_shape=[jax.ShapeDtypeStruct((2, rows, columns), BF)] * 2,
        compiler_params=limits(),
        cost_estimate=estimate(
            flops=flops, bytes_accessed=nbytes + 8 * rows * columns, transcendentals=0
        ),
    )(*lefts, *rights)


def rms_scale(values, gain):
    inverse = lax.rsqrt(jnp.mean(values * values, axis=-1, keepdims=True) + epsilon)
    return (inverse, values * inverse * gain)


def norm_back(grad, values, inverse, gain):
    scaled = grad * gain
    inner = jnp.mean(scaled * values, axis=-1, keepdims=True)
    return inverse * scaled - values * inverse**3 * inner


def rotary_tables(length):
    position = jnp.arange(length, dtype=jnp.float32)
    freqs = jnp.exp(-jnp.log(10000.0) * jnp.arange(HD // 2, dtype=jnp.float32) * 2.0 / HD)
    angle = position[:, None] * freqs[None, :]
    cosine, sine = jnp.cos(angle), jnp.sin(angle)
    return (jnp.concatenate([cosine, cosine], 1), jnp.concatenate([-sine, sine], 1))


def after(value, *earlier):
    return lax.optimization_barrier((value, *earlier))[0]


def swap(array, bit, size):
    return lax.ppermute(array, "tensor", [(t, t ^ bit) for t in range(size)])


def bit_orders(size):
    bits = [1 << step for step in range(size.bit_length() - 1)]
    return (bits, bits[1:] + bits[:1])


def relative(array, me, size):
    part = array.shape[0] // size
    return jnp.stack(
        [lax.dynamic_slice_in_dim(array, (me ^ step) * part, part, 0) for step in range(size)]
    )


def absolute(blocks, me):
    parts = [
        lax.dynamic_index_in_dim(blocks, me ^ step, 0, keepdims=False)
        for step in range(blocks.shape[0])
    ]
    return jnp.concatenate(parts, axis=0)


def scatter_sum(blocks):
    size = blocks.shape[0]
    half = blocks.shape[2] // 2
    sums = []
    for group, order in enumerate(bit_orders(size)):
        held = {
            place: blocks[place, :, group * half : (group + 1) * half].astype(F32)
            for place in range(size)
        }
        for bit in order:
            sent = [place for place in held if place & bit]
            got = swap(jnp.stack([held[place].astype(BF) for place in sent]), bit, size)
            held = {
                place ^ bit: held[place ^ bit] + got[at].astype(F32)
                for at, place in enumerate(sent)
            }
        sums.append(held[0])
    return jnp.concatenate(sums, axis=1)


def gather_part(own, size, group, earlier=()):
    held, came = {0: own}, []
    for bit in bit_orders(size)[group][::-1]:
        places = list(held)
        sent = jnp.stack([held[place] for place in places])
        came.append(swap(after(sent, *earlier) if came else sent, bit, size))
        for at, place in enumerate(places):
            held[place ^ bit] = came[-1][at]
    return [held[place] for place in range(size)], came[0], came[-1]


def gather_rows(own, size, earlier=()):
    half = own.shape[1] // 2
    low, low_first, low_last = gather_part(own[:, :half], size, 0, earlier)
    high, high_first, high_last = gather_part(own[:, half:], size, 1, earlier)
    rows = jnp.stack([jnp.concatenate(pair, axis=1) for pair in zip(low, high)])
    return rows, [low_first, high_first], [low_last, high_last]


def product_scatter(terms, size, width, earlier=(), free=()):
    if size != 4:
        total = 0.0
        for left, right, at in terms:
            depth = left.shape[1]
            total = total + last_dims(left, right[:, at * depth : (at + 1) * depth])
        return scatter_sum(total.reshape(size, -1, width)), [total], [total], total
    sent = row_products(terms, 1, width)
    first = [swap(after(sent[half], *free), 1 + half, size) for half in range(2)]
    lefts = after([left for left, _, _ in terms], *sent, *earlier)
    terms = [(left, right, at) for left, (_, right, at) in zip(lefts, terms)]
    kept = row_products(terms, 0, width)
    held = [kept[half].astype(F32) + first[half].astype(F32) for half in range(2)]
    last = [swap(held[half][1].astype(BF), 2 - half, size) for half in range(2)]
    total = [held[half][0] + last[half].astype(F32) for half in range(2)]
    return jnp.concatenate(total, axis=1), first, last, kept[0]


def input_kernel(
    place_ref,
    mine_ref,
    other_ref,
    hidden_ref,
    mid_ref,
    gain_ref,
    *refs,
):
    lower = place_ref[2] == 0
    out_ref = refs[-1]
    parts = []
    for weights in (mine_ref, other_ref):
        total, start = None, 0
        for heads_ref in refs[:-1]:
            stop = start + heads_ref.shape[2]
            for at in range(heads_ref.shape[0]):
                part = last_dims(heads_ref[at], weights[at, :, start:stop])
                total = part if total is None else total + part
            start = stop
        parts.append(total)
    grad = jnp.concatenate(
        [jnp.where(lower, parts[0], parts[1]), jnp.where(lower, parts[1], parts[0])], axis=1
    )
    values = hidden_ref[...].astype(F32)
    inverse = lax.rsqrt(jnp.mean(values * values, axis=1, keepdims=True) + epsilon)
    scaled = grad * gain_ref[...]
    inner = jnp.mean(scaled * values, axis=1, keepdims=True)
    out_ref[...] = (
        mid_ref[...].astype(F32) + inverse * scaled - values * (inverse**3 * inner)
    )


def input_gradient(place, heads, halves, hidden_in, grad_mid, gain, size):
    length, width = hidden_in.shape
    wide = halves[0].shape[2]
    rows = length // size
    half = pl.BlockSpec((size, width // 2, wide), lambda r, place: (0, 0, 0))
    return pl.pallas_call(
        input_kernel,
        grid_spec=pltpu.PrefetchScalarGridSpec(
            num_scalar_prefetch=1,
            grid=(size,),
            in_specs=[
                half,
                half,
                pl.BlockSpec((rows, width), lambda r, place: (r, 0)),
                pl.BlockSpec((rows, width), lambda r, place: (r ^ place[0], 0)),
                pl.BlockSpec((1, width), lambda r, place: (0, 0)),
            ]
            + [
                pl.BlockSpec((size, rows, part.shape[2]), lambda r, place: (0, r, 0))
                for part in heads
            ],
            out_specs=pl.BlockSpec((rows, width), lambda r, place: (r, 0)),
        ),
        out_shape=jax.ShapeDtypeStruct((length, width), F32),
        compiler_params=limits(),
        cost_estimate=estimate(
            flops=2 * length * width * wide * size,
            bytes_accessed=2 * size * wide * (length + width) + 8 * length * width,
            transcendentals=length,
        ),
    )(place, *halves, hidden_in, grad_mid, gain[None], *heads)


def local(
    hidden_in,
    self_out,
    out_grad,
    lengths,
    w_query,
    w_key,
    w_value,
    w_output,
    w_gate,
    w_up,
    w_down,
    attn_gain,
    ffn_gain,
    kv_gain,
):
    me = lax.axis_index("tensor")
    size = lax.axis_size("tensor")
    dp_size = lax.axis_size("dp")
    length, width = hidden_in.shape
    quarter = length // size
    wide, units = w_query.shape[1], w_gate.shape[1]
    early = units * 3 // 4 // 256 * 256
    late = round_up(units - early, 128)

    def columns(array, start, count):
        kept = array[:, start : start + count]
        return jnp.pad(kept, ((0, 0), (0, count - kept.shape[1])))

    w_flip = w_down.T
    mine = [jnp.concatenate([w_query, w_key, w_value, w_output.T], axis=1)]
    for start, count in ((0, early), (early, late)):
        mine.append(
            jnp.concatenate([columns(w, start, count) for w in (w_gate, w_up, w_flip)], axis=1)
        )
    w_heads, w_early, w_late = [lax.all_gather(w, "dp", axis=0, tiled=True) for w in mine]
    gains = lax.all_gather(jnp.stack([attn_gain, ffn_gain, kv_gain]), "dp", axis=1, tiled=True)
    gains = gains.astype(F32)
    attn_scale, ffn_scale, kv_scale = gains[0], gains[1], gains[2]

    core = lax.axis_index("dp") % 2
    place = jnp.stack([me, lengths[0], core])
    valid = jnp.arange(length, dtype=jnp.int32) < lengths[0]
    cosine, sine = rotary_tables(length)
    hidden = hidden_in.astype(F32)
    selfout = self_out.astype(F32)
    x_inverse, x_normed = rms_scale(hidden, attn_scale)
    normed = x_normed.astype(BF)
    s_inverse, s_normed = rms_scale(selfout, kv_scale)
    kv_normed = s_normed.astype(BF)

    def own_rows(array):
        return lax.dynamic_slice_in_dim(array, me * quarter, quarter, 0)

    hidden_own = own_rows(hidden_in).astype(F32)
    self_own = own_rows(self_out).astype(F32)
    grad_y_low = relative(jnp.where(valid[:, None], out_grad, jnp.zeros((), BF)), me, size)
    grad_y = grad_y_low[0].astype(F32)
    grad_y_low = grad_y_low.reshape(length, width)

    queries, keys, values, attended_low, attended_flip = attend_forward(
        place, normed, kv_normed, w_heads, cosine, sine, size
    )
    mid_sum, _, _, _ = product_scatter([(attended_low, w_heads, 3)], size, width)
    mid = hidden_own + mid_sum
    m_inverse, m_normed = rms_scale(mid, ffn_scale)
    ffn_in, _, ffn_last = gather_rows(m_normed.astype(BF), size)
    ffn_in = ffn_in.reshape(length, width)

    half_rows = lax.dynamic_slice_in_dim(w_heads[:, :wide], core * (width // 2), width // 2, 0)
    query_half, query_first, query_last = gather_rows(after(half_rows, *ffn_last), size)
    query_other = lax.ppermute(query_half, "dp", [(i, i ^ 1) for i in range(dp_size)])
    query_halves = (query_half, query_other)

    act_early, gate_early, up_early, flip_early = feed_forward(ffn_in, grad_y_low, w_early)

    def unit_grads(flip):
        return products([(flip, 0, 0), (flip, 1, 0), (flip, 2, 1)], [ffn_in, grad_y_low])

    grads_early = unit_grads(flip_early)
    sum_early = lax.psum_scatter(after(grads_early, w_late, *query_last), "dp", scatter_dimension=1, tiled=True)
    act_late, gate_late, up_late, flip_late = feed_forward(
        after(ffn_in, grads_early), grad_y_low, w_late
    )
    back_sum, _, _, _ = product_scatter(
        [
            (gate_early, w_early, 0),
            (up_early, w_early, 1),
            (gate_late, w_late, 0),
            (up_late, w_late, 1),
        ],
        size,
        width,
    )
    mid_part = norm_back(back_sum, mid, m_inverse, ffn_scale)
    grad_mid = grad_y + mid_part
    mid_low = grad_mid.astype(BF)
    grad_mid_low, mid_first, mid_last = gather_rows(mid_low, size)
    grad_mid_low = grad_mid_low.reshape(length, width)
    act_early, act_late = after((act_early, act_late), *mid_first)
    out_sum, out_first, out_last, out_done = product_scatter(
        [(act_early, w_early, 2), (act_late, w_late, 2)], size, width, free=mid_last
    )
    grads_late = unit_grads(after(flip_late, mid_low))
    sum_late = lax.psum_scatter(after(grads_late, *mid_first), "dp", scatter_dimension=1, tiled=True)
    grad_mid_low = after(grad_mid_low, grads_late, out_done)

    group = head_group(wide)
    groups = wide // group
    backs, heads_q, q_first, q_last = [], [], [], []
    grad_in = grad_mid_low
    for at in range(groups):
        backs.append(
            attend_backward(
                place, grad_in, w_heads, queries, keys, values, cosine, sine, size, at
            )
        )
        part, first, last = gather_part(backs[-1][0], size, at % 2)
        heads_q.append(jnp.stack(part))
        q_first.append(first)
        q_last.append(last)
        grad_in = after(grad_mid_low, backs[-1][0])
    kv_terms = [(backs[at][1], w_heads, at + groups) for at in range(groups)]
    kv_terms += [(backs[at][2], w_heads, at + 2 * groups) for at in range(groups)]
    lefts = after([left for left, _, _ in kv_terms], *out_first, *q_first[:-1])
    kv_terms = [(left, right, at) for left, (_, right, at) in zip(lefts, kv_terms)]
    grad_kv_normed, kv_first, kv_last, kv_done = product_scatter(
        kv_terms, size, width, earlier=(q_first[-1], *out_last)
    )
    layer_own = after((mid + out_sum).astype(BF), *kv_first)
    layer_rows, layer_first, _ = gather_rows(layer_own, size)
    layer_out = absolute(layer_rows, me)
    grads_heads = products(
        [(backs[at][3], lead, min(lead, 1)) for lead in range(3) for at in range(groups)]
        + [(attended_flip[None], 0, 2)],
        [after(normed, kv_done), kv_normed, after(grad_mid_low, sum_early)],
    )
    grads_heads = after(grads_heads, *kv_first, *q_last[:-1])
    sum_heads = lax.psum_scatter(grads_heads, "dp", scatter_dimension=1, tiled=True).astype(F32)
    s_part = norm_back(grad_kv_normed, self_own, own_rows(s_inverse), kv_scale)
    self_rows, self_first, _ = gather_rows(s_part.astype(BF), size)
    self_grad = absolute(self_rows, me).astype(F32)
    heads_q[0] = after(heads_q[0], *self_first, *layer_first)
    input_grad = input_gradient(
        place, heads_q, query_halves, hidden_in, grad_mid_low, attn_scale, size
    )

    def unit_sums(at):
        early_rows = sum_early[at * early : (at + 1) * early]
        late_rows = sum_late[at * late : at * late + units - early]
        return jnp.concatenate([early_rows, late_rows], axis=0).astype(F32)

    sum_query, sum_key, sum_value = [
        sum_heads[at * wide : (at + 1) * wide].T for at in range(3)
    ]
    sum_gate, sum_up = unit_sums(0).T, unit_sums(1).T

    def gain_part(gain, *pairs):
        total = 0.0
        for weights, grads in pairs:
            total = total + jnp.sum(weights.astype(F32) * grads, axis=1)
        return total / gain.astype(F32)

    gain_sums = jnp.stack(
        [
            gain_part(attn_gain, (w_query, sum_query)),
            gain_part(ffn_gain, (w_gate, sum_gate), (w_up, sum_up)),
            gain_part(kv_gain, (w_key, sum_key), (w_value, sum_value)),
        ]
    )
    others = [
        lax.ppermute(gain_sums, "tensor", [(t, t ^ step) for t in range(size)])
        for step in range(1, size)
    ]
    for other in others:
        gain_sums = gain_sums + other

    return (
        layer_out,
        input_grad,
        self_grad,
        sum_query,
        sum_key,
        sum_value,
        sum_heads[3 * wide :],
        sum_gate,
        sum_up,
        unit_sums(2),
        gain_sums[0],
        gain_sums[1],
        gain_sums[2],
    )


def solution(mesh):
    placed = (
        P("dp", None),
        P("dp", None),
        P("dp", None),
        P("dp"),
        P("dp", "tensor"),
        P("dp", "tensor"),
        P("dp", "tensor"),
        P("tensor", "dp"),
        P("dp", "tensor"),
        P("dp", "tensor"),
        P("tensor", "dp"),
        P("dp"),
        P("dp"),
        P("dp"),
    )
    return jax.shard_map(
        local,
        mesh=mesh,
        in_specs=placed,
        out_specs=(
            P("dp", None),
            P("dp", None),
            P("dp", None),
            P("dp", "tensor"),
            P("dp", "tensor"),
            P("dp", "tensor"),
            P("tensor", "dp"),
            P("dp", "tensor"),
            P("dp", "tensor"),
            P("tensor", "dp"),
            P("dp"),
            P("dp"),
            P("dp"),
        ),
        check_vma=False,
    )
```

```python
import functools

import jax
import jax.numpy as jnp
from jax import lax
from jax.experimental import pallas as pl
from jax.experimental.pallas import tpu as pltpu
from jax.sharding import PartitionSpec as P

HD = 128
QROWS = 256
BF = jnp.bfloat16
F32 = jnp.float32
epsilon = 1e-06
VMEM_LIMIT = 60 * 1024 * 1024
WEIGHT = 1


def plain_dot(left, right):
    return jnp.dot(left, right, preferred_element_type=jnp.float32)


def last_dims(left, right):
    return lax.dot_general(
        left, right, (((1,), (1,)), ((), ())), preferred_element_type=jnp.float32
    )


def round_up(number, unit):
    return (number + unit - 1) // unit * unit


def head_group(wide):
    return 2 * HD if wide % (2 * HD) == 0 else HD


def limits():
    return pltpu.CompilerParams(vmem_limit_bytes=VMEM_LIMIT)


def estimate(flops, bytes_accessed, transcendentals):
    return pl.CostEstimate(
        flops=flops // WEIGHT,
        bytes_accessed=bytes_accessed // WEIGHT,
        transcendentals=transcendentals // WEIGHT,
    )


def turn(values, cosine, sine):
    return values * cosine + pltpu.roll(values, HD // 2, 1) * sine


def forward_kernel(
    size,
    place_ref,
    normed_ref,
    kv_ref,
    wq_ref,
    wk_ref,
    wv_ref,
    cos_ref,
    sin_ref,
    q_ref,
    k_ref,
    v_ref,
    out_ref,
    flip_ref,
):
    me, live = place_ref[0], place_ref[1]
    length = normed_ref.shape[0]
    group = wq_ref.shape[1]
    part = length // size
    cosine, sine = cos_ref[...], sin_ref[...]
    q_pre = plain_dot(normed_ref[...], wq_ref[...])
    for at in range(0, group, HD):
        q_ref[:, at : at + HD] = turn(q_pre[:, at : at + HD], cosine, sine).astype(BF)
    k_pre = plain_dot(kv_ref[...], wk_ref[...])
    for at in range(0, group, HD):
        k_ref[:, at : at + HD] = turn(k_pre[:, at : at + HD], cosine, sine).astype(BF)
    v_ref[...] = plain_dot(kv_ref[...], wv_ref[...]).astype(BF)
    for at in range(0, group, HD):
        for start in range(0, length, QROWS):
            stop = start + QROWS
            scores = last_dims(q_ref[start:stop, at : at + HD], k_ref[:stop, at : at + HD])
            scores = scores * HD ** (-0.5)
            rows = start + lax.broadcasted_iota(jnp.int32, (QROWS, 1), 0)
            bound = jnp.minimum(rows, live - 1)
            columns = lax.broadcasted_iota(jnp.int32, (QROWS, stop), 1)
            scores = jnp.where(columns <= bound, scores, -1e30)
            largest = jnp.max(scores, axis=1, keepdims=True)
            expo = jnp.exp(scores - largest)
            probs = (expo / jnp.sum(expo, axis=1, keepdims=True)).astype(BF)
            result = plain_dot(probs, v_ref[:stop, at : at + HD])
            flipped = result.T.astype(BF)
            result = result.astype(BF)
            step = min(part, QROWS)
            for piece in range(0, QROWS, step):
                block = (start + piece) // part
                row = pl.multiple_of((block ^ me) * part, part) + (start + piece) % part
                rows_at = pl.ds(pl.multiple_of(row, 128), step)
                out_ref[rows_at, at : at + HD] = result[piece : piece + step]
                flip_ref[at : at + HD, rows_at] = flipped[:, piece : piece + step]


def attend_forward(place, normed, kv_normed, weights, cosine, sine, size):
    length, width = normed.shape
    wide = weights.shape[1] // 4
    group = head_group(wide)
    groups = wide // group
    whole = pl.BlockSpec((length, width), lambda g: (0, 0))
    table = pl.BlockSpec((length, HD), lambda g: (0, 0))
    heads = pl.BlockSpec((length, group), lambda g: (0, g))
    out = jax.ShapeDtypeStruct((length, wide), BF)
    return pl.pallas_call(
        functools.partial(forward_kernel, size),
        grid=(groups,),
        in_specs=[
            pl.BlockSpec(memory_space=pltpu.SMEM),
            whole,
            whole,
            pl.BlockSpec((width, group), lambda g: (0, g)),
            pl.BlockSpec((width, group), lambda g: (0, g + groups)),
            pl.BlockSpec((width, group), lambda g: (0, g + 2 * groups)),
            table,
            table,
        ],
        out_specs=[heads] * 4 + [pl.BlockSpec((group, length), lambda g: (g, 0))],
        out_shape=[out] * 4 + [jax.ShapeDtypeStruct((wide, length), BF)],
        compiler_params=limits(),
        cost_estimate=estimate(
            flops=6 * length * width * wide + 3 * length * length * wide,
            bytes_accessed=4 * length * width + 6 * width * wide + 8 * length * wide,
            transcendentals=length * length * wide // HD,
        ),
    )(place, normed, kv_normed, weights, weights, weights, cosine, sine)


def backward_kernel(
    size,
    place_ref,
    grad_ref,
    wo_ref,
    q_ref,
    k_ref,
    v_ref,
    cos_ref,
    sin_ref,
    gq_ref,
    rk_ref,
    rv_ref,
    flip_ref,
    ga_ref,
    kt_ref,
    sum_k,
    sum_v,
):
    me, live = place_ref[0], place_ref[1]
    length = grad_ref.shape[0]
    group = wo_ref.shape[1]
    part = length // size
    scale = HD ** (-0.5)
    cosine, sine = cos_ref[...], -sin_ref[...]

    def home(row):
        block = row // part
        return pl.multiple_of(pl.multiple_of((block ^ me) * part, part) + row % part, 128)

    for block in range(size):
        ga_ref[pl.ds(home(block * part), part), :] = plain_dot(
            grad_ref[block * part : (block + 1) * part, :], wo_ref[...]
        ).astype(BF)
    for at in range(0, group, HD):
        kt_ref[...] = k_ref[:, at : at + HD].T
        for start in reversed(range(0, length, QROWS)):
            stop = start + QROWS
            queries = q_ref[start:stop, at : at + HD]
            grads = ga_ref[start:stop, at : at + HD]
            scores = last_dims(k_ref[:stop, at : at + HD], queries) * scale
            columns = start + lax.broadcasted_iota(jnp.int32, (1, QROWS), 1)
            bound = jnp.minimum(columns, live - 1)
            rows = lax.broadcasted_iota(jnp.int32, (stop, QROWS), 0)
            scores = jnp.where(rows <= bound, scores, -1e30)
            largest = jnp.max(scores, axis=0, keepdims=True)
            expo = jnp.exp(scores - largest)
            probs = expo * (1.0 / jnp.sum(expo, axis=0, keepdims=True))
            grad_probs = last_dims(v_ref[:stop, at : at + HD], grads)
            inner = jnp.sum(probs * grad_probs, axis=0, keepdims=True)
            grad_scores = (probs * (grad_probs - inner)).astype(BF)
            add_k = plain_dot(grad_scores, queries)
            add_v = plain_dot(probs.astype(BF), grads)
            if stop == length:
                sum_k[...] = add_k
                sum_v[...] = add_v
            else:
                sum_k[:stop] += add_k
                sum_v[:stop] += add_v
            grad_q = plain_dot(kt_ref[:, :stop], grad_scores).T * scale
            grad_q = turn(grad_q, cosine[start:stop], sine[start:stop])
            flip_ref[0, at : at + HD, start:stop] = grad_q.T.astype(BF)
            gq_ref[start:stop, at : at + HD] = grad_q.astype(BF)
        grad_k = turn(sum_k[...] * scale, cosine, sine)
        grad_v = sum_v[...]
        flip_ref[1, at : at + HD, :] = grad_k.T.astype(BF)
        flip_ref[2, at : at + HD, :] = grad_v.T.astype(BF)
        grad_k, grad_v = grad_k.astype(BF), grad_v.astype(BF)
        for block in range(size):
            rows = slice(block * part, (block + 1) * part)
            rk_ref[pl.ds(home(block * part), part), at : at + HD] = grad_k[rows]
            rv_ref[pl.ds(home(block * part), part), at : at + HD] = grad_v[rows]


def attend_backward(place, grad_mid_low, weights, queries, keys, values, cosine, sine, size, at):
    length, width = grad_mid_low.shape
    wide = queries.shape[1]
    group = head_group(wide)
    groups = wide // group
    table = pl.BlockSpec((length, HD), lambda g: (0, 0))
    heads = pl.BlockSpec((length, group), lambda g: (0, at))
    outs = pl.BlockSpec((length, group), lambda g: (0, 0))
    out = jax.ShapeDtypeStruct((length, group), BF)
    return pl.pallas_call(
        functools.partial(backward_kernel, size),
        grid=(1,),
        in_specs=[
            pl.BlockSpec(memory_space=pltpu.SMEM),
            pl.BlockSpec((length, width), lambda g: (0, 0)),
            pl.BlockSpec((width, group), lambda g: (0, at + 3 * groups)),
            heads,
            heads,
            heads,
            table,
            table,
        ],
        out_specs=[outs] * 3 + [pl.BlockSpec((3, group, length), lambda g: (0, 0, 0))],
        out_shape=[out] * 3 + [jax.ShapeDtypeStruct((3, group, length), BF)],
        scratch_shapes=[
            pltpu.VMEM((length, group), BF),
            pltpu.VMEM((HD, length), BF),
            pltpu.VMEM((length, HD), F32),
            pltpu.VMEM((length, HD), F32),
        ],
        compiler_params=limits(),
        cost_estimate=estimate(
            flops=2 * length * width * group + 10 * length * length * group,
            bytes_accessed=2 * length * width + 2 * width * group + 18 * length * group,
            transcendentals=length * length * group // HD,
        ),
    )(place, grad_mid_low, weights, queries, keys, values, cosine, sine)


def feed_kernel(x_ref, g_ref, wg_ref, wu_ref, wd_ref, act_ref, gate_ref, up_ref, flip_ref):
    gate = plain_dot(x_ref[...], wg_ref[...])
    up = plain_dot(x_ref[...], wu_ref[...])
    grad = plain_dot(g_ref[...], wd_ref[...])
    sigma = 1.0 / (1.0 + jnp.exp(-gate))
    silu = gate * sigma
    act = silu * up
    grad_up = grad * silu
    grad_gate = grad * up * (sigma + silu * (1.0 - sigma))
    act_ref[...] = act.astype(BF)
    up_ref[...] = grad_up.astype(BF)
    gate_ref[...] = grad_gate.astype(BF)
    flip_ref[0] = grad_gate.T.astype(BF)
    flip_ref[1] = grad_up.T.astype(BF)
    flip_ref[2] = act.T.astype(BF)


def feed_forward(ffn_in, grad_low, weights):
    length, width = ffn_in.shape
    units = weights.shape[1] // 3
    step = 256 if units % 256 == 0 else units if units <= 512 else 128
    steps = units // step
    whole = pl.BlockSpec((length, width), lambda f: (0, 0))
    out = pl.BlockSpec((length, step), lambda f: (0, f))
    return pl.pallas_call(
        feed_kernel,
        grid=(steps,),
        in_specs=[
            whole,
            whole,
            pl.BlockSpec((width, step), lambda f: (0, f)),
            pl.BlockSpec((width, step), lambda f: (0, f + steps)),
            pl.BlockSpec((width, step), lambda f: (0, f + 2 * steps)),
        ],
        out_specs=[out] * 3 + [pl.BlockSpec((3, step, length), lambda f: (0, f, 0))],
        out_shape=[jax.ShapeDtypeStruct((length, units), BF)] * 3
        + [jax.ShapeDtypeStruct((3, units, length), BF)],
        compiler_params=limits(),
        cost_estimate=estimate(
            flops=6 * length * width * units,
            bytes_accessed=4 * length * width + 6 * width * units + 12 * length * units,
            transcendentals=2 * length * units,
        ),
    )(ffn_in, grad_low, weights, weights, weights)


def products_kernel(counts, *refs):
    step = pl.program_id(0)
    lefts, rights, out_ref = refs[: len(counts)], refs[len(counts) : -1], refs[-1]
    first = 0
    for (steps, right), left in zip(counts, lefts):

        @pl.when((step >= first) & (step < first + steps))
        def _(left=left, right=right):
            out_ref[...] = plain_dot(left[...], rights[right][...]).astype(BF)

        first += steps


def products(terms, rights):
    length, width = rights[0].shape
    step = 256 if all(left.shape[1] % 256 == 0 for left, _, _ in terms) else 128
    counts = tuple((left.shape[1] // step, at) for left, _, at in terms)
    total = sum(steps for steps, _ in counts)
    left_specs = []
    first = 0
    for (steps, _), (_, lead, _) in zip(counts, terms):

        def block(i, first=first, last=steps - 1, lead=lead):
            return (lead, lax.max(lax.min(i - first, last), 0), 0)

        left_specs.append(pl.BlockSpec((None, step, length), block))
        first += steps
    return pl.pallas_call(
        functools.partial(products_kernel, counts),
        grid=(total,),
        in_specs=left_specs + [pl.BlockSpec((length, width), lambda i: (0, 0))] * len(rights),
        out_specs=pl.BlockSpec((step, width), lambda i: (i, 0)),
        out_shape=jax.ShapeDtypeStruct((total * step, width), BF),
        compiler_params=limits(),
        cost_estimate=estimate(
            flops=2 * total * step * length * width,
            bytes_accessed=2 * (total * step * (length + width) + len(rights) * length * width),
            transcendentals=0,
        ),
    )(*[left for left, _, _ in terms], *rights)


def rows_kernel(count, steps, *refs):
    lefts, rights, outs = refs[: 2 * count], refs[2 * count : -2], refs[-2:]
    for half in range(2):

        @pl.when(pl.program_id(0) // steps == half)
        def _(half=half):
            for piece in range(2):
                total = None
                for at, right in enumerate(rights):
                    part = last_dims(lefts[2 * at + piece][...], right[...])
                    total = part if total is None else total + part
                outs[half][piece] = total.astype(BF)


def row_products(terms, side, width):
    columns = width // 2
    step = 512 if columns % 512 == 0 else columns
    steps = columns // step
    left_specs, right_specs, lefts, rights = [], [], [], []
    flops = nbytes = 0
    for left, right, at in terms:
        rows, depth = left.shape[0] // 4, left.shape[1]
        for piece in range(2):

            def block(j, piece=piece):
                upper = j // steps
                return ((1 - upper) * (2 * piece + side) + upper * (2 * side + piece), 0)

            lefts.append(left)
            left_specs.append(pl.BlockSpec((rows, depth), block))
        right_specs.append(pl.BlockSpec((step, depth), lambda j, at=at: (j, at)))
        rights.append(right)
        flops += 8 * rows * depth * columns
        nbytes += 4 * depth * (2 * rows + columns)
    return pl.pallas_call(
        functools.partial(rows_kernel, len(terms), steps),
        grid=(2 * steps,),
        in_specs=left_specs + right_specs,
        out_specs=[
            pl.BlockSpec((2, rows, step), lambda j: (0, 0, lax.min(j, steps - 1))),
            pl.BlockSpec((2, rows, step), lambda j: (0, 0, lax.max(j - steps, 0))),
        ],
        out_shape=[jax.ShapeDtypeStruct((2, rows, columns), BF)] * 2,
        compiler_params=limits(),
        cost_estimate=estimate(
            flops=flops, bytes_accessed=nbytes + 8 * rows * columns, transcendentals=0
        ),
    )(*lefts, *rights)


def rms_scale(values, gain):
    inverse = lax.rsqrt(jnp.mean(values * values, axis=-1, keepdims=True) + epsilon)
    return (inverse, values * inverse * gain)


def norm_back(grad, values, inverse, gain):
    scaled = grad * gain
    inner = jnp.mean(scaled * values, axis=-1, keepdims=True)
    return inverse * scaled - values * inverse**3 * inner


def rotary_tables(length):
    position = jnp.arange(length, dtype=jnp.float32)
    freqs = jnp.exp(-jnp.log(10000.0) * jnp.arange(HD // 2, dtype=jnp.float32) * 2.0 / HD)
    angle = position[:, None] * freqs[None, :]
    cosine, sine = jnp.cos(angle), jnp.sin(angle)
    return (jnp.concatenate([cosine, cosine], 1), jnp.concatenate([-sine, sine], 1))


def after(value, *earlier):
    return lax.optimization_barrier((value, *earlier))[0]


def swap(array, bit, size):
    return lax.ppermute(array, "tensor", [(t, t ^ bit) for t in range(size)])


def bit_orders(size):
    bits = [1 << step for step in range(size.bit_length() - 1)]
    return (bits, bits[1:] + bits[:1])


def relative(array, me, size):
    part = array.shape[0] // size
    return jnp.stack(
        [lax.dynamic_slice_in_dim(array, (me ^ step) * part, part, 0) for step in range(size)]
    )


def scatter_sum(blocks):
    size = blocks.shape[0]
    half = blocks.shape[2] // 2
    sums = []
    for group, order in enumerate(bit_orders(size)):
        held = {
            place: blocks[place, :, group * half : (group + 1) * half].astype(F32)
            for place in range(size)
        }
        for bit in order:
            sent = [place for place in held if place & bit]
            got = swap(jnp.stack([held[place].astype(BF) for place in sent]), bit, size)
            held = {
                place ^ bit: held[place ^ bit] + got[at].astype(F32)
                for at, place in enumerate(sent)
            }
        sums.append(held[0])
    return jnp.concatenate(sums, axis=1)


def gather_start(own, size, group):
    return gather_step({0: (own[None], 0)}, bit_orders(size)[group][-1], size)


def gather_step(held, bit, size, earlier=()):
    places = list(held)
    sent = jnp.stack([held[place][0][held[place][1]] for place in places])
    got = swap(after(sent, *earlier), bit, size)
    return {**held, **{place ^ bit: (got, at) for at, place in enumerate(places)}}, got


def gather_end(held, size, group, earlier=()):
    got = None
    for bit in bit_orders(size)[group][-2::-1]:
        held, got = gather_step(held, bit, size, earlier)
    return [held[place] for place in range(size)], got


def halves_start(own, size):
    half = own.shape[1] // 2
    parts = (own[:, :half], own[:, half:])
    state = [gather_start(part, size, group) for group, part in enumerate(parts)]
    return [held for held, _ in state], [got for _, got in state]


def halves_end(state, size, earlier=()):
    ends = [gather_end(held, size, group, earlier) for group, held in enumerate(state)]
    return [parts for parts, _ in ends], [got for _, got in ends]


def assemble_kernel(cases, shift_ref, *refs):
    out_ref = refs[-1]
    place = pl.program_id(0) ^ shift_ref[0]
    for case, picks in enumerate(cases):

        @pl.when(place == case)
        def _(picks=picks):
            columns = 0
            for at, index in picks:
                part = refs[at][index]
                out_ref[:, columns : columns + part.shape[1]] = part.astype(out_ref.dtype)
                columns += part.shape[1]


def arrays_of(halves):
    arrays, picks = [], []
    for parts in halves:
        picks.append([])
        for array, index in parts:
            known = [at for at, other in enumerate(arrays) if other is array]
            if not known:
                arrays.append(array)
            picks[-1].append((known[0] if known else len(arrays) - 1, index))
    return arrays, picks


def assemble(halves, shift, dtype):
    arrays, picks = arrays_of(halves)
    size = len(picks[0])
    rows = arrays[0].shape[1]
    width = sum(parts[0][0].shape[2] for parts in halves)
    return pl.pallas_call(
        functools.partial(assemble_kernel, list(zip(*picks))),
        grid=(size,),
        in_specs=[pl.BlockSpec(memory_space=pltpu.SMEM)]
        + [pl.BlockSpec(array.shape, lambda r: (0, 0, 0)) for array in arrays],
        out_specs=pl.BlockSpec((rows, width), lambda r: (r, 0)),
        out_shape=jax.ShapeDtypeStruct((size * rows, width), dtype),
        compiler_params=limits(),
        cost_estimate=estimate(
            flops=size * rows * width, bytes_accessed=6 * size * rows * width, transcendentals=0
        ),
    )(shift, *arrays)


def scatter_start(terms, size, width, earlier=(), free=()):
    if size != 4:
        total = 0.0
        for left, right, at in terms:
            depth = left.shape[1]
            total = total + last_dims(left, right[:, at * depth : (at + 1) * depth])
        return total, [total], [total], [total]
    sent = row_products(terms, 1, width)
    lefts = after([left for left, _, _ in terms], *sent, *earlier)
    terms = [(left, right, at) for left, (_, right, at) in zip(lefts, terms)]
    kept = row_products(terms, 0, width)
    if free:
        free = (*free, *kept)
    first = [swap(after(sent[half], *free), 1 + half, size) for half in range(2)]
    return (first, kept), sent, first, kept


def scatter_end(state, size, width, earlier=()):
    if size != 4:
        total = scatter_sum(state.reshape(size, -1, width))
        return total, [total], [total]
    first, kept = state
    first = after(first, *earlier)
    held = [kept[half].astype(F32) + first[half].astype(F32) for half in range(2)]
    sent = [held[half][1].astype(BF) for half in range(2)]
    last = [swap(sent[half], 2 - half, size) for half in range(2)]
    total = [held[half][0] + last[half].astype(F32) for half in range(2)]
    return jnp.concatenate(total, axis=1), sent, last


def input_kernel(picks, sizes, place_ref, hidden_ref, mid_ref, gain_ref, *refs):
    lower = place_ref[2] == 0
    out_ref = refs[-1]
    heads_picks, mine_picks, other_picks = picks
    heads_size, weights_size = sizes
    parts = []
    for weights_picks in (mine_picks, other_picks):
        total = None
        for half, parts_of in enumerate(weights_picks):
            start = half * weights_size
            heads_of = heads_picks[start // heads_size]
            start = start % heads_size
            for (head, row), (weight, place) in zip(heads_of, parts_of):
                left = refs[head][row, :, start : start + weights_size]
                part = last_dims(left, refs[weight][place])
                total = part if total is None else total + part
        parts.append(total)
    grad = jnp.concatenate(
        [jnp.where(lower, parts[0], parts[1]), jnp.where(lower, parts[1], parts[0])], axis=1
    )
    values = hidden_ref[...].astype(F32)
    inverse = lax.rsqrt(jnp.mean(values * values, axis=1, keepdims=True) + epsilon)
    scaled = grad * gain_ref[...]
    inner = jnp.mean(scaled * values, axis=1, keepdims=True)
    out_ref[...] = (
        mid_ref[...].astype(F32) + inverse * scaled - values * (inverse**3 * inner)
    )


def input_gradient(place, heads, mine, other, hidden_in, grad_mid, gain, size):
    length, width = hidden_in.shape
    rows = length // size
    arrays, picks = [], []
    for group in (heads, mine, other):
        more, at = arrays_of(group)
        picks.append([[(len(arrays) + array, index) for array, index in part] for part in at])
        arrays += more
        if group is heads:
            count = len(arrays)
    sizes = (heads[0][0][0].shape[2], mine[0][0][0].shape[2])
    wide = sum(part[0][0].shape[2] for part in heads)
    return pl.pallas_call(
        functools.partial(input_kernel, picks, sizes),
        grid_spec=pltpu.PrefetchScalarGridSpec(
            num_scalar_prefetch=1,
            grid=(size,),
            in_specs=[
                pl.BlockSpec((rows, width), lambda r, place: (r, 0)),
                pl.BlockSpec((rows, width), lambda r, place: (r ^ place[0], 0)),
                pl.BlockSpec((1, width), lambda r, place: (0, 0)),
            ]
            + [
                pl.BlockSpec((array.shape[0], rows, array.shape[2]), lambda r, place: (0, r, 0))
                for array in arrays[:count]
            ]
            + [pl.BlockSpec(array.shape, lambda r, place: (0, 0, 0)) for array in arrays[count:]],
            out_specs=pl.BlockSpec((rows, width), lambda r, place: (r, 0)),
        ),
        out_shape=jax.ShapeDtypeStruct((length, width), F32),
        compiler_params=limits(),
        cost_estimate=estimate(
            flops=2 * length * width * wide * size,
            bytes_accessed=2 * size * wide * (length + width) + 8 * length * width,
            transcendentals=length,
        ),
    )(place, hidden_in, grad_mid, gain[None], *arrays)


def local(
    hidden_in,
    self_out,
    out_grad,
    lengths,
    w_query,
    w_key,
    w_value,
    w_output,
    w_gate,
    w_up,
    w_down,
    attn_gain,
    ffn_gain,
    kv_gain,
):
    me = lax.axis_index("tensor")
    size = lax.axis_size("tensor")
    dp_size = lax.axis_size("dp")
    length, width = hidden_in.shape
    quarter = length // size
    wide, units = w_query.shape[1], w_gate.shape[1]
    early = units * 3 // 4 // 256 * 256
    late = round_up(units - early, 128)

    def columns(array, start, count):
        kept = array[:, start : start + count]
        return jnp.pad(kept, ((0, 0), (0, count - kept.shape[1])))

    w_flip = w_down.T
    mine = [jnp.concatenate([w_query, w_key, w_value, w_output.T], axis=1)]
    for start, count in ((0, early), (early, late)):
        mine.append(
            jnp.concatenate([columns(w, start, count) for w in (w_gate, w_up, w_flip)], axis=1)
        )
    w_heads, w_early, w_late = [lax.all_gather(w, "dp", axis=0, tiled=True) for w in mine]
    gains = lax.all_gather(jnp.stack([attn_gain, ffn_gain, kv_gain]), "dp", axis=1, tiled=True)
    gains = gains.astype(F32)
    attn_scale, ffn_scale, kv_scale = gains[0], gains[1], gains[2]

    core = lax.axis_index("dp") % 2
    place = jnp.stack([me, lengths[0], core])
    valid = jnp.arange(length, dtype=jnp.int32) < lengths[0]
    cosine, sine = rotary_tables(length)
    hidden = hidden_in.astype(F32)
    selfout = self_out.astype(F32)
    x_inverse, x_normed = rms_scale(hidden, attn_scale)
    normed = x_normed.astype(BF)
    s_inverse, s_normed = rms_scale(selfout, kv_scale)
    kv_normed = s_normed.astype(BF)

    def own_rows(array):
        return lax.dynamic_slice_in_dim(array, me * quarter, quarter, 0)

    hidden_own = own_rows(hidden_in).astype(F32)
    self_own = own_rows(self_out).astype(F32)
    grad_y_low = relative(jnp.where(valid[:, None], out_grad, jnp.zeros((), BF)), me, size)
    grad_y = grad_y_low[0].astype(F32)
    grad_y_low = grad_y_low.reshape(length, width)

    queries, keys, values, attended_low, attended_flip = attend_forward(
        place, normed, kv_normed, w_heads, cosine, sine, size
    )
    state, _, _, _ = scatter_start([(attended_low, w_heads, 3)], size, width)
    mid_sum, _, _ = scatter_end(state, size, width)
    mid = hidden_own + mid_sum
    m_inverse, m_normed = rms_scale(mid, ffn_scale)
    held, _ = halves_start(m_normed.astype(BF), size)
    parts, ffn_last = halves_end(held, size)
    still = jnp.zeros((1,), jnp.int32)
    ffn_in = assemble(parts, still, BF)

    half_rows = lax.dynamic_slice_in_dim(w_heads[:, :wide], core * (width // 2), width // 2, 0)
    held, _ = halves_start(after(half_rows, *ffn_last), size)
    query_mine, query_last = halves_end(held, size)

    act_early, gate_early, up_early, flip_early = feed_forward(ffn_in, grad_y_low, w_early)

    def unit_grads(flip):
        return products([(flip, 0, 0), (flip, 1, 0), (flip, 2, 1)], [ffn_in, grad_y_low])

    grads_early = unit_grads(flip_early)
    sum_early = lax.psum_scatter(after(grads_early, w_late, *query_last), "dp", scatter_dimension=1, tiled=True)
    act_late, gate_late, up_late, flip_late = feed_forward(
        after(ffn_in, grads_early), grad_y_low, w_late
    )
    state, _, _, _ = scatter_start(
        [
            (gate_early, w_early, 0),
            (up_early, w_early, 1),
            (gate_late, w_late, 0),
            (up_late, w_late, 1),
        ],
        size,
        width,
    )
    back_sum, _, _ = scatter_end(state, size, width)
    mid_part = norm_back(back_sum, mid, m_inverse, ffn_scale)
    grad_mid = grad_y + mid_part
    mid_low = grad_mid.astype(BF)
    held, mid_first = halves_start(mid_low, size)
    parts, mid_last = halves_end(held, size)
    grad_mid_low = assemble(parts, still, BF)
    act_early, act_late = after((act_early, act_late), *mid_first)
    out_state, _, out_first, out_kept = scatter_start(
        [(act_early, w_early, 2), (act_late, w_late, 2)], size, width, free=mid_last
    )
    grads_late = unit_grads(after(flip_late, mid_low))
    sum_late = lax.psum_scatter(
        after(grads_late, *mid_first), "dp", scatter_dimension=1, tiled=True
    )
    grad_mid_low = after(grad_mid_low, grads_late, *out_kept)

    group = head_group(wide)
    groups = wide // group
    backs, heads_held, q_first = [], [], []
    grad_in = grad_mid_low
    for at in range(groups):
        backs.append(
            attend_backward(
                place, grad_in, w_heads, queries, keys, values, cosine, sine, size, at
            )
        )
        held, first = gather_start(backs[-1][0], size, at % 2)
        heads_held.append(held)
        q_first.append(first)
        grad_in = after(grad_mid_low, backs[-1][0])
    kv_terms = [(backs[at][1], w_heads, at + groups) for at in range(groups)]
    kv_terms += [(backs[at][2], w_heads, at + 2 * groups) for at in range(groups)]
    lefts = after([left for left, _, _ in kv_terms], *out_first, *q_first[:-1])
    kv_terms = [(left, right, at) for left, (_, right, at) in zip(lefts, kv_terms)]
    kv_state, kv_sent, kv_first, kv_kept = scatter_start(
        kv_terms, size, width, earlier=q_first[-1:]
    )
    grad_kv_normed, kv_more, kv_last = scatter_end(kv_state, size, width)
    heads_q, q_last = [], []
    for at in range(groups):
        parts, last = gather_end(heads_held[at], size, at % 2, kv_more)
        heads_q.append(parts)
        q_last.append(last)
    out_sum, out_more, out_last = scatter_end(out_state, size, width, kv_more)
    layer_own = (mid + out_sum).astype(BF)
    layer_held, layer_first = halves_start(layer_own, size)
    layer_parts, _ = halves_end(layer_held, size)
    layer_out = assemble(layer_parts, place, BF)
    grads_heads = products(
        [(backs[at][3], lead, min(lead, 1)) for lead in range(3) for at in range(groups)]
        + [(attended_flip[None], 0, 2)],
        [after(normed, kv_kept[0]), kv_normed, after(grad_mid_low, sum_early)],
    )
    grads_heads = after(grads_heads, *kv_first)
    sum_heads = lax.psum_scatter(grads_heads, "dp", scatter_dimension=1, tiled=True).astype(F32)
    def unit_sums(at):
        early_rows = sum_early[at * early : (at + 1) * early]
        late_rows = sum_late[at * late : at * late + units - early]
        return jnp.concatenate([early_rows, late_rows], axis=0).astype(F32)

    def gain_part(gain, *pairs):
        total = 0.0
        for weights, grads in pairs:
            total = total + jnp.sum(weights.astype(F32) * grads, axis=1)
        return total / gain.astype(F32)

    s_part = norm_back(grad_kv_normed, self_own, own_rows(s_inverse), kv_scale)
    self_own_grad = s_part.astype(BF)
    self_held, self_first = halves_start(self_own_grad, size)

    weights_in = after((w_gate, w_up), *self_first)
    sum_gate, sum_up, sum_down = unit_sums(0).T, unit_sums(1).T, unit_sums(2)
    ffn_gain_sum = gain_part(ffn_gain, (weights_in[0], sum_gate), (weights_in[1], sum_up))

    query_arrays, query_picks = arrays_of(query_mine)
    other_arrays = [
        lax.ppermute(array, "dp", [(i, i ^ 1) for i in range(dp_size)])
        for array in after(query_arrays, *kv_more)
    ]
    query_other = [[(other_arrays[at], index) for at, index in part] for part in query_picks]
    input_grad = input_gradient(
        place,
        heads_q,
        query_mine,
        query_other,
        after(hidden_in, self_own_grad),
        grad_mid_low,
        attn_scale,
        size,
    )
    self_parts, _ = halves_end(self_held, size, [input_grad])
    weights_in = after((w_query, w_key, w_value), *self_first)
    sum_query, sum_key, sum_value = [
        sum_heads[at * wide : (at + 1) * wide].T for at in range(3)
    ]
    gain_sums = jnp.stack(
        [
            gain_part(attn_gain, (weights_in[0], sum_query)),
            ffn_gain_sum,
            gain_part(kv_gain, (weights_in[1], sum_key), (weights_in[2], sum_value)),
        ]
    )
    self_grad = assemble(self_parts, after(place, gain_sums), F32)
    others = [
        lax.ppermute(gain_sums, "tensor", [(t, t ^ step) for t in range(size)])
        for step in range(1, size)
    ]
    for other in others:
        gain_sums = gain_sums + other

    return (
        layer_out,
        input_grad,
        self_grad,
        sum_query,
        sum_key,
        sum_value,
        sum_heads[3 * wide :],
        sum_gate,
        sum_up,
        sum_down,
        gain_sums[0],
        gain_sums[1],
        gain_sums[2],
    )


def solution(mesh):
    placed = (
        P("dp", None),
        P("dp", None),
        P("dp", None),
        P("dp"),
        P("dp", "tensor"),
        P("dp", "tensor"),
        P("dp", "tensor"),
        P("tensor", "dp"),
        P("dp", "tensor"),
        P("dp", "tensor"),
        P("tensor", "dp"),
        P("dp"),
        P("dp"),
        P("dp"),
    )
    return jax.shard_map(
        local,
        mesh=mesh,
        in_specs=placed,
        out_specs=(
            P("dp", None),
            P("dp", None),
            P("dp", None),
            P("dp", "tensor"),
            P("dp", "tensor"),
            P("dp", "tensor"),
            P("tensor", "dp"),
            P("dp", "tensor"),
            P("dp", "tensor"),
            P("tensor", "dp"),
            P("dp"),
            P("dp"),
            P("dp"),
        ),
        check_vma=False,
    )
```

```python
import functools

import jax
import jax.numpy as jnp
from jax import lax
from jax.experimental import pallas as pl
from jax.experimental.pallas import tpu as pltpu
from jax.sharding import PartitionSpec as P

HD = 128
QROWS = 256
BF = jnp.bfloat16
F32 = jnp.float32
epsilon = 1e-06
VMEM_LIMIT = 60 * 1024 * 1024
WEIGHT = 1


def plain_dot(left, right):
    return jnp.dot(left, right, preferred_element_type=jnp.float32)


def last_dims(left, right):
    return lax.dot_general(
        left, right, (((1,), (1,)), ((), ())), preferred_element_type=jnp.float32
    )


def round_up(number, unit):
    return (number + unit - 1) // unit * unit


def head_group(wide):
    return 2 * HD if wide % (2 * HD) == 0 else HD


def limits():
    return pltpu.CompilerParams(vmem_limit_bytes=VMEM_LIMIT)


def estimate(flops, bytes_accessed, transcendentals):
    return pl.CostEstimate(
        flops=flops // WEIGHT,
        bytes_accessed=bytes_accessed // WEIGHT,
        transcendentals=transcendentals // WEIGHT,
    )


def turn(values, cosine, sine):
    return values * cosine + pltpu.roll(values, HD // 2, 1) * sine


def forward_kernel(
    size,
    place_ref,
    normed_ref,
    kv_ref,
    wq_ref,
    wk_ref,
    wv_ref,
    cos_ref,
    sin_ref,
    q_ref,
    k_ref,
    v_ref,
    out_ref,
    flip_ref,
):
    me, live = place_ref[0], place_ref[1]
    length = normed_ref.shape[0]
    group = wq_ref.shape[1]
    part = length // size
    cosine, sine = cos_ref[...], sin_ref[...]
    q_pre = plain_dot(normed_ref[...], wq_ref[...])
    for at in range(0, group, HD):
        q_ref[:, at : at + HD] = turn(q_pre[:, at : at + HD], cosine, sine).astype(BF)
    k_pre = plain_dot(kv_ref[...], wk_ref[...])
    for at in range(0, group, HD):
        k_ref[:, at : at + HD] = turn(k_pre[:, at : at + HD], cosine, sine).astype(BF)
    v_ref[...] = plain_dot(kv_ref[...], wv_ref[...]).astype(BF)
    for at in range(0, group, HD):
        for start in range(0, length, QROWS):
            stop = start + QROWS
            scores = last_dims(q_ref[start:stop, at : at + HD], k_ref[:stop, at : at + HD])
            scores = scores * HD ** (-0.5)
            rows = start + lax.broadcasted_iota(jnp.int32, (QROWS, 1), 0)
            bound = jnp.minimum(rows, live - 1)
            columns = lax.broadcasted_iota(jnp.int32, (QROWS, stop), 1)
            scores = jnp.where(columns <= bound, scores, -1e30)
            largest = jnp.max(scores, axis=1, keepdims=True)
            expo = jnp.exp(scores - largest)
            probs = (expo / jnp.sum(expo, axis=1, keepdims=True)).astype(BF)
            result = plain_dot(probs, v_ref[:stop, at : at + HD])
            flipped = result.T.astype(BF)
            result = result.astype(BF)
            step = min(part, QROWS)
            for piece in range(0, QROWS, step):
                block = (start + piece) // part
                row = pl.multiple_of((block ^ me) * part, part) + (start + piece) % part
                rows_at = pl.ds(pl.multiple_of(row, 128), step)
                out_ref[rows_at, at : at + HD] = result[piece : piece + step]
                flip_ref[at : at + HD, rows_at] = flipped[:, piece : piece + step]


def attend_forward(place, normed, kv_normed, weights, cosine, sine, size):
    length, width = normed.shape
    wide = weights.shape[1] // 4
    group = head_group(wide)
    groups = wide // group
    whole = pl.BlockSpec((length, width), lambda g: (0, 0))
    table = pl.BlockSpec((length, HD), lambda g: (0, 0))
    heads = pl.BlockSpec((length, group), lambda g: (0, g))
    out = jax.ShapeDtypeStruct((length, wide), BF)
    return pl.pallas_call(
        functools.partial(forward_kernel, size),
        grid=(groups,),
        in_specs=[
            pl.BlockSpec(memory_space=pltpu.SMEM),
            whole,
            whole,
            pl.BlockSpec((width, group), lambda g: (0, g)),
            pl.BlockSpec((width, group), lambda g: (0, g + groups)),
            pl.BlockSpec((width, group), lambda g: (0, g + 2 * groups)),
            table,
            table,
        ],
        out_specs=[heads] * 4 + [pl.BlockSpec((group, length), lambda g: (g, 0))],
        out_shape=[out] * 4 + [jax.ShapeDtypeStruct((wide, length), BF)],
        compiler_params=limits(),
        cost_estimate=estimate(
            flops=6 * length * width * wide + 3 * length * length * wide,
            bytes_accessed=4 * length * width + 6 * width * wide + 8 * length * wide,
            transcendentals=length * length * wide // HD,
        ),
    )(place, normed, kv_normed, weights, weights, weights, cosine, sine)


def backward_kernel(
    picks,
    place_ref,
    wo_ref,
    q_ref,
    k_ref,
    v_ref,
    cos_ref,
    sin_ref,
    *refs,
):
    gq_ref, rk_ref, rv_ref, flip_ref, ga_ref, kt_ref, sum_k, sum_v = refs[-8:]
    me, live = place_ref[0], place_ref[1]
    length = q_ref.shape[0]
    size = len(picks[0])
    group = wo_ref.shape[1]
    part = length // size
    scale = HD ** (-0.5)
    cosine, sine = cos_ref[...], -sin_ref[...]

    def home(row):
        block = row // part
        return pl.multiple_of(pl.multiple_of((block ^ me) * part, part) + row % part, 128)

    for block in range(size):
        total, start = None, 0
        for half in picks:
            array, index = half[block]
            stop = start + refs[array].shape[2]
            term = plain_dot(refs[array][index], wo_ref[start:stop, :])
            total = term if total is None else total + term
            start = stop
        ga_ref[pl.ds(home(block * part), part), :] = total.astype(BF)
    for at in range(0, group, HD):
        kt_ref[...] = k_ref[:, at : at + HD].T
        for start in reversed(range(0, length, QROWS)):
            stop = start + QROWS
            queries = q_ref[start:stop, at : at + HD]
            grads = ga_ref[start:stop, at : at + HD]
            scores = last_dims(k_ref[:stop, at : at + HD], queries) * scale
            columns = start + lax.broadcasted_iota(jnp.int32, (1, QROWS), 1)
            bound = jnp.minimum(columns, live - 1)
            rows = lax.broadcasted_iota(jnp.int32, (stop, QROWS), 0)
            scores = jnp.where(rows <= bound, scores, -1e30)
            largest = jnp.max(scores, axis=0, keepdims=True)
            expo = jnp.exp(scores - largest)
            probs = expo * (1.0 / jnp.sum(expo, axis=0, keepdims=True))
            grad_probs = last_dims(v_ref[:stop, at : at + HD], grads)
            inner = jnp.sum(probs * grad_probs, axis=0, keepdims=True)
            grad_scores = (probs * (grad_probs - inner)).astype(BF)
            add_k = plain_dot(grad_scores, queries)
            add_v = plain_dot(probs.astype(BF), grads)
            if stop == length:
                sum_k[...] = add_k
                sum_v[...] = add_v
            else:
                sum_k[:stop] += add_k
                sum_v[:stop] += add_v
            grad_q = plain_dot(kt_ref[:, :stop], grad_scores).T * scale
            grad_q = turn(grad_q, cosine[start:stop], sine[start:stop])
            flip_ref[0, at : at + HD, start:stop] = grad_q.T.astype(BF)
            gq_ref[start:stop, at : at + HD] = grad_q.astype(BF)
        grad_k = turn(sum_k[...] * scale, cosine, sine)
        grad_v = sum_v[...]
        flip_ref[1, at : at + HD, :] = grad_k.T.astype(BF)
        flip_ref[2, at : at + HD, :] = grad_v.T.astype(BF)
        grad_k, grad_v = grad_k.astype(BF), grad_v.astype(BF)
        for block in range(size):
            rows = slice(block * part, (block + 1) * part)
            rk_ref[pl.ds(home(block * part), part), at : at + HD] = grad_k[rows]
            rv_ref[pl.ds(home(block * part), part), at : at + HD] = grad_v[rows]


def attend_backward(place, grads, weights, queries, keys, values, cosine, sine, at):
    arrays, picks = grads
    length, wide = queries.shape
    width = weights.shape[0]
    group = head_group(wide)
    groups = wide // group
    table = pl.BlockSpec((length, HD), lambda g: (0, 0))
    heads = pl.BlockSpec((length, group), lambda g: (0, at))
    outs = pl.BlockSpec((length, group), lambda g: (0, 0))
    out = jax.ShapeDtypeStruct((length, group), BF)
    return pl.pallas_call(
        functools.partial(backward_kernel, picks),
        grid=(1,),
        in_specs=[
            pl.BlockSpec(memory_space=pltpu.SMEM),
            pl.BlockSpec((width, group), lambda g: (0, at + 3 * groups)),
            heads,
            heads,
            heads,
            table,
            table,
        ]
        + [pl.BlockSpec(array.shape, lambda g: (0, 0, 0)) for array in arrays],
        out_specs=[outs] * 3 + [pl.BlockSpec((3, group, length), lambda g: (0, 0, 0))],
        out_shape=[out] * 3 + [jax.ShapeDtypeStruct((3, group, length), BF)],
        scratch_shapes=[
            pltpu.VMEM((length, group), BF),
            pltpu.VMEM((HD, length), BF),
            pltpu.VMEM((length, HD), F32),
            pltpu.VMEM((length, HD), F32),
        ],
        compiler_params=limits(),
        cost_estimate=estimate(
            flops=2 * length * width * group + 10 * length * length * group,
            bytes_accessed=2 * length * width + 2 * width * group + 18 * length * group,
            transcendentals=length * length * group // HD,
        ),
    )(place, weights, queries, keys, values, cosine, sine, *arrays)


def feed_kernel(x_ref, g_ref, wg_ref, wu_ref, wd_ref, act_ref, gate_ref, up_ref, flip_ref):
    gate = plain_dot(x_ref[...], wg_ref[...])
    up = plain_dot(x_ref[...], wu_ref[...])
    grad = plain_dot(g_ref[...], wd_ref[...])
    sigma = 1.0 / (1.0 + jnp.exp(-gate))
    silu = gate * sigma
    act = silu * up
    grad_up = grad * silu
    grad_gate = grad * up * (sigma + silu * (1.0 - sigma))
    act_ref[...] = act.astype(BF)
    up_ref[...] = grad_up.astype(BF)
    gate_ref[...] = grad_gate.astype(BF)
    flip_ref[0] = grad_gate.T.astype(BF)
    flip_ref[1] = grad_up.T.astype(BF)
    flip_ref[2] = act.T.astype(BF)


def feed_forward(ffn_in, grad_low, weights):
    length, width = ffn_in.shape
    units = weights.shape[1] // 3
    step = 256 if units % 256 == 0 else units if units <= 512 else 128
    steps = units // step
    whole = pl.BlockSpec((length, width), lambda f: (0, 0))
    out = pl.BlockSpec((length, step), lambda f: (0, f))
    return pl.pallas_call(
        feed_kernel,
        grid=(steps,),
        in_specs=[
            whole,
            whole,
            pl.BlockSpec((width, step), lambda f: (0, f)),
            pl.BlockSpec((width, step), lambda f: (0, f + steps)),
            pl.BlockSpec((width, step), lambda f: (0, f + 2 * steps)),
        ],
        out_specs=[out] * 3 + [pl.BlockSpec((3, step, length), lambda f: (0, f, 0))],
        out_shape=[jax.ShapeDtypeStruct((length, units), BF)] * 3
        + [jax.ShapeDtypeStruct((3, units, length), BF)],
        compiler_params=limits(),
        cost_estimate=estimate(
            flops=6 * length * width * units,
            bytes_accessed=4 * length * width + 6 * width * units + 12 * length * units,
            transcendentals=2 * length * units,
        ),
    )(ffn_in, grad_low, weights, weights, weights)


def products_kernel(counts, forms, *refs):
    step = pl.program_id(0)
    lefts, rights, out_ref = refs[: len(counts)], refs[len(counts) : -1], refs[-1]
    first = 0
    for (steps, right), left in zip(counts, lefts):

        @pl.when((step >= first) & (step < first + steps))
        def _(left=left, form=forms[right]):
            if isinstance(form, int):
                out_ref[...] = plain_dot(left[...], rights[form][...]).astype(BF)
                return
            start = 0
            for half in form:
                total = None
                for place, (array, index) in enumerate(half):
                    rows, columns = rights[array].shape[1:]
                    part = plain_dot(
                        left[:, place * rows : (place + 1) * rows], rights[array][index]
                    )
                    total = part if total is None else total + part
                out_ref[:, start : start + columns] = total.astype(BF)
                start += columns

        first += steps


def products(terms, rights):
    length = terms[0][0].shape[2]
    width = rights[0].shape[1]
    step = 256 if all(left.shape[1] % 256 == 0 for left, _, _ in terms) else 128
    counts = tuple((left.shape[1] // step, at) for left, _, at in terms)
    total = sum(steps for steps, _ in counts)
    arrays, forms = [], []
    for right in rights:
        if isinstance(right, tuple):
            more, picks = right
            forms.append([[(len(arrays) + at, index) for at, index in half] for half in picks])
            arrays += more
        else:
            forms.append(len(arrays))
            arrays.append(right)
    left_specs = []
    first = 0
    for (steps, _), (_, lead, _) in zip(counts, terms):

        def block(i, first=first, last=steps - 1, lead=lead):
            return (lead, lax.max(lax.min(i - first, last), 0), 0)

        left_specs.append(pl.BlockSpec((None, step, length), block))
        first += steps
    right_specs = [
        pl.BlockSpec(array.shape, lambda i, ndim=array.ndim: (0,) * ndim) for array in arrays
    ]
    return pl.pallas_call(
        functools.partial(products_kernel, counts, forms),
        grid=(total,),
        in_specs=left_specs + right_specs,
        out_specs=pl.BlockSpec((step, width), lambda i: (i, 0)),
        out_shape=jax.ShapeDtypeStruct((total * step, width), BF),
        compiler_params=limits(),
        cost_estimate=estimate(
            flops=2 * total * step * length * width,
            bytes_accessed=2 * (total * step * (length + width) + len(rights) * length * width),
            transcendentals=0,
        ),
    )(*[left for left, _, _ in terms], *arrays)


def rows_kernel(count, sides, steps, *refs):
    outs = refs[-2 * len(sides) :]
    lefts, rights = refs[: -2 * len(sides) - count], refs[-2 * len(sides) - count : -2 * len(sides)]
    for half in range(2):

        @pl.when(pl.program_id(0) // steps == half)
        def _(half=half):
            for number, side in enumerate(sides):
                for piece in range(2):
                    if len(sides) == 1:
                        row, parts = piece, 2
                    else:
                        row, parts = (2 * side + piece if half else 2 * piece + side), 4
                    total = None
                    for at, right in enumerate(rights):
                        part = last_dims(lefts[parts * at + row][...], right[...])
                        total = part if total is None else total + part
                    outs[2 * number + half][piece] = total.astype(BF)


def row_products(terms, sides, width):
    columns = width // 2
    step = 512 if columns % 512 == 0 else columns
    steps = columns // step
    left_specs, right_specs, lefts, rights = [], [], [], []
    flops = nbytes = 0
    for left, right, at in terms:
        rows, depth = left.shape[0] // 4, left.shape[1]
        for piece in range(2 * len(sides)):

            def block(j, piece=piece):
                if len(sides) == 2:
                    return (piece, 0)
                upper, side = j // steps, sides[0]
                return ((1 - upper) * (2 * piece + side) + upper * (2 * side + piece), 0)

            lefts.append(left)
            left_specs.append(pl.BlockSpec((rows, depth), block))
        right_specs.append(pl.BlockSpec((step, depth), lambda j, at=at: (j, at)))
        rights.append(right)
        flops += 8 * rows * depth * columns * len(sides)
        nbytes += 4 * depth * (2 * rows + columns)
    outs = pl.pallas_call(
        functools.partial(rows_kernel, len(terms), sides, steps),
        grid=(2 * steps,),
        in_specs=left_specs + right_specs,
        out_specs=[
            pl.BlockSpec((2, rows, step), lambda j: (0, 0, lax.min(j, steps - 1))),
            pl.BlockSpec((2, rows, step), lambda j: (0, 0, lax.max(j - steps, 0))),
        ]
        * len(sides),
        out_shape=[jax.ShapeDtypeStruct((2, rows, columns), BF)] * (2 * len(sides)),
        compiler_params=limits(),
        cost_estimate=estimate(
            flops=flops,
            bytes_accessed=nbytes + 8 * rows * columns * len(sides),
            transcendentals=0,
        ),
    )(*lefts, *rights)
    return [outs[2 * number : 2 * number + 2] for number in range(len(sides))]


def rms_scale(values, gain):
    inverse = lax.rsqrt(jnp.mean(values * values, axis=-1, keepdims=True) + epsilon)
    return (inverse, values * inverse * gain)


def norm_back(grad, values, inverse, gain):
    scaled = grad * gain
    inner = jnp.mean(scaled * values, axis=-1, keepdims=True)
    return inverse * scaled - values * inverse**3 * inner


def rotary_tables(length):
    position = jnp.arange(length, dtype=jnp.float32)
    freqs = jnp.exp(-jnp.log(10000.0) * jnp.arange(HD // 2, dtype=jnp.float32) * 2.0 / HD)
    angle = position[:, None] * freqs[None, :]
    cosine, sine = jnp.cos(angle), jnp.sin(angle)
    return (jnp.concatenate([cosine, cosine], 1), jnp.concatenate([-sine, sine], 1))


def after(value, *earlier):
    return lax.optimization_barrier((value, *earlier))[0]


def swap(array, bit, size):
    return lax.ppermute(array, "tensor", [(t, t ^ bit) for t in range(size)])


def bit_orders(size):
    bits = [1 << step for step in range(size.bit_length() - 1)]
    return (bits, bits[1:] + bits[:1])


def relative(array, me, size):
    part = array.shape[0] // size
    return jnp.stack(
        [lax.dynamic_slice_in_dim(array, (me ^ step) * part, part, 0) for step in range(size)]
    )


def scatter_sum(blocks):
    size = blocks.shape[0]
    half = blocks.shape[2] // 2
    sums = []
    for group, order in enumerate(bit_orders(size)):
        held = {
            place: blocks[place, :, group * half : (group + 1) * half].astype(F32)
            for place in range(size)
        }
        for bit in order:
            sent = [place for place in held if place & bit]
            got = swap(jnp.stack([held[place].astype(BF) for place in sent]), bit, size)
            held = {
                place ^ bit: held[place ^ bit] + got[at].astype(F32)
                for at, place in enumerate(sent)
            }
        sums.append(held[0])
    return jnp.concatenate(sums, axis=1)


def gather_start(own, size, group):
    return gather_step({0: (own[None], 0)}, bit_orders(size)[group][-1], size)


def gather_step(held, bit, size, earlier=()):
    places = list(held)
    sent = after([held[place][0][held[place][1]] for place in places], *earlier)
    got = swap(jnp.stack(sent), bit, size)
    return {**held, **{place ^ bit: (got, at) for at, place in enumerate(places)}}, got


def gather_end(held, size, group, earlier=()):
    got = None
    for bit in bit_orders(size)[group][-2::-1]:
        held, got = gather_step(held, bit, size, earlier)
    return [held[place] for place in range(size)], got


def halves_start(own, size):
    half = own.shape[1] // 2
    parts = (own[:, :half], own[:, half:])
    state = [gather_start(part, size, group) for group, part in enumerate(parts)]
    return [held for held, _ in state], [got for _, got in state]


def halves_end(state, size, earlier=()):
    ends = [gather_end(held, size, group, earlier) for group, held in enumerate(state)]
    return [parts for parts, _ in ends], [got for _, got in ends]


def gather_split(own, size, earlier=()):
    half = own.shape[1] // 2
    state, first, last = [], [], []
    for part, order in zip((own[:, :half], own[:, half:]), bit_orders(size)):
        held, came = {0: part}, []
        for bit in order[::-1]:
            for place in list(held):
                sent = after(held[place], *earlier) if place else held[place]
                held[place ^ bit] = swap(sent, bit, size)
                came.append(held[place ^ bit])
        state.append([(held[place][None], 0) for place in range(size)])
        first.append(came[0])
        last.append(came[-1])
    return state, first, last


def assemble_kernel(cases, shift_ref, *refs):
    out_ref = refs[-1]
    place = pl.program_id(0) ^ shift_ref[0]
    for case, picks in enumerate(cases):

        @pl.when(place == case)
        def _(picks=picks):
            columns = 0
            for at, index in picks:
                part = refs[at][index]
                out_ref[:, columns : columns + part.shape[1]] = part.astype(out_ref.dtype)
                columns += part.shape[1]


def arrays_of(halves):
    arrays, picks = [], []
    for parts in halves:
        picks.append([])
        for array, index in parts:
            known = [at for at, other in enumerate(arrays) if other is array]
            if not known:
                arrays.append(array)
            picks[-1].append((known[0] if known else len(arrays) - 1, index))
    return arrays, picks


def assemble(halves, shift, dtype):
    arrays, picks = arrays_of(halves)
    size = len(picks[0])
    rows = arrays[0].shape[1]
    width = sum(parts[0][0].shape[2] for parts in halves)
    return pl.pallas_call(
        functools.partial(assemble_kernel, list(zip(*picks))),
        grid=(size,),
        in_specs=[pl.BlockSpec(memory_space=pltpu.SMEM)]
        + [pl.BlockSpec(array.shape, lambda r: (0, 0, 0)) for array in arrays],
        out_specs=pl.BlockSpec((rows, width), lambda r: (r, 0)),
        out_shape=jax.ShapeDtypeStruct((size * rows, width), dtype),
        compiler_params=limits(),
        cost_estimate=estimate(
            flops=size * rows * width, bytes_accessed=6 * size * rows * width, transcendentals=0
        ),
    )(shift, *arrays)


def scatter_start(terms, size, width, free=(), together=False):
    if size != 4:
        total = 0.0
        for left, right, at in terms:
            depth = left.shape[1]
            total = total + last_dims(left, right[:, at * depth : (at + 1) * depth])
        return total, [total], [total], [total]
    if together:
        sent, kept = row_products(terms, (1, 0), width)
    else:
        (sent,) = row_products(terms, (1,), width)
        lefts = after([left for left, _, _ in terms], *sent)
        terms = [(left, right, at) for left, (_, right, at) in zip(lefts, terms)]
        (kept,) = row_products(terms, (0,), width)
    if free:
        free = (*free, *kept)
    first = [swap(after(sent[half], *free), 1 + half, size) for half in range(2)]
    return (first, kept), sent, first, kept


def scatter_end(state, size, width, earlier=()):
    if size != 4:
        total = scatter_sum(state.reshape(size, -1, width))
        return total, [total], [total]
    first, kept = state
    first = after(first, *earlier)
    held = [kept[half].astype(F32) + first[half].astype(F32) for half in range(2)]
    sent = [held[half][1].astype(BF) for half in range(2)]
    last = [swap(sent[half], 2 - half, size) for half in range(2)]
    total = [held[half][0] + last[half].astype(F32) for half in range(2)]
    return jnp.concatenate(total, axis=1), sent, last


def input_kernel(picks, sizes, place_ref, hidden_ref, mid_ref, gain_ref, *refs):
    lower = place_ref[2] == 0
    out_ref = refs[-1]
    heads_picks, mine_picks, other_picks = picks
    heads_size, weights_size = sizes
    parts = []
    for weights_picks in (mine_picks, other_picks):
        total = None
        for half, parts_of in enumerate(weights_picks):
            start = half * weights_size
            heads_of = heads_picks[start // heads_size]
            start = start % heads_size
            for (head, row), (weight, place) in zip(heads_of, parts_of):
                left = refs[head][row, :, start : start + weights_size]
                part = last_dims(left, refs[weight][place])
                total = part if total is None else total + part
        parts.append(total)
    grad = jnp.concatenate(
        [jnp.where(lower, parts[0], parts[1]), jnp.where(lower, parts[1], parts[0])], axis=1
    )
    values = hidden_ref[...].astype(F32)
    inverse = lax.rsqrt(jnp.mean(values * values, axis=1, keepdims=True) + epsilon)
    scaled = grad * gain_ref[...]
    inner = jnp.mean(scaled * values, axis=1, keepdims=True)
    out_ref[...] = (
        mid_ref[...].astype(F32) + inverse * scaled - values * (inverse**3 * inner)
    )


def input_gradient(place, heads, mine, other, hidden_in, grad_mid, gain, size):
    length, width = hidden_in.shape
    rows = length // size
    arrays, picks = [], []
    for group in (heads, mine, other):
        more, at = arrays_of(group)
        picks.append([[(len(arrays) + array, index) for array, index in part] for part in at])
        arrays += more
        if group is heads:
            count = len(arrays)
    sizes = (heads[0][0][0].shape[2], mine[0][0][0].shape[2])
    wide = sum(part[0][0].shape[2] for part in heads)
    return pl.pallas_call(
        functools.partial(input_kernel, picks, sizes),
        grid_spec=pltpu.PrefetchScalarGridSpec(
            num_scalar_prefetch=1,
            grid=(size,),
            in_specs=[
                pl.BlockSpec((rows, width), lambda r, place: (r, 0)),
                pl.BlockSpec((rows, width), lambda r, place: (r ^ place[0], 0)),
                pl.BlockSpec((1, width), lambda r, place: (0, 0)),
            ]
            + [
                pl.BlockSpec((array.shape[0], rows, array.shape[2]), lambda r, place: (0, r, 0))
                for array in arrays[:count]
            ]
            + [pl.BlockSpec(array.shape, lambda r, place: (0, 0, 0)) for array in arrays[count:]],
            out_specs=pl.BlockSpec((rows, width), lambda r, place: (r, 0)),
        ),
        out_shape=jax.ShapeDtypeStruct((length, width), F32),
        compiler_params=limits(),
        cost_estimate=estimate(
            flops=2 * length * width * wide * size,
            bytes_accessed=2 * size * wide * (length + width) + 8 * length * width,
            transcendentals=length,
        ),
    )(place, hidden_in, grad_mid, gain[None], *arrays)


def local(
    hidden_in,
    self_out,
    out_grad,
    lengths,
    w_query,
    w_key,
    w_value,
    w_output,
    w_gate,
    w_up,
    w_down,
    attn_gain,
    ffn_gain,
    kv_gain,
):
    me = lax.axis_index("tensor")
    size = lax.axis_size("tensor")
    dp_size = lax.axis_size("dp")
    length, width = hidden_in.shape
    quarter = length // size
    wide, units = w_query.shape[1], w_gate.shape[1]
    early = units * 3 // 4 // 256 * 256
    late = round_up(units - early, 128)

    def columns(array, start, count):
        kept = array[:, start : start + count]
        return jnp.pad(kept, ((0, 0), (0, count - kept.shape[1])))

    w_flip = w_down.T
    mine = [jnp.concatenate([w_query, w_key, w_value, w_output.T], axis=1)]
    for start, count in ((0, early), (early, late)):
        mine.append(
            jnp.concatenate([columns(w, start, count) for w in (w_gate, w_up, w_flip)], axis=1)
        )
    w_heads, w_early, w_late = [lax.all_gather(w, "dp", axis=0, tiled=True) for w in mine]
    gains = lax.all_gather(jnp.stack([attn_gain, ffn_gain, kv_gain]), "dp", axis=1, tiled=True)
    gains = gains.astype(F32)
    attn_scale, ffn_scale, kv_scale = gains[0], gains[1], gains[2]

    core = lax.axis_index("dp") % 2
    place = jnp.stack([me, lengths[0], core])
    valid = jnp.arange(length, dtype=jnp.int32) < lengths[0]
    cosine, sine = rotary_tables(length)
    hidden = hidden_in.astype(F32)
    selfout = self_out.astype(F32)
    x_inverse, x_normed = rms_scale(hidden, attn_scale)
    normed = x_normed.astype(BF)
    s_inverse, s_normed = rms_scale(selfout, kv_scale)
    kv_normed = s_normed.astype(BF)

    def own_rows(array):
        return lax.dynamic_slice_in_dim(array, me * quarter, quarter, 0)

    hidden_own = own_rows(hidden_in).astype(F32)
    self_own = own_rows(self_out).astype(F32)
    grad_y_low = relative(jnp.where(valid[:, None], out_grad, jnp.zeros((), BF)), me, size)
    grad_y = grad_y_low[0].astype(F32)
    grad_y_low = grad_y_low.reshape(length, width)

    queries, keys, values, attended_low, attended_flip = attend_forward(
        place, normed, kv_normed, w_heads, cosine, sine, size
    )
    state, _, _, _ = scatter_start([(attended_low, w_heads, 3)], size, width)
    mid_sum, _, _ = scatter_end(state, size, width)
    mid = hidden_own + mid_sum
    m_inverse, m_normed = rms_scale(mid, ffn_scale)
    held, _ = halves_start(m_normed.astype(BF), size)
    parts, ffn_last = halves_end(held, size)
    still = jnp.zeros((1,), jnp.int32)
    ffn_in = assemble(parts, still, BF)

    half_rows = lax.dynamic_slice_in_dim(w_heads[:, :wide], core * (width // 2), width // 2, 0)
    held, _ = halves_start(after(half_rows, *ffn_last), size)
    query_mine, query_last = halves_end(held, size)

    act_early, gate_early, up_early, flip_early = feed_forward(ffn_in, grad_y_low, w_early)

    def unit_grads(flip):
        return products([(flip, 0, 0), (flip, 1, 0), (flip, 2, 1)], [ffn_in, grad_y_low])

    grads_early = unit_grads(flip_early)
    sum_early = lax.psum_scatter(after(grads_early, w_late, *query_last), "dp", scatter_dimension=1, tiled=True)
    act_late, gate_late, up_late, flip_late = feed_forward(
        after(ffn_in, grads_early), grad_y_low, w_late
    )
    state, _, _, _ = scatter_start(
        [
            (gate_early, w_early, 0),
            (up_early, w_early, 1),
            (gate_late, w_late, 0),
            (up_late, w_late, 1),
        ],
        size,
        width,
    )
    back_sum, _, _ = scatter_end(state, size, width)
    mid_part = norm_back(back_sum, mid, m_inverse, ffn_scale)
    grad_mid = grad_y + mid_part
    mid_low = grad_mid.astype(BF)
    parts, mid_first, mid_last = gather_split(mid_low, size)
    mid_arrays, mid_picks = arrays_of(parts)
    act_early, act_late = after((act_early, act_late), *mid_first)
    out_state, _, out_first, out_kept = scatter_start(
        [(act_early, w_early, 2), (act_late, w_late, 2)], size, width, free=mid_last
    )
    grads_late = unit_grads(after(flip_late, mid_low))
    sum_late = lax.psum_scatter(
        after(grads_late, *mid_first), "dp", scatter_dimension=1, tiled=True
    )
    mid_arrays = after(mid_arrays, grads_late, *out_kept)

    group = head_group(wide)
    groups = wide // group
    backs, heads_held, q_first = [], [], []
    grad_in = mid_arrays
    for at in range(groups):
        backs.append(
            attend_backward(
                place, (grad_in, mid_picks), w_heads, queries, keys, values, cosine, sine, at
            )
        )
        held, first = gather_start(backs[-1][0], size, at % 2)
        heads_held.append(held)
        q_first.append(first)
        grad_in = after(mid_arrays, backs[-1][0])
    kv_terms = [(backs[at][1], w_heads, at + groups) for at in range(groups)]
    kv_terms += [(backs[at][2], w_heads, at + 2 * groups) for at in range(groups)]
    lefts = after([left for left, _, _ in kv_terms], *out_first, *q_first[:-1])
    kv_terms = [(left, right, at) for left, (_, right, at) in zip(lefts, kv_terms)]
    kv_state, kv_sent, kv_first, kv_kept = scatter_start(
        kv_terms, size, width, together=True
    )
    grad_kv_normed, kv_more, kv_last = scatter_end(kv_state, size, width)
    heads_q, q_last = [], []
    for at in range(groups):
        parts, last = gather_end(heads_held[at], size, at % 2, kv_kept)
        heads_q.append(parts)
        q_last.append(last)
    out_sum, out_more, out_last = scatter_end(out_state, size, width, kv_more)
    layer_own = (mid + out_sum).astype(BF)
    layer_held, layer_first = halves_start(layer_own, size)
    layer_parts, _ = halves_end(layer_held, size)
    layer_out = assemble(layer_parts, place, BF)
    grads_heads = products(
        [(backs[at][3], lead, min(lead, 1)) for lead in range(3) for at in range(groups)]
        + [(attended_flip[None], 0, 2)],
        [after(normed, sum_early, *kv_kept), kv_normed, (mid_arrays, mid_picks)],
    )
    grads_heads = after(grads_heads, *kv_first, *q_last)
    sum_heads = lax.psum_scatter(grads_heads, "dp", scatter_dimension=1, tiled=True).astype(F32)
    def unit_sums(at):
        early_rows = sum_early[at * early : (at + 1) * early]
        late_rows = sum_late[at * late : at * late + units - early]
        return jnp.concatenate([early_rows, late_rows], axis=0).astype(F32)

    def gain_part(gain, *pairs):
        total = 0.0
        for weights, grads in pairs:
            total = total + jnp.sum(weights.astype(F32) * grads, axis=1)
        return total / gain.astype(F32)

    s_part = norm_back(grad_kv_normed, self_own, own_rows(s_inverse), kv_scale)
    self_own_grad = s_part.astype(BF)
    self_held, self_first = halves_start(self_own_grad, size)

    weights_in = after((w_gate, w_up), *self_first)
    sum_gate, sum_up, sum_down = unit_sums(0).T, unit_sums(1).T, unit_sums(2)
    ffn_gain_sum = gain_part(ffn_gain, (weights_in[0], sum_gate), (weights_in[1], sum_up))

    mid_parts = [[(mid_arrays[at], index) for at, index in part] for part in mid_picks]
    grad_mid_low = assemble(mid_parts, after(still, self_own_grad), BF)

    query_arrays, query_picks = arrays_of(query_mine)
    other_arrays = [
        lax.ppermute(array, "dp", [(i, i ^ 1) for i in range(dp_size)])
        for array in after(query_arrays, *kv_more)
    ]
    query_other = [[(other_arrays[at], index) for at, index in part] for part in query_picks]
    input_grad = input_gradient(
        place,
        heads_q,
        query_mine,
        query_other,
        after(hidden_in, self_own_grad),
        grad_mid_low,
        attn_scale,
        size,
    )
    self_parts, _ = halves_end(self_held, size, [input_grad])
    weights_in = after((w_query, w_key, w_value), *self_first)
    sum_query, sum_key, sum_value = [
        sum_heads[at * wide : (at + 1) * wide].T for at in range(3)
    ]
    gain_sums = jnp.stack(
        [
            gain_part(attn_gain, (weights_in[0], sum_query)),
            ffn_gain_sum,
            gain_part(kv_gain, (weights_in[1], sum_key), (weights_in[2], sum_value)),
        ]
    )
    self_grad = assemble(self_parts, after(place, gain_sums), F32)
    others = [
        lax.ppermute(gain_sums, "tensor", [(t, t ^ step) for t in range(size)])
        for step in range(1, size)
    ]
    for other in others:
        gain_sums = gain_sums + other

    return (
        layer_out,
        input_grad,
        self_grad,
        sum_query,
        sum_key,
        sum_value,
        sum_heads[3 * wide :],
        sum_gate,
        sum_up,
        sum_down,
        gain_sums[0],
        gain_sums[1],
        gain_sums[2],
    )


def solution(mesh):
    placed = (
        P("dp", None),
        P("dp", None),
        P("dp", None),
        P("dp"),
        P("dp", "tensor"),
        P("dp", "tensor"),
        P("dp", "tensor"),
        P("tensor", "dp"),
        P("dp", "tensor"),
        P("dp", "tensor"),
        P("tensor", "dp"),
        P("dp"),
        P("dp"),
        P("dp"),
    )
    return jax.shard_map(
        local,
        mesh=mesh,
        in_specs=placed,
        out_specs=(
            P("dp", None),
            P("dp", None),
            P("dp", None),
            P("dp", "tensor"),
            P("dp", "tensor"),
            P("dp", "tensor"),
            P("tensor", "dp"),
            P("dp", "tensor"),
            P("dp", "tensor"),
            P("tensor", "dp"),
            P("dp"),
            P("dp"),
            P("dp"),
        ),
        check_vma=False,
    )
```

```python
import functools

import jax
import jax.numpy as jnp
from jax import lax
from jax.experimental import pallas as pl
from jax.experimental.pallas import tpu as pltpu
from jax.sharding import PartitionSpec as P

HD = 128
QROWS = 256
BF = jnp.bfloat16
F32 = jnp.float32
epsilon = 1e-06
VMEM_LIMIT = 60 * 1024 * 1024
WEIGHT = 1


def plain_dot(left, right):
    return jnp.dot(left, right, preferred_element_type=jnp.float32)


def last_dims(left, right):
    return lax.dot_general(
        left, right, (((1,), (1,)), ((), ())), preferred_element_type=jnp.float32
    )


def round_up(number, unit):
    return (number + unit - 1) // unit * unit


def head_group(wide):
    return 2 * HD if wide % (2 * HD) == 0 else HD


def limits():
    return pltpu.CompilerParams(vmem_limit_bytes=VMEM_LIMIT)


def estimate(flops, bytes_accessed, transcendentals):
    return pl.CostEstimate(
        flops=flops // WEIGHT,
        bytes_accessed=bytes_accessed // WEIGHT,
        transcendentals=transcendentals // WEIGHT,
    )


def turn(values, cosine, sine):
    return values * cosine + pltpu.roll(values, HD // 2, 1) * sine


def forward_kernel(
    size,
    place_ref,
    normed_ref,
    kv_ref,
    wq_ref,
    wk_ref,
    wv_ref,
    cos_ref,
    sin_ref,
    q_ref,
    k_ref,
    v_ref,
    out_ref,
    flip_ref,
):
    me, live = place_ref[0], place_ref[1]
    length = normed_ref.shape[0]
    group = wq_ref.shape[1]
    part = length // size
    cosine, sine = cos_ref[...], sin_ref[...]
    q_pre = plain_dot(normed_ref[...], wq_ref[...])
    for at in range(0, group, HD):
        q_ref[:, at : at + HD] = turn(q_pre[:, at : at + HD], cosine, sine).astype(BF)
    k_pre = plain_dot(kv_ref[...], wk_ref[...])
    for at in range(0, group, HD):
        k_ref[:, at : at + HD] = turn(k_pre[:, at : at + HD], cosine, sine).astype(BF)
    v_ref[...] = plain_dot(kv_ref[...], wv_ref[...]).astype(BF)
    for at in range(0, group, HD):
        for start in range(0, length, QROWS):
            stop = start + QROWS
            scores = last_dims(q_ref[start:stop, at : at + HD], k_ref[:stop, at : at + HD])
            scores = scores * HD ** (-0.5)
            rows = start + lax.broadcasted_iota(jnp.int32, (QROWS, 1), 0)
            bound = jnp.minimum(rows, live - 1)
            columns = lax.broadcasted_iota(jnp.int32, (QROWS, stop), 1)
            scores = jnp.where(columns <= bound, scores, -1e30)
            largest = jnp.max(scores, axis=1, keepdims=True)
            expo = jnp.exp(scores - largest)
            probs = (expo / jnp.sum(expo, axis=1, keepdims=True)).astype(BF)
            result = plain_dot(probs, v_ref[:stop, at : at + HD])
            flipped = result.T.astype(BF)
            result = result.astype(BF)
            step = min(part, QROWS)
            for piece in range(0, QROWS, step):
                block = (start + piece) // part
                row = pl.multiple_of((block ^ me) * part, part) + (start + piece) % part
                rows_at = pl.ds(pl.multiple_of(row, 128), step)
                out_ref[rows_at, at : at + HD] = result[piece : piece + step]
                flip_ref[at : at + HD, rows_at] = flipped[:, piece : piece + step]


def attend_forward(place, normed, kv_normed, weights, cosine, sine, size):
    length, width = normed.shape
    wide = weights.shape[1] // 4
    group = head_group(wide)
    groups = wide // group
    whole = pl.BlockSpec((length, width), lambda g: (0, 0))
    table = pl.BlockSpec((length, HD), lambda g: (0, 0))
    heads = pl.BlockSpec((length, group), lambda g: (0, g))
    out = jax.ShapeDtypeStruct((length, wide), BF)
    return pl.pallas_call(
        functools.partial(forward_kernel, size),
        grid=(groups,),
        in_specs=[
            pl.BlockSpec(memory_space=pltpu.SMEM),
            whole,
            whole,
            pl.BlockSpec((width, group), lambda g: (0, g)),
            pl.BlockSpec((width, group), lambda g: (0, g + groups)),
            pl.BlockSpec((width, group), lambda g: (0, g + 2 * groups)),
            table,
            table,
        ],
        out_specs=[heads] * 4 + [pl.BlockSpec((group, length), lambda g: (g, 0))],
        out_shape=[out] * 4 + [jax.ShapeDtypeStruct((wide, length), BF)],
        compiler_params=limits(),
        cost_estimate=estimate(
            flops=6 * length * width * wide + 3 * length * length * wide,
            bytes_accessed=4 * length * width + 6 * width * wide + 8 * length * wide,
            transcendentals=length * length * wide // HD,
        ),
    )(place, normed, kv_normed, weights, weights, weights, cosine, sine)


def backward_kernel(
    picks,
    place_ref,
    wo_ref,
    q_ref,
    k_ref,
    v_ref,
    cos_ref,
    sin_ref,
    *refs,
):
    gq_ref, rk_ref, rv_ref, flip_ref, ga_ref, kt_ref, sum_k, sum_v = refs[-8:]
    me, live = place_ref[0], place_ref[1]
    length = q_ref.shape[0]
    size = len(picks[0])
    group = wo_ref.shape[1]
    part = length // size
    scale = HD ** (-0.5)
    cosine, sine = cos_ref[...], -sin_ref[...]

    def home(row):
        block = row // part
        return pl.multiple_of(pl.multiple_of((block ^ me) * part, part) + row % part, 128)

    for block in range(size):
        total, start = None, 0
        for half in picks:
            array, index = half[block]
            stop = start + refs[array].shape[2]
            term = plain_dot(refs[array][index], wo_ref[start:stop, :])
            total = term if total is None else total + term
            start = stop
        ga_ref[pl.ds(home(block * part), part), :] = total.astype(BF)
    for at in range(0, group, HD):
        kt_ref[...] = k_ref[:, at : at + HD].T
        for start in reversed(range(0, length, QROWS)):
            stop = start + QROWS
            queries = q_ref[start:stop, at : at + HD]
            grads = ga_ref[start:stop, at : at + HD]
            scores = last_dims(k_ref[:stop, at : at + HD], queries) * scale
            columns = start + lax.broadcasted_iota(jnp.int32, (1, QROWS), 1)
            bound = jnp.minimum(columns, live - 1)
            rows = lax.broadcasted_iota(jnp.int32, (stop, QROWS), 0)
            scores = jnp.where(rows <= bound, scores, -1e30)
            largest = jnp.max(scores, axis=0, keepdims=True)
            expo = jnp.exp(scores - largest)
            probs = expo * (1.0 / jnp.sum(expo, axis=0, keepdims=True))
            grad_probs = last_dims(v_ref[:stop, at : at + HD], grads)
            inner = jnp.sum(probs * grad_probs, axis=0, keepdims=True)
            grad_scores = (probs * (grad_probs - inner)).astype(BF)
            add_k = plain_dot(grad_scores, queries)
            add_v = plain_dot(probs.astype(BF), grads)
            if stop == length:
                sum_k[...] = add_k
                sum_v[...] = add_v
            else:
                sum_k[:stop] += add_k
                sum_v[:stop] += add_v
            grad_q = plain_dot(kt_ref[:, :stop], grad_scores).T * scale
            grad_q = turn(grad_q, cosine[start:stop], sine[start:stop])
            flip_ref[0, at : at + HD, start:stop] = grad_q.T.astype(BF)
            gq_ref[start:stop, at : at + HD] = grad_q.astype(BF)
        grad_k = turn(sum_k[...] * scale, cosine, sine)
        grad_v = sum_v[...]
        flip_ref[1, at : at + HD, :] = grad_k.T.astype(BF)
        flip_ref[2, at : at + HD, :] = grad_v.T.astype(BF)
        grad_k, grad_v = grad_k.astype(BF), grad_v.astype(BF)
        for block in range(size):
            rows = slice(block * part, (block + 1) * part)
            rk_ref[pl.ds(home(block * part), part), at : at + HD] = grad_k[rows]
            rv_ref[pl.ds(home(block * part), part), at : at + HD] = grad_v[rows]


def attend_backward(place, grads, weights, queries, keys, values, cosine, sine, at):
    arrays, picks = grads
    length, wide = queries.shape
    width = weights.shape[0]
    group = head_group(wide)
    groups = wide // group
    table = pl.BlockSpec((length, HD), lambda g: (0, 0))
    heads = pl.BlockSpec((length, group), lambda g: (0, at))
    outs = pl.BlockSpec((length, group), lambda g: (0, 0))
    out = jax.ShapeDtypeStruct((length, group), BF)
    return pl.pallas_call(
        functools.partial(backward_kernel, picks),
        grid=(1,),
        in_specs=[
            pl.BlockSpec(memory_space=pltpu.SMEM),
            pl.BlockSpec((width, group), lambda g: (0, at + 3 * groups)),
            heads,
            heads,
            heads,
            table,
            table,
        ]
        + [pl.BlockSpec(array.shape, lambda g: (0, 0, 0)) for array in arrays],
        out_specs=[outs] * 3 + [pl.BlockSpec((3, group, length), lambda g: (0, 0, 0))],
        out_shape=[out] * 3 + [jax.ShapeDtypeStruct((3, group, length), BF)],
        scratch_shapes=[
            pltpu.VMEM((length, group), BF),
            pltpu.VMEM((HD, length), BF),
            pltpu.VMEM((length, HD), F32),
            pltpu.VMEM((length, HD), F32),
        ],
        compiler_params=limits(),
        cost_estimate=estimate(
            flops=2 * length * width * group + 10 * length * length * group,
            bytes_accessed=2 * length * width + 2 * width * group + 18 * length * group,
            transcendentals=length * length * group // HD,
        ),
    )(place, weights, queries, keys, values, cosine, sine, *arrays)


def feed_kernel(x_ref, g_ref, wg_ref, wu_ref, wd_ref, act_ref, gate_ref, up_ref, flip_ref):
    gate = plain_dot(x_ref[...], wg_ref[...])
    up = plain_dot(x_ref[...], wu_ref[...])
    grad = plain_dot(g_ref[...], wd_ref[...])
    sigma = 1.0 / (1.0 + jnp.exp(-gate))
    silu = gate * sigma
    act = silu * up
    grad_up = grad * silu
    grad_gate = grad * up * (sigma + silu * (1.0 - sigma))
    act_ref[...] = act.astype(BF)
    up_ref[...] = grad_up.astype(BF)
    gate_ref[...] = grad_gate.astype(BF)
    flip_ref[0] = grad_gate.T.astype(BF)
    flip_ref[1] = grad_up.T.astype(BF)
    flip_ref[2] = act.T.astype(BF)


def feed_forward(ffn_in, grad_low, weights):
    length, width = ffn_in.shape
    units = weights.shape[1] // 3
    step = 256 if units % 256 == 0 else units if units <= 512 else 128
    steps = units // step
    whole = pl.BlockSpec((length, width), lambda f: (0, 0))
    out = pl.BlockSpec((length, step), lambda f: (0, f))
    return pl.pallas_call(
        feed_kernel,
        grid=(steps,),
        in_specs=[
            whole,
            whole,
            pl.BlockSpec((width, step), lambda f: (0, f)),
            pl.BlockSpec((width, step), lambda f: (0, f + steps)),
            pl.BlockSpec((width, step), lambda f: (0, f + 2 * steps)),
        ],
        out_specs=[out] * 3 + [pl.BlockSpec((3, step, length), lambda f: (0, f, 0))],
        out_shape=[jax.ShapeDtypeStruct((length, units), BF)] * 3
        + [jax.ShapeDtypeStruct((3, units, length), BF)],
        compiler_params=limits(),
        cost_estimate=estimate(
            flops=6 * length * width * units,
            bytes_accessed=4 * length * width + 6 * width * units + 12 * length * units,
            transcendentals=2 * length * units,
        ),
    )(ffn_in, grad_low, weights, weights, weights)


def products_kernel(counts, forms, *refs):
    step = pl.program_id(0)
    lefts, rights, out_ref = refs[: len(counts)], refs[len(counts) : -1], refs[-1]
    first = 0
    for (steps, right), left in zip(counts, lefts):

        @pl.when((step >= first) & (step < first + steps))
        def _(left=left, form=forms[right]):
            if isinstance(form, int):
                out_ref[...] = plain_dot(left[...], rights[form][...]).astype(BF)
                return
            start = 0
            for half in form:
                total = None
                for place, (array, index) in enumerate(half):
                    rows, columns = rights[array].shape[1:]
                    part = plain_dot(
                        left[:, place * rows : (place + 1) * rows], rights[array][index]
                    )
                    total = part if total is None else total + part
                out_ref[:, start : start + columns] = total.astype(BF)
                start += columns

        first += steps


def products(terms, rights):
    length = terms[0][0].shape[2]
    width = rights[0].shape[1]
    step = 256 if all(left.shape[1] % 256 == 0 for left, _, _ in terms) else 128
    counts = tuple((left.shape[1] // step, at) for left, _, at in terms)
    total = sum(steps for steps, _ in counts)
    arrays, forms = [], []
    for right in rights:
        if isinstance(right, tuple):
            more, picks = right
            forms.append([[(len(arrays) + at, index) for at, index in half] for half in picks])
            arrays += more
        else:
            forms.append(len(arrays))
            arrays.append(right)
    left_specs = []
    first = 0
    for (steps, _), (_, lead, _) in zip(counts, terms):

        def block(i, first=first, last=steps - 1, lead=lead):
            return (lead, lax.max(lax.min(i - first, last), 0), 0)

        left_specs.append(pl.BlockSpec((None, step, length), block))
        first += steps
    right_specs = [
        pl.BlockSpec(array.shape, lambda i, ndim=array.ndim: (0,) * ndim) for array in arrays
    ]
    return pl.pallas_call(
        functools.partial(products_kernel, counts, forms),
        grid=(total,),
        in_specs=left_specs + right_specs,
        out_specs=pl.BlockSpec((step, width), lambda i: (i, 0)),
        out_shape=jax.ShapeDtypeStruct((total * step, width), BF),
        compiler_params=limits(),
        cost_estimate=estimate(
            flops=2 * total * step * length * width,
            bytes_accessed=2 * (total * step * (length + width) + len(rights) * length * width),
            transcendentals=0,
        ),
    )(*[left for left, _, _ in terms], *arrays)


def rows_kernel(count, sides, steps, *refs):
    outs = refs[-2 * len(sides) :]
    lefts, rights = refs[: -2 * len(sides) - count], refs[-2 * len(sides) - count : -2 * len(sides)]
    for half in range(2):

        @pl.when(pl.program_id(0) // steps == half)
        def _(half=half):
            for number, side in enumerate(sides):
                for piece in range(2):
                    if len(sides) == 1:
                        row, parts = piece, 2
                    else:
                        row, parts = (2 * side + piece if half else 2 * piece + side), 4
                    total = None
                    for at, right in enumerate(rights):
                        part = last_dims(lefts[parts * at + row][...], right[...])
                        total = part if total is None else total + part
                    outs[2 * number + half][piece] = total.astype(BF)


def row_products(terms, sides, width):
    columns = width // 2
    step = 512 if columns % 512 == 0 else columns
    steps = columns // step
    left_specs, right_specs, lefts, rights = [], [], [], []
    flops = nbytes = 0
    for left, right, at in terms:
        rows, depth = left.shape[0] // 4, left.shape[1]
        for piece in range(2 * len(sides)):

            def block(j, piece=piece):
                if len(sides) == 2:
                    return (piece, 0)
                upper, side = j // steps, sides[0]
                return ((1 - upper) * (2 * piece + side) + upper * (2 * side + piece), 0)

            lefts.append(left)
            left_specs.append(pl.BlockSpec((rows, depth), block))
        right_specs.append(pl.BlockSpec((step, depth), lambda j, at=at: (j, at)))
        rights.append(right)
        flops += 8 * rows * depth * columns * len(sides)
        nbytes += 4 * depth * (2 * rows + columns)
    outs = pl.pallas_call(
        functools.partial(rows_kernel, len(terms), sides, steps),
        grid=(2 * steps,),
        in_specs=left_specs + right_specs,
        out_specs=[
            pl.BlockSpec((2, rows, step), lambda j: (0, 0, lax.min(j, steps - 1))),
            pl.BlockSpec((2, rows, step), lambda j: (0, 0, lax.max(j - steps, 0))),
        ]
        * len(sides),
        out_shape=[jax.ShapeDtypeStruct((2, rows, columns), BF)] * (2 * len(sides)),
        compiler_params=limits(),
        cost_estimate=estimate(
            flops=flops,
            bytes_accessed=nbytes + 8 * rows * columns * len(sides),
            transcendentals=0,
        ),
    )(*lefts, *rights)
    return [outs[2 * number : 2 * number + 2] for number in range(len(sides))]


def rms_scale(values, gain):
    inverse = lax.rsqrt(jnp.mean(values * values, axis=-1, keepdims=True) + epsilon)
    return (inverse, values * inverse * gain)


def norm_back(grad, values, inverse, gain):
    scaled = grad * gain
    inner = jnp.mean(scaled * values, axis=-1, keepdims=True)
    return inverse * scaled - values * inverse**3 * inner


def rotary_tables(length):
    position = jnp.arange(length, dtype=jnp.float32)
    freqs = jnp.exp(-jnp.log(10000.0) * jnp.arange(HD // 2, dtype=jnp.float32) * 2.0 / HD)
    angle = position[:, None] * freqs[None, :]
    cosine, sine = jnp.cos(angle), jnp.sin(angle)
    return (jnp.concatenate([cosine, cosine], 1), jnp.concatenate([-sine, sine], 1))


def after(value, *earlier):
    return lax.optimization_barrier((value, *earlier))[0]


def swap(array, bit, size):
    return lax.ppermute(array, "tensor", [(t, t ^ bit) for t in range(size)])


def bit_orders(size):
    bits = [1 << step for step in range(size.bit_length() - 1)]
    return (bits, bits[1:] + bits[:1])


def relative(array, me, size):
    part = array.shape[0] // size
    return jnp.stack(
        [lax.dynamic_slice_in_dim(array, (me ^ step) * part, part, 0) for step in range(size)]
    )


def scatter_sum(blocks):
    size = blocks.shape[0]
    half = blocks.shape[2] // 2
    sums = []
    for group, order in enumerate(bit_orders(size)):
        held = {
            place: blocks[place, :, group * half : (group + 1) * half].astype(F32)
            for place in range(size)
        }
        for bit in order:
            sent = [place for place in held if place & bit]
            got = swap(jnp.stack([held[place].astype(BF) for place in sent]), bit, size)
            held = {
                place ^ bit: held[place ^ bit] + got[at].astype(F32)
                for at, place in enumerate(sent)
            }
        sums.append(held[0])
    return jnp.concatenate(sums, axis=1)


def gather_start(own, size, group):
    return gather_step({0: (own[None], 0)}, bit_orders(size)[group][-1], size)


def gather_step(held, bit, size, earlier=()):
    places = list(held)
    sent = after([held[place][0][held[place][1]] for place in places], *earlier)
    got = swap(jnp.stack(sent), bit, size)
    return {**held, **{place ^ bit: (got, at) for at, place in enumerate(places)}}, got


def gather_end(held, size, group, earlier=()):
    got = None
    for bit in bit_orders(size)[group][-2::-1]:
        held, got = gather_step(held, bit, size, earlier)
    return [held[place] for place in range(size)], got


def halves_start(own, size):
    half = own.shape[1] // 2
    parts = (own[:, :half], own[:, half:])
    state = [gather_start(part, size, group) for group, part in enumerate(parts)]
    return [held for held, _ in state], [got for _, got in state]


def halves_end(state, size, earlier=()):
    ends = [gather_end(held, size, group, earlier) for group, held in enumerate(state)]
    return [parts for parts, _ in ends], [got for _, got in ends]


def gather_split(own, size, earlier=()):
    half = own.shape[1] // 2
    state, first, last = [], [], []
    for part, order in zip((own[:, :half], own[:, half:]), bit_orders(size)):
        held, came = {0: part}, []
        for bit in order[::-1]:
            for place in list(held):
                sent = after(held[place], *earlier) if place else held[place]
                held[place ^ bit] = swap(sent, bit, size)
                came.append(held[place ^ bit])
        state.append([(held[place][None], 0) for place in range(size)])
        first.append(came[0])
        last.append(came[-1])
    return state, first, last


def assemble_kernel(cases, shift_ref, *refs):
    out_ref = refs[-1]
    place = pl.program_id(0) ^ shift_ref[0]
    for case, picks in enumerate(cases):

        @pl.when(place == case)
        def _(picks=picks):
            columns = 0
            for at, index in picks:
                part = refs[at][index]
                out_ref[:, columns : columns + part.shape[1]] = part.astype(out_ref.dtype)
                columns += part.shape[1]


def arrays_of(halves):
    arrays, picks = [], []
    for parts in halves:
        picks.append([])
        for array, index in parts:
            known = [at for at, other in enumerate(arrays) if other is array]
            if not known:
                arrays.append(array)
            picks[-1].append((known[0] if known else len(arrays) - 1, index))
    return arrays, picks


def assemble(halves, shift, dtype):
    arrays, picks = arrays_of(halves)
    size = len(picks[0])
    rows = arrays[0].shape[1]
    width = sum(parts[0][0].shape[2] for parts in halves)
    return pl.pallas_call(
        functools.partial(assemble_kernel, list(zip(*picks))),
        grid=(size,),
        in_specs=[pl.BlockSpec(memory_space=pltpu.SMEM)]
        + [pl.BlockSpec(array.shape, lambda r: (0, 0, 0)) for array in arrays],
        out_specs=pl.BlockSpec((rows, width), lambda r: (r, 0)),
        out_shape=jax.ShapeDtypeStruct((size * rows, width), dtype),
        compiler_params=limits(),
        cost_estimate=estimate(
            flops=size * rows * width, bytes_accessed=6 * size * rows * width, transcendentals=0
        ),
    )(shift, *arrays)


def scatter_start(terms, size, width, free=(), together=False):
    if size != 4:
        total = 0.0
        for left, right, at in terms:
            depth = left.shape[1]
            total = total + last_dims(left, right[:, at * depth : (at + 1) * depth])
        return total, [total], [total], [total]
    if together:
        sent, kept = row_products(terms, (1, 0), width)
    else:
        (sent,) = row_products(terms, (1,), width)
        lefts = after([left for left, _, _ in terms], *sent)
        terms = [(left, right, at) for left, (_, right, at) in zip(lefts, terms)]
        (kept,) = row_products(terms, (0,), width)
    if free:
        free = (*free, *kept)
    first = [swap(after(sent[half], *free), 1 + half, size) for half in range(2)]
    return (first, kept), sent, first, kept


def scatter_end(state, size, width, earlier=()):
    if size != 4:
        total = scatter_sum(state.reshape(size, -1, width))
        return total, [total], [total]
    first, kept = state
    first = after(first, *earlier)
    held = [kept[half].astype(F32) + first[half].astype(F32) for half in range(2)]
    sent = [held[half][1].astype(BF) for half in range(2)]
    last = [swap(sent[half], 2 - half, size) for half in range(2)]
    total = [held[half][0] + last[half].astype(F32) for half in range(2)]
    return jnp.concatenate(total, axis=1), sent, last


def input_kernel(picks, sizes, place_ref, hidden_ref, mid_ref, gain_ref, *refs):
    lower = place_ref[2] == 0
    out_ref = refs[-1]
    heads_picks, mine_picks, other_picks = picks
    heads_size, weights_size = sizes
    parts = []
    for weights_picks in (mine_picks, other_picks):
        total = None
        for half, parts_of in enumerate(weights_picks):
            start = half * weights_size
            heads_of = heads_picks[start // heads_size]
            start = start % heads_size
            for (head, row), (weight, place) in zip(heads_of, parts_of):
                left = refs[head][row, :, start : start + weights_size]
                part = last_dims(left, refs[weight][place])
                total = part if total is None else total + part
        parts.append(total)
    grad = jnp.concatenate(
        [jnp.where(lower, parts[0], parts[1]), jnp.where(lower, parts[1], parts[0])], axis=1
    )
    values = hidden_ref[...].astype(F32)
    inverse = lax.rsqrt(jnp.mean(values * values, axis=1, keepdims=True) + epsilon)
    scaled = grad * gain_ref[...]
    inner = jnp.mean(scaled * values, axis=1, keepdims=True)
    out_ref[...] = (
        mid_ref[...].astype(F32) + inverse * scaled - values * (inverse**3 * inner)
    )


def input_gradient(place, heads, mine, other, hidden_in, grad_mid, gain, size):
    length, width = hidden_in.shape
    rows = length // size
    arrays, picks = [], []
    for group in (heads, mine, other):
        more, at = arrays_of(group)
        picks.append([[(len(arrays) + array, index) for array, index in part] for part in at])
        arrays += more
        if group is heads:
            count = len(arrays)
    sizes = (heads[0][0][0].shape[2], mine[0][0][0].shape[2])
    wide = sum(part[0][0].shape[2] for part in heads)
    return pl.pallas_call(
        functools.partial(input_kernel, picks, sizes),
        grid_spec=pltpu.PrefetchScalarGridSpec(
            num_scalar_prefetch=1,
            grid=(size,),
            in_specs=[
                pl.BlockSpec((rows, width), lambda r, place: (r, 0)),
                pl.BlockSpec((rows, width), lambda r, place: (r ^ place[0], 0)),
                pl.BlockSpec((1, width), lambda r, place: (0, 0)),
            ]
            + [
                pl.BlockSpec((array.shape[0], rows, array.shape[2]), lambda r, place: (0, r, 0))
                for array in arrays[:count]
            ]
            + [pl.BlockSpec(array.shape, lambda r, place: (0, 0, 0)) for array in arrays[count:]],
            out_specs=pl.BlockSpec((rows, width), lambda r, place: (r, 0)),
        ),
        out_shape=jax.ShapeDtypeStruct((length, width), F32),
        compiler_params=limits(),
        cost_estimate=estimate(
            flops=2 * length * width * wide * size,
            bytes_accessed=2 * size * wide * (length + width) + 8 * length * width,
            transcendentals=length,
        ),
    )(place, hidden_in, grad_mid, gain[None], *arrays)


def local(
    hidden_in,
    self_out,
    out_grad,
    lengths,
    w_query,
    w_key,
    w_value,
    w_output,
    w_gate,
    w_up,
    w_down,
    attn_gain,
    ffn_gain,
    kv_gain,
):
    me = lax.axis_index("tensor")
    size = lax.axis_size("tensor")
    dp_size = lax.axis_size("dp")
    length, width = hidden_in.shape
    quarter = length // size
    wide, units = w_query.shape[1], w_gate.shape[1]
    early = units * 3 // 4 // 256 * 256
    late = round_up(units - early, 128)

    def columns(array, start, count):
        kept = array[:, start : start + count]
        return jnp.pad(kept, ((0, 0), (0, count - kept.shape[1])))

    w_flip = w_down.T
    mine = [jnp.concatenate([w_query, w_key, w_value, w_output.T], axis=1)]
    for start, count in ((0, early), (early, late)):
        mine.append(
            jnp.concatenate([columns(w, start, count) for w in (w_gate, w_up, w_flip)], axis=1)
        )
    w_heads, w_early, w_late = [lax.all_gather(w, "dp", axis=0, tiled=True) for w in mine]
    gains = lax.all_gather(jnp.stack([attn_gain, ffn_gain, kv_gain]), "dp", axis=1, tiled=True)
    gains = gains.astype(F32)
    attn_scale, ffn_scale, kv_scale = gains[0], gains[1], gains[2]

    core = lax.axis_index("dp") % 2
    place = jnp.stack([me, lengths[0], core])
    valid = jnp.arange(length, dtype=jnp.int32) < lengths[0]
    cosine, sine = rotary_tables(length)
    hidden = hidden_in.astype(F32)
    selfout = self_out.astype(F32)
    x_inverse, x_normed = rms_scale(hidden, attn_scale)
    normed = x_normed.astype(BF)
    s_inverse, s_normed = rms_scale(selfout, kv_scale)
    kv_normed = s_normed.astype(BF)

    def own_rows(array):
        return lax.dynamic_slice_in_dim(array, me * quarter, quarter, 0)

    hidden_own = own_rows(hidden_in).astype(F32)
    self_own = own_rows(self_out).astype(F32)
    grad_y_low = relative(jnp.where(valid[:, None], out_grad, jnp.zeros((), BF)), me, size)
    grad_y = grad_y_low[0].astype(F32)
    grad_y_low = grad_y_low.reshape(length, width)

    queries, keys, values, attended_low, attended_flip = attend_forward(
        place, normed, kv_normed, w_heads, cosine, sine, size
    )
    state, _, _, _ = scatter_start([(attended_low, w_heads, 3)], size, width)
    mid_sum, _, _ = scatter_end(state, size, width)
    mid = hidden_own + mid_sum
    m_inverse, m_normed = rms_scale(mid, ffn_scale)
    held, _ = halves_start(m_normed.astype(BF), size)
    parts, ffn_last = halves_end(held, size)
    still = jnp.zeros((1,), jnp.int32)
    ffn_in = assemble(parts, still, BF)

    half_rows = lax.dynamic_slice_in_dim(w_heads[:, :wide], core * (width // 2), width // 2, 0)
    held, _ = halves_start(after(half_rows, *ffn_last), size)
    query_mine, query_last = halves_end(held, size)

    act_early, gate_early, up_early, flip_early = feed_forward(ffn_in, grad_y_low, w_early)

    def unit_grads(flip):
        return products([(flip, 0, 0), (flip, 1, 0), (flip, 2, 1)], [ffn_in, grad_y_low])

    grads_early = unit_grads(flip_early)
    sum_early = lax.psum_scatter(after(grads_early, w_late, *query_last), "dp", scatter_dimension=1, tiled=True)
    act_late, gate_late, up_late, flip_late = feed_forward(
        after(ffn_in, grads_early), grad_y_low, w_late
    )
    state, _, _, _ = scatter_start(
        [
            (gate_early, w_early, 0),
            (up_early, w_early, 1),
            (gate_late, w_late, 0),
            (up_late, w_late, 1),
        ],
        size,
        width,
    )
    back_sum, _, _ = scatter_end(state, size, width)
    mid_part = norm_back(back_sum, mid, m_inverse, ffn_scale)
    grad_mid = grad_y + mid_part
    mid_low = grad_mid.astype(BF)
    parts, mid_first, mid_last = gather_split(mid_low, size)
    mid_arrays, mid_picks = arrays_of(parts)
    act_early, act_late = after((act_early, act_late), *mid_first)
    out_state, _, out_first, out_kept = scatter_start(
        [(act_early, w_early, 2), (act_late, w_late, 2)], size, width, free=mid_last
    )
    grads_late = unit_grads(after(flip_late, mid_low))
    sum_late = lax.psum_scatter(
        after(grads_late, *mid_first), "dp", scatter_dimension=1, tiled=True
    )
    mid_arrays = after(mid_arrays, grads_late, *out_kept)

    group = head_group(wide)
    groups = wide // group
    backs, heads_held, q_first = [], [], []
    grad_in = mid_arrays
    for at in range(groups):
        backs.append(
            attend_backward(
                place, (grad_in, mid_picks), w_heads, queries, keys, values, cosine, sine, at
            )
        )
        held, first = gather_start(backs[-1][0], size, at % 2)
        heads_held.append(held)
        q_first.append(first)
        grad_in = after(mid_arrays, backs[-1][0])
    kv_terms = [(backs[at][1], w_heads, at + groups) for at in range(groups)]
    kv_terms += [(backs[at][2], w_heads, at + 2 * groups) for at in range(groups)]
    lefts = after([left for left, _, _ in kv_terms], *out_first, *q_first[:-1])
    kv_terms = [(left, right, at) for left, (_, right, at) in zip(lefts, kv_terms)]
    kv_state, kv_sent, kv_first, kv_kept = scatter_start(
        kv_terms, size, width, together=True
    )
    grad_kv_normed, kv_more, kv_last = scatter_end(kv_state, size, width)
    heads_q, q_last = [], []
    for at in range(groups):
        parts, last = gather_end(heads_held[at], size, at % 2, kv_kept)
        heads_q.append(parts)
        q_last.append(last)
    out_sum, out_more, out_last = scatter_end(out_state, size, width, kv_more)
    layer_own = (mid + out_sum).astype(BF)
    layer_held, layer_first = halves_start(layer_own, size)
    layer_parts, _ = halves_end(layer_held, size)
    layer_out = assemble(layer_parts, place, BF)
    grads_heads = products(
        [(backs[at][3], lead, min(lead, 1)) for lead in range(3) for at in range(groups)]
        + [(attended_flip[None], 0, 2)],
        [after(normed, sum_early, *kv_kept), kv_normed, (mid_arrays, mid_picks)],
    )
    mid_parts = [[(mid_arrays[at], index) for at, index in part] for part in mid_picks]
    grad_mid_low = assemble(mid_parts, after(still, *kv_kept), BF)
    grads_heads = after(grads_heads, *kv_first, *q_last, grad_mid_low)
    sum_heads = lax.psum_scatter(grads_heads, "dp", scatter_dimension=1, tiled=True).astype(F32)
    def unit_sums(at):
        early_rows = sum_early[at * early : (at + 1) * early]
        late_rows = sum_late[at * late : at * late + units - early]
        return jnp.concatenate([early_rows, late_rows], axis=0).astype(F32)

    def gain_part(gain, *pairs):
        total = 0.0
        for weights, grads in pairs:
            total = total + jnp.sum(weights.astype(F32) * grads, axis=1)
        return total / gain.astype(F32)

    s_part = norm_back(grad_kv_normed, self_own, own_rows(s_inverse), kv_scale)
    self_own_grad = s_part.astype(BF)
    self_held, self_first = halves_start(self_own_grad, size)

    weights_in = after((w_gate, w_up), *self_first)
    sum_gate, sum_up, sum_down = unit_sums(0).T, unit_sums(1).T, unit_sums(2)
    ffn_gain_sum = gain_part(ffn_gain, (weights_in[0], sum_gate), (weights_in[1], sum_up))


    query_arrays, query_picks = arrays_of(query_mine)
    other_arrays = [
        lax.ppermute(array, "dp", [(i, i ^ 1) for i in range(dp_size)])
        for array in after(query_arrays, *kv_more)
    ]
    query_other = [[(other_arrays[at], index) for at, index in part] for part in query_picks]
    input_grad = input_gradient(
        place,
        heads_q,
        query_mine,
        query_other,
        after(hidden_in, self_own_grad),
        grad_mid_low,
        attn_scale,
        size,
    )
    self_parts, _ = halves_end(self_held, size, [input_grad])
    weights_in = after((w_query, w_key, w_value), *self_first)
    sum_query, sum_key, sum_value = [
        sum_heads[at * wide : (at + 1) * wide].T for at in range(3)
    ]
    gain_sums = jnp.stack(
        [
            gain_part(attn_gain, (weights_in[0], sum_query)),
            ffn_gain_sum,
            gain_part(kv_gain, (weights_in[1], sum_key), (weights_in[2], sum_value)),
        ]
    )
    self_grad = assemble(self_parts, after(place, gain_sums), F32)
    others = [
        lax.ppermute(gain_sums, "tensor", [(t, t ^ step) for t in range(size)])
        for step in range(1, size)
    ]
    for other in others:
        gain_sums = gain_sums + other

    return (
        layer_out,
        input_grad,
        self_grad,
        sum_query,
        sum_key,
        sum_value,
        sum_heads[3 * wide :],
        sum_gate,
        sum_up,
        sum_down,
        gain_sums[0],
        gain_sums[1],
        gain_sums[2],
    )


def solution(mesh):
    placed = (
        P("dp", None),
        P("dp", None),
        P("dp", None),
        P("dp"),
        P("dp", "tensor"),
        P("dp", "tensor"),
        P("dp", "tensor"),
        P("tensor", "dp"),
        P("dp", "tensor"),
        P("dp", "tensor"),
        P("tensor", "dp"),
        P("dp"),
        P("dp"),
        P("dp"),
    )
    return jax.shard_map(
        local,
        mesh=mesh,
        in_specs=placed,
        out_specs=(
            P("dp", None),
            P("dp", None),
            P("dp", None),
            P("dp", "tensor"),
            P("dp", "tensor"),
            P("dp", "tensor"),
            P("tensor", "dp"),
            P("dp", "tensor"),
            P("dp", "tensor"),
            P("tensor", "dp"),
            P("dp"),
            P("dp"),
            P("dp"),
        ),
        check_vma=False,
    )
```

```python
import functools

import jax
import jax.numpy as jnp
from jax import lax
from jax.experimental import pallas as pl
from jax.experimental.pallas import tpu as pltpu
from jax.sharding import PartitionSpec as P

HD = 128
QROWS = 256
BF = jnp.bfloat16
F32 = jnp.float32
epsilon = 1e-06
VMEM_LIMIT = 60 * 1024 * 1024
WEIGHT = 1


def plain_dot(left, right):
    return jnp.dot(left, right, preferred_element_type=jnp.float32)


def last_dims(left, right):
    return lax.dot_general(
        left, right, (((1,), (1,)), ((), ())), preferred_element_type=jnp.float32
    )


def round_up(number, unit):
    return (number + unit - 1) // unit * unit


def head_group(wide):
    return 2 * HD if wide % (2 * HD) == 0 else HD


def limits():
    return pltpu.CompilerParams(vmem_limit_bytes=VMEM_LIMIT)


def estimate(flops, bytes_accessed, transcendentals):
    return pl.CostEstimate(
        flops=flops // WEIGHT,
        bytes_accessed=bytes_accessed // WEIGHT,
        transcendentals=transcendentals // WEIGHT,
    )


def turn(values, cosine, sine):
    return values * cosine + pltpu.roll(values, HD // 2, 1) * sine


def forward_kernel(
    size,
    place_ref,
    normed_ref,
    kv_ref,
    wq_ref,
    wk_ref,
    wv_ref,
    cos_ref,
    sin_ref,
    q_ref,
    k_ref,
    v_ref,
    out_ref,
    flip_ref,
):
    me, live = place_ref[0], place_ref[1]
    length = normed_ref.shape[0]
    group = wq_ref.shape[1]
    part = length // size
    cosine, sine = cos_ref[...], sin_ref[...]
    q_pre = plain_dot(normed_ref[...], wq_ref[...])
    for at in range(0, group, HD):
        q_ref[:, at : at + HD] = turn(q_pre[:, at : at + HD], cosine, sine).astype(BF)
    k_pre = plain_dot(kv_ref[...], wk_ref[...])
    for at in range(0, group, HD):
        k_ref[:, at : at + HD] = turn(k_pre[:, at : at + HD], cosine, sine).astype(BF)
    v_ref[...] = plain_dot(kv_ref[...], wv_ref[...]).astype(BF)
    for at in range(0, group, HD):
        for start in range(0, length, QROWS):
            stop = start + QROWS
            scores = last_dims(q_ref[start:stop, at : at + HD], k_ref[:stop, at : at + HD])
            scores = scores * HD ** (-0.5)
            rows = start + lax.broadcasted_iota(jnp.int32, (QROWS, 1), 0)
            bound = jnp.minimum(rows, live - 1)
            columns = lax.broadcasted_iota(jnp.int32, (QROWS, stop), 1)
            scores = jnp.where(columns <= bound, scores, -1e30)
            largest = jnp.max(scores, axis=1, keepdims=True)
            expo = jnp.exp(scores - largest)
            probs = (expo / jnp.sum(expo, axis=1, keepdims=True)).astype(BF)
            result = plain_dot(probs, v_ref[:stop, at : at + HD])
            flipped = result.T.astype(BF)
            result = result.astype(BF)
            step = min(part, QROWS)
            for piece in range(0, QROWS, step):
                block = (start + piece) // part
                row = pl.multiple_of((block ^ me) * part, part) + (start + piece) % part
                rows_at = pl.ds(pl.multiple_of(row, 128), step)
                out_ref[rows_at, at : at + HD] = result[piece : piece + step]
                flip_ref[at : at + HD, rows_at] = flipped[:, piece : piece + step]


def attend_forward(place, normed, kv_normed, weights, cosine, sine, size):
    length, width = normed.shape
    wide = weights.shape[1] // 4
    group = head_group(wide)
    groups = wide // group
    whole = pl.BlockSpec((length, width), lambda g: (0, 0))
    table = pl.BlockSpec((length, HD), lambda g: (0, 0))
    heads = pl.BlockSpec((length, group), lambda g: (0, g))
    out = jax.ShapeDtypeStruct((length, wide), BF)
    return pl.pallas_call(
        functools.partial(forward_kernel, size),
        grid=(groups,),
        in_specs=[
            pl.BlockSpec(memory_space=pltpu.SMEM),
            whole,
            whole,
            pl.BlockSpec((width, group), lambda g: (0, g)),
            pl.BlockSpec((width, group), lambda g: (0, g + groups)),
            pl.BlockSpec((width, group), lambda g: (0, g + 2 * groups)),
            table,
            table,
        ],
        out_specs=[heads] * 4 + [pl.BlockSpec((group, length), lambda g: (g, 0))],
        out_shape=[out] * 4 + [jax.ShapeDtypeStruct((wide, length), BF)],
        compiler_params=limits(),
        cost_estimate=estimate(
            flops=6 * length * width * wide + 3 * length * length * wide,
            bytes_accessed=4 * length * width + 6 * width * wide + 8 * length * wide,
            transcendentals=length * length * wide // HD,
        ),
    )(place, normed, kv_normed, weights, weights, weights, cosine, sine)


def backward_kernel(
    picks,
    place_ref,
    wo_ref,
    q_ref,
    k_ref,
    v_ref,
    cos_ref,
    sin_ref,
    *refs,
):
    gq_ref, rk_ref, rv_ref, flip_ref, ga_ref, kt_ref, sum_k, sum_v = refs[-8:]
    me, live = place_ref[0], place_ref[1]
    length = q_ref.shape[0]
    size = len(picks[0])
    group = wo_ref.shape[1]
    part = length // size
    scale = HD ** (-0.5)
    cosine, sine = cos_ref[...], -sin_ref[...]

    def home(row):
        block = row // part
        return pl.multiple_of(pl.multiple_of((block ^ me) * part, part) + row % part, 128)

    for block in range(size):
        total, start = None, 0
        for half in picks:
            array, index = half[block]
            stop = start + refs[array].shape[2]
            term = plain_dot(refs[array][index], wo_ref[start:stop, :])
            total = term if total is None else total + term
            start = stop
        ga_ref[pl.ds(home(block * part), part), :] = total.astype(BF)
    for at in range(0, group, HD):
        kt_ref[...] = k_ref[:, at : at + HD].T
        for start in reversed(range(0, length, QROWS)):
            stop = start + QROWS
            queries = q_ref[start:stop, at : at + HD]
            grads = ga_ref[start:stop, at : at + HD]
            scores = last_dims(k_ref[:stop, at : at + HD], queries) * scale
            columns = start + lax.broadcasted_iota(jnp.int32, (1, QROWS), 1)
            bound = jnp.minimum(columns, live - 1)
            rows = lax.broadcasted_iota(jnp.int32, (stop, QROWS), 0)
            scores = jnp.where(rows <= bound, scores, -1e30)
            largest = jnp.max(scores, axis=0, keepdims=True)
            expo = jnp.exp(scores - largest)
            probs = expo * (1.0 / jnp.sum(expo, axis=0, keepdims=True))
            grad_probs = last_dims(v_ref[:stop, at : at + HD], grads)
            inner = jnp.sum(probs * grad_probs, axis=0, keepdims=True)
            grad_scores = (probs * (grad_probs - inner)).astype(BF)
            add_k = plain_dot(grad_scores, queries)
            add_v = plain_dot(probs.astype(BF), grads)
            if stop == length:
                sum_k[...] = add_k
                sum_v[...] = add_v
            else:
                sum_k[:stop] += add_k
                sum_v[:stop] += add_v
            grad_q = plain_dot(kt_ref[:, :stop], grad_scores).T * scale
            grad_q = turn(grad_q, cosine[start:stop], sine[start:stop])
            flip_ref[0, at : at + HD, start:stop] = grad_q.T.astype(BF)
            gq_ref[start:stop, at : at + HD] = grad_q.astype(BF)
        grad_k = turn(sum_k[...] * scale, cosine, sine)
        grad_v = sum_v[...]
        flip_ref[1, at : at + HD, :] = grad_k.T.astype(BF)
        flip_ref[2, at : at + HD, :] = grad_v.T.astype(BF)
        grad_k, grad_v = grad_k.astype(BF), grad_v.astype(BF)
        for block in range(size):
            rows = slice(block * part, (block + 1) * part)
            rk_ref[pl.ds(home(block * part), part), at : at + HD] = grad_k[rows]
            rv_ref[pl.ds(home(block * part), part), at : at + HD] = grad_v[rows]


def attend_backward(place, grads, weights, queries, keys, values, cosine, sine, at):
    arrays, picks = grads
    length, wide = queries.shape
    width = weights.shape[0]
    group = head_group(wide)
    groups = wide // group
    table = pl.BlockSpec((length, HD), lambda g: (0, 0))
    heads = pl.BlockSpec((length, group), lambda g: (0, at))
    outs = pl.BlockSpec((length, group), lambda g: (0, 0))
    out = jax.ShapeDtypeStruct((length, group), BF)
    return pl.pallas_call(
        functools.partial(backward_kernel, picks),
        grid=(1,),
        in_specs=[
            pl.BlockSpec(memory_space=pltpu.SMEM),
            pl.BlockSpec((width, group), lambda g: (0, at + 3 * groups)),
            heads,
            heads,
            heads,
            table,
            table,
        ]
        + [pl.BlockSpec(array.shape, lambda g: (0, 0, 0)) for array in arrays],
        out_specs=[outs] * 3 + [pl.BlockSpec((3, group, length), lambda g: (0, 0, 0))],
        out_shape=[out] * 3 + [jax.ShapeDtypeStruct((3, group, length), BF)],
        scratch_shapes=[
            pltpu.VMEM((length, group), BF),
            pltpu.VMEM((HD, length), BF),
            pltpu.VMEM((length, HD), F32),
            pltpu.VMEM((length, HD), F32),
        ],
        compiler_params=limits(),
        cost_estimate=estimate(
            flops=2 * length * width * group + 10 * length * length * group,
            bytes_accessed=2 * length * width + 2 * width * group + 18 * length * group,
            transcendentals=length * length * group // HD,
        ),
    )(place, weights, queries, keys, values, cosine, sine, *arrays)


def feed_kernel(x_ref, g_ref, wg_ref, wu_ref, wd_ref, act_ref, gate_ref, up_ref, flip_ref):
    gate = plain_dot(x_ref[...], wg_ref[...])
    up = plain_dot(x_ref[...], wu_ref[...])
    grad = plain_dot(g_ref[...], wd_ref[...])
    sigma = 1.0 / (1.0 + jnp.exp(-gate))
    silu = gate * sigma
    act = silu * up
    grad_up = grad * silu
    grad_gate = grad * up * (sigma + silu * (1.0 - sigma))
    act_ref[...] = act.astype(BF)
    up_ref[...] = grad_up.astype(BF)
    gate_ref[...] = grad_gate.astype(BF)
    flip_ref[0] = grad_gate.T.astype(BF)
    flip_ref[1] = grad_up.T.astype(BF)
    flip_ref[2] = act.T.astype(BF)


def feed_forward(ffn_in, grad_low, weights):
    length, width = ffn_in.shape
    units = weights.shape[1] // 3
    step = 256 if units % 256 == 0 else units if units <= 512 else 128
    steps = units // step
    whole = pl.BlockSpec((length, width), lambda f: (0, 0))
    out = pl.BlockSpec((length, step), lambda f: (0, f))
    return pl.pallas_call(
        feed_kernel,
        grid=(steps,),
        in_specs=[
            whole,
            whole,
            pl.BlockSpec((width, step), lambda f: (0, f)),
            pl.BlockSpec((width, step), lambda f: (0, f + steps)),
            pl.BlockSpec((width, step), lambda f: (0, f + 2 * steps)),
        ],
        out_specs=[out] * 3 + [pl.BlockSpec((3, step, length), lambda f: (0, f, 0))],
        out_shape=[jax.ShapeDtypeStruct((length, units), BF)] * 3
        + [jax.ShapeDtypeStruct((3, units, length), BF)],
        compiler_params=limits(),
        cost_estimate=estimate(
            flops=6 * length * width * units,
            bytes_accessed=4 * length * width + 6 * width * units + 12 * length * units,
            transcendentals=2 * length * units,
        ),
    )(ffn_in, grad_low, weights, weights, weights)


def products_kernel(counts, forms, *refs):
    step = pl.program_id(0)
    lefts, rights, out_ref = refs[: len(counts)], refs[len(counts) : -1], refs[-1]
    first = 0
    for (steps, right), left in zip(counts, lefts):

        @pl.when((step >= first) & (step < first + steps))
        def _(left=left, form=forms[right]):
            if isinstance(form, int):
                out_ref[...] = plain_dot(left[...], rights[form][...]).astype(BF)
                return
            start = 0
            for half in form:
                total = None
                for place, (array, index) in enumerate(half):
                    rows, columns = rights[array].shape[1:]
                    part = plain_dot(
                        left[:, place * rows : (place + 1) * rows], rights[array][index]
                    )
                    total = part if total is None else total + part
                out_ref[:, start : start + columns] = total.astype(BF)
                start += columns

        first += steps


def products(terms, rights):
    length = terms[0][0].shape[2]
    width = rights[0].shape[1]
    step = 256 if all(left.shape[1] % 256 == 0 for left, _, _ in terms) else 128
    counts = tuple((left.shape[1] // step, at) for left, _, at in terms)
    total = sum(steps for steps, _ in counts)
    arrays, forms = [], []
    for right in rights:
        if isinstance(right, tuple):
            more, picks = right
            forms.append([[(len(arrays) + at, index) for at, index in half] for half in picks])
            arrays += more
        else:
            forms.append(len(arrays))
            arrays.append(right)
    left_specs = []
    first = 0
    for (steps, _), (_, lead, _) in zip(counts, terms):

        def block(i, first=first, last=steps - 1, lead=lead):
            return (lead, lax.max(lax.min(i - first, last), 0), 0)

        left_specs.append(pl.BlockSpec((None, step, length), block))
        first += steps
    right_specs = [
        pl.BlockSpec(array.shape, lambda i, ndim=array.ndim: (0,) * ndim) for array in arrays
    ]
    return pl.pallas_call(
        functools.partial(products_kernel, counts, forms),
        grid=(total,),
        in_specs=left_specs + right_specs,
        out_specs=pl.BlockSpec((step, width), lambda i: (i, 0)),
        out_shape=jax.ShapeDtypeStruct((total * step, width), BF),
        compiler_params=limits(),
        cost_estimate=estimate(
            flops=2 * total * step * length * width,
            bytes_accessed=2 * (total * step * (length + width) + len(rights) * length * width),
            transcendentals=0,
        ),
    )(*[left for left, _, _ in terms], *arrays)


def rows_kernel(count, sides, steps, *refs):
    outs = refs[-2 * len(sides) :]
    lefts, rights = refs[: -2 * len(sides) - count], refs[-2 * len(sides) - count : -2 * len(sides)]
    for half in range(2):

        @pl.when(pl.program_id(0) // steps == half)
        def _(half=half):
            for number, side in enumerate(sides):
                for piece in range(2):
                    if len(sides) == 1:
                        row, parts = piece, 2
                    else:
                        row, parts = (2 * side + piece if half else 2 * piece + side), 4
                    total = None
                    for at, right in enumerate(rights):
                        part = last_dims(lefts[parts * at + row][...], right[...])
                        total = part if total is None else total + part
                    outs[2 * number + half][piece] = total.astype(BF)


def row_products(terms, sides, width):
    columns = width // 2
    step = 512 if columns % 512 == 0 else columns
    steps = columns // step
    left_specs, right_specs, lefts, rights = [], [], [], []
    flops = nbytes = 0
    for left, right, at in terms:
        rows, depth = left.shape[0] // 4, left.shape[1]
        for piece in range(2 * len(sides)):

            def block(j, piece=piece):
                if len(sides) == 2:
                    return (piece, 0)
                upper, side = j // steps, sides[0]
                return ((1 - upper) * (2 * piece + side) + upper * (2 * side + piece), 0)

            lefts.append(left)
            left_specs.append(pl.BlockSpec((rows, depth), block))
        right_specs.append(pl.BlockSpec((step, depth), lambda j, at=at: (j, at)))
        rights.append(right)
        flops += 8 * rows * depth * columns * len(sides)
        nbytes += 4 * depth * (2 * rows + columns)
    outs = pl.pallas_call(
        functools.partial(rows_kernel, len(terms), sides, steps),
        grid=(2 * steps,),
        in_specs=left_specs + right_specs,
        out_specs=[
            pl.BlockSpec((2, rows, step), lambda j: (0, 0, lax.min(j, steps - 1))),
            pl.BlockSpec((2, rows, step), lambda j: (0, 0, lax.max(j - steps, 0))),
        ]
        * len(sides),
        out_shape=[jax.ShapeDtypeStruct((2, rows, columns), BF)] * (2 * len(sides)),
        compiler_params=limits(),
        cost_estimate=estimate(
            flops=flops,
            bytes_accessed=nbytes + 8 * rows * columns * len(sides),
            transcendentals=0,
        ),
    )(*lefts, *rights)
    return [outs[2 * number : 2 * number + 2] for number in range(len(sides))]


def rms_scale(values, gain):
    inverse = lax.rsqrt(jnp.mean(values * values, axis=-1, keepdims=True) + epsilon)
    return (inverse, values * inverse * gain)


def norm_back(grad, values, inverse, gain):
    scaled = grad * gain
    inner = jnp.mean(scaled * values, axis=-1, keepdims=True)
    return inverse * scaled - values * inverse**3 * inner


def rotary_tables(length):
    position = jnp.arange(length, dtype=jnp.float32)
    freqs = jnp.exp(-jnp.log(10000.0) * jnp.arange(HD // 2, dtype=jnp.float32) * 2.0 / HD)
    angle = position[:, None] * freqs[None, :]
    cosine, sine = jnp.cos(angle), jnp.sin(angle)
    return (jnp.concatenate([cosine, cosine], 1), jnp.concatenate([-sine, sine], 1))


def after(value, *earlier):
    return lax.optimization_barrier((value, *earlier))[0]


def swap(array, bit, size):
    return lax.ppermute(array, "tensor", [(t, t ^ bit) for t in range(size)])


def bit_orders(size):
    bits = [1 << step for step in range(size.bit_length() - 1)]
    return (bits, bits[1:] + bits[:1])


def relative(array, me, size):
    part = array.shape[0] // size
    return jnp.stack(
        [lax.dynamic_slice_in_dim(array, (me ^ step) * part, part, 0) for step in range(size)]
    )


def scatter_sum(blocks):
    size = blocks.shape[0]
    half = blocks.shape[2] // 2
    sums = []
    for group, order in enumerate(bit_orders(size)):
        held = {
            place: blocks[place, :, group * half : (group + 1) * half].astype(F32)
            for place in range(size)
        }
        for bit in order:
            sent = [place for place in held if place & bit]
            got = swap(jnp.stack([held[place].astype(BF) for place in sent]), bit, size)
            held = {
                place ^ bit: held[place ^ bit] + got[at].astype(F32)
                for at, place in enumerate(sent)
            }
        sums.append(held[0])
    return jnp.concatenate(sums, axis=1)


def gather_start(own, size, group):
    return gather_step({0: (own[None], 0)}, bit_orders(size)[group][-1], size)


def gather_step(held, bit, size, earlier=()):
    places = list(held)
    sent = after([held[place][0][held[place][1]] for place in places], *earlier)
    got = swap(jnp.stack(sent), bit, size)
    return {**held, **{place ^ bit: (got, at) for at, place in enumerate(places)}}, got


def gather_end(held, size, group, earlier=()):
    got = None
    for bit in bit_orders(size)[group][-2::-1]:
        held, got = gather_step(held, bit, size, earlier)
    return [held[place] for place in range(size)], got


def halves_start(own, size):
    half = own.shape[1] // 2
    parts = (own[:, :half], own[:, half:])
    state = [gather_start(part, size, group) for group, part in enumerate(parts)]
    return [held for held, _ in state], [got for _, got in state]


def halves_end(state, size, earlier=()):
    ends = [gather_end(held, size, group, earlier) for group, held in enumerate(state)]
    return [parts for parts, _ in ends], [got for _, got in ends]


def gather_split(own, size, earlier=()):
    half = own.shape[1] // 2
    state, first, last = [], [], []
    for part, order in zip((own[:, :half], own[:, half:]), bit_orders(size)):
        held, came = {0: part}, []
        for bit in order[::-1]:
            for place in list(held):
                sent = after(held[place], *earlier) if place else held[place]
                held[place ^ bit] = swap(sent, bit, size)
                came.append(held[place ^ bit])
        state.append([(held[place][None], 0) for place in range(size)])
        first.append(came[0])
        last.append(came[-1])
    return state, first, last


def assemble_kernel(cases, shift_ref, *refs):
    out_ref = refs[-1]
    place = pl.program_id(0) ^ shift_ref[0]
    for case, picks in enumerate(cases):

        @pl.when(place == case)
        def _(picks=picks):
            columns = 0
            for at, index in picks:
                part = refs[at][index]
                out_ref[:, columns : columns + part.shape[1]] = part.astype(out_ref.dtype)
                columns += part.shape[1]


def arrays_of(halves):
    arrays, picks = [], []
    for parts in halves:
        picks.append([])
        for array, index in parts:
            known = [at for at, other in enumerate(arrays) if other is array]
            if not known:
                arrays.append(array)
            picks[-1].append((known[0] if known else len(arrays) - 1, index))
    return arrays, picks


def assemble(halves, shift, dtype):
    arrays, picks = arrays_of(halves)
    size = len(picks[0])
    rows = arrays[0].shape[1]
    width = sum(parts[0][0].shape[2] for parts in halves)
    return pl.pallas_call(
        functools.partial(assemble_kernel, list(zip(*picks))),
        grid=(size,),
        in_specs=[pl.BlockSpec(memory_space=pltpu.SMEM)]
        + [pl.BlockSpec(array.shape, lambda r: (0, 0, 0)) for array in arrays],
        out_specs=pl.BlockSpec((rows, width), lambda r: (r, 0)),
        out_shape=jax.ShapeDtypeStruct((size * rows, width), dtype),
        compiler_params=limits(),
        cost_estimate=estimate(
            flops=size * rows * width, bytes_accessed=6 * size * rows * width, transcendentals=0
        ),
    )(shift, *arrays)


def scatter_start(terms, size, width, free=(), together=False):
    if size != 4:
        total = 0.0
        for left, right, at in terms:
            depth = left.shape[1]
            total = total + last_dims(left, right[:, at * depth : (at + 1) * depth])
        return total, [total], [total], [total]
    if together:
        sent, kept = row_products(terms, (1, 0), width)
    else:
        (sent,) = row_products(terms, (1,), width)
        lefts = after([left for left, _, _ in terms], *sent)
        terms = [(left, right, at) for left, (_, right, at) in zip(lefts, terms)]
        (kept,) = row_products(terms, (0,), width)
    if free:
        free = (*free, *kept)
    first = [swap(after(sent[half], *free), 1 + half, size) for half in range(2)]
    return (first, kept), sent, first, kept


def scatter_end(state, size, width, earlier=()):
    if size != 4:
        total = scatter_sum(state.reshape(size, -1, width))
        return total, [total], [total]
    first, kept = state
    first = after(first, *earlier)
    held = [kept[half].astype(F32) + first[half].astype(F32) for half in range(2)]
    sent = [held[half][1].astype(BF) for half in range(2)]
    last = [swap(sent[half], 2 - half, size) for half in range(2)]
    total = [held[half][0] + last[half].astype(F32) for half in range(2)]
    return jnp.concatenate(total, axis=1), sent, last


def input_kernel(picks, sizes, place_ref, hidden_ref, mid_ref, gain_ref, *refs):
    lower = place_ref[2] == 0
    out_ref = refs[-1]
    heads_picks, mine_picks, other_picks = picks
    heads_size, weights_size = sizes
    parts = []
    for weights_picks in (mine_picks, other_picks):
        total = None
        for half, parts_of in enumerate(weights_picks):
            start = half * weights_size
            heads_of = heads_picks[start // heads_size]
            start = start % heads_size
            for (head, row), (weight, place) in zip(heads_of, parts_of):
                left = refs[head][row, :, start : start + weights_size]
                part = last_dims(left, refs[weight][place])
                total = part if total is None else total + part
        parts.append(total)
    grad = jnp.concatenate(
        [jnp.where(lower, parts[0], parts[1]), jnp.where(lower, parts[1], parts[0])], axis=1
    )
    values = hidden_ref[...].astype(F32)
    inverse = lax.rsqrt(jnp.mean(values * values, axis=1, keepdims=True) + epsilon)
    scaled = grad * gain_ref[...]
    inner = jnp.mean(scaled * values, axis=1, keepdims=True)
    out_ref[...] = (
        mid_ref[...].astype(F32) + inverse * scaled - values * (inverse**3 * inner)
    )


def input_gradient(place, heads, mine, other, hidden_in, grad_mid, gain, size):
    length, width = hidden_in.shape
    rows = length // size
    arrays, picks = [], []
    for group in (heads, mine, other):
        more, at = arrays_of(group)
        picks.append([[(len(arrays) + array, index) for array, index in part] for part in at])
        arrays += more
        if group is heads:
            count = len(arrays)
    sizes = (heads[0][0][0].shape[2], mine[0][0][0].shape[2])
    wide = sum(part[0][0].shape[2] for part in heads)
    return pl.pallas_call(
        functools.partial(input_kernel, picks, sizes),
        grid_spec=pltpu.PrefetchScalarGridSpec(
            num_scalar_prefetch=1,
            grid=(size,),
            in_specs=[
                pl.BlockSpec((rows, width), lambda r, place: (r, 0)),
                pl.BlockSpec((rows, width), lambda r, place: (r ^ place[0], 0)),
                pl.BlockSpec((1, width), lambda r, place: (0, 0)),
            ]
            + [
                pl.BlockSpec((array.shape[0], rows, array.shape[2]), lambda r, place: (0, r, 0))
                for array in arrays[:count]
            ]
            + [pl.BlockSpec(array.shape, lambda r, place: (0, 0, 0)) for array in arrays[count:]],
            out_specs=pl.BlockSpec((rows, width), lambda r, place: (r, 0)),
        ),
        out_shape=jax.ShapeDtypeStruct((length, width), F32),
        compiler_params=limits(),
        cost_estimate=estimate(
            flops=2 * length * width * wide * size,
            bytes_accessed=2 * size * wide * (length + width) + 8 * length * width,
            transcendentals=length,
        ),
    )(place, hidden_in, grad_mid, gain[None], *arrays)


def local(
    hidden_in,
    self_out,
    out_grad,
    lengths,
    w_query,
    w_key,
    w_value,
    w_output,
    w_gate,
    w_up,
    w_down,
    attn_gain,
    ffn_gain,
    kv_gain,
):
    me = lax.axis_index("tensor")
    size = lax.axis_size("tensor")
    dp_size = lax.axis_size("dp")
    length, width = hidden_in.shape
    quarter = length // size
    wide, units = w_query.shape[1], w_gate.shape[1]
    early = units * 3 // 4 // 256 * 256
    late = round_up(units - early, 128)

    def columns(array, start, count):
        kept = array[:, start : start + count]
        return jnp.pad(kept, ((0, 0), (0, count - kept.shape[1])))

    w_flip = w_down.T
    mine = [jnp.concatenate([w_query, w_key, w_value, w_output.T], axis=1)]
    for start, count in ((0, early), (early, late)):
        mine.append(
            jnp.concatenate([columns(w, start, count) for w in (w_gate, w_up, w_flip)], axis=1)
        )
    w_heads, w_early, w_late = [lax.all_gather(w, "dp", axis=0, tiled=True) for w in mine]
    gains = lax.all_gather(jnp.stack([attn_gain, ffn_gain, kv_gain]), "dp", axis=1, tiled=True)
    gains = gains.astype(F32)
    attn_scale, ffn_scale, kv_scale = gains[0], gains[1], gains[2]

    core = lax.axis_index("dp") % 2
    place = jnp.stack([me, lengths[0], core])
    valid = jnp.arange(length, dtype=jnp.int32) < lengths[0]
    cosine, sine = rotary_tables(length)
    hidden = hidden_in.astype(F32)
    selfout = self_out.astype(F32)
    x_inverse, x_normed = rms_scale(hidden, attn_scale)
    normed = x_normed.astype(BF)
    s_inverse, s_normed = rms_scale(selfout, kv_scale)
    kv_normed = s_normed.astype(BF)

    def own_rows(array):
        return lax.dynamic_slice_in_dim(array, me * quarter, quarter, 0)

    hidden_own = own_rows(hidden_in).astype(F32)
    self_own = own_rows(self_out).astype(F32)
    grad_y_low = relative(jnp.where(valid[:, None], out_grad, jnp.zeros((), BF)), me, size)
    grad_y = grad_y_low[0].astype(F32)
    grad_y_low = grad_y_low.reshape(length, width)

    queries, keys, values, attended_low, attended_flip = attend_forward(
        place, normed, kv_normed, w_heads, cosine, sine, size
    )
    state, _, _, _ = scatter_start([(attended_low, w_heads, 3)], size, width)
    mid_sum, _, _ = scatter_end(state, size, width)
    mid = hidden_own + mid_sum
    m_inverse, m_normed = rms_scale(mid, ffn_scale)
    held, _ = halves_start(m_normed.astype(BF), size)
    parts, ffn_last = halves_end(held, size)
    still = jnp.zeros((1,), jnp.int32)
    ffn_in = assemble(parts, still, BF)

    half_rows = lax.dynamic_slice_in_dim(w_heads[:, :wide], core * (width // 2), width // 2, 0)
    held, _ = halves_start(after(half_rows, *ffn_last), size)
    query_mine, query_last = halves_end(held, size)

    act_early, gate_early, up_early, flip_early = feed_forward(ffn_in, grad_y_low, w_early)

    def unit_grads(flip):
        return products([(flip, 0, 0), (flip, 1, 0), (flip, 2, 1)], [ffn_in, grad_y_low])

    grads_early = unit_grads(flip_early)
    sum_early = lax.psum_scatter(after(grads_early, w_late, *query_last), "dp", scatter_dimension=1, tiled=True)
    act_late, gate_late, up_late, flip_late = feed_forward(
        after(ffn_in, grads_early), grad_y_low, w_late
    )
    state, _, _, _ = scatter_start(
        [
            (gate_early, w_early, 0),
            (up_early, w_early, 1),
            (gate_late, w_late, 0),
            (up_late, w_late, 1),
        ],
        size,
        width,
    )
    back_sum, _, _ = scatter_end(state, size, width)
    mid_part = norm_back(back_sum, mid, m_inverse, ffn_scale)
    grad_mid = grad_y + mid_part
    mid_low = grad_mid.astype(BF)
    parts, mid_first, mid_last = gather_split(mid_low, size)
    mid_arrays, mid_picks = arrays_of(parts)
    act_early, act_late = after((act_early, act_late), *mid_first)
    out_state, _, out_first, out_kept = scatter_start(
        [(act_early, w_early, 2), (act_late, w_late, 2)], size, width, free=mid_last
    )
    grads_late = unit_grads(after(flip_late, mid_low))
    sum_late = lax.psum_scatter(
        after(grads_late, *mid_first), "dp", scatter_dimension=1, tiled=True
    )
    mid_arrays = after(mid_arrays, grads_late, *out_kept)

    group = head_group(wide)
    groups = wide // group
    backs, heads_held, q_first = [], [], []
    grad_in = mid_arrays
    for at in range(groups):
        backs.append(
            attend_backward(
                place, (grad_in, mid_picks), w_heads, queries, keys, values, cosine, sine, at
            )
        )
        held, first = gather_start(backs[-1][0], size, at % 2)
        heads_held.append(held)
        q_first.append(first)
        grad_in = after(mid_arrays, backs[-1][0])
    kv_terms = [(backs[at][1], w_heads, at + groups) for at in range(groups)]
    kv_terms += [(backs[at][2], w_heads, at + 2 * groups) for at in range(groups)]
    lefts = after([left for left, _, _ in kv_terms], *out_first, *q_first[:-1])
    kv_terms = [(left, right, at) for left, (_, right, at) in zip(lefts, kv_terms)]
    kv_state, kv_sent, kv_first, kv_kept = scatter_start(
        kv_terms, size, width, together=True
    )
    grad_kv_normed, kv_more, kv_last = scatter_end(kv_state, size, width)
    heads_q, q_last = [], []
    for at in range(groups):
        parts, last = gather_end(heads_held[at], size, at % 2, kv_kept)
        heads_q.append(parts)
        q_last.append(last)
    out_sum, out_more, out_last = scatter_end(out_state, size, width, kv_more)
    layer_own = (mid + out_sum).astype(BF)
    layer_held, layer_first = halves_start(layer_own, size)
    layer_parts, layer_last = halves_end(layer_held, size)
    layer_out = assemble(layer_parts, place, BF)
    grads_heads = products(
        [(backs[at][3], lead, min(lead, 1)) for lead in range(3) for at in range(groups)]
        + [(attended_flip[None], 0, 2)],
        [after(normed, sum_early, *kv_kept), kv_normed, (mid_arrays, mid_picks)],
    )
    mid_parts = [[(mid_arrays[at], index) for at, index in part] for part in mid_picks]
    grad_mid_low = assemble(mid_parts, after(still, *kv_kept), BF)
    grads_heads = after(grads_heads, *kv_first, *q_last, grad_mid_low)
    sum_heads = lax.psum_scatter(grads_heads, "dp", scatter_dimension=1, tiled=True).astype(F32)
    def unit_sums(at):
        early_rows = sum_early[at * early : (at + 1) * early]
        late_rows = sum_late[at * late : at * late + units - early]
        return jnp.concatenate([early_rows, late_rows], axis=0).astype(F32)

    def gain_part(gain, *pairs):
        total = 0.0
        for weights, grads in pairs:
            total = total + jnp.sum(weights.astype(F32) * grads, axis=1)
        return total / gain.astype(F32)

    s_part = norm_back(grad_kv_normed, self_own, own_rows(s_inverse), kv_scale)
    self_own_grad = s_part.astype(BF)
    self_held, self_first = halves_start(self_own_grad, size)

    weights_in = after((w_gate, w_up), *layer_last)
    sum_gate, sum_up, sum_down = unit_sums(0).T, unit_sums(1).T, unit_sums(2)
    ffn_gain_sum = gain_part(ffn_gain, (weights_in[0], sum_gate), (weights_in[1], sum_up))


    query_arrays, query_picks = arrays_of(query_mine)
    other_arrays = [
        lax.ppermute(array, "dp", [(i, i ^ 1) for i in range(dp_size)])
        for array in after(query_arrays, *kv_more)
    ]
    query_other = [[(other_arrays[at], index) for at, index in part] for part in query_picks]
    input_grad = input_gradient(
        place,
        heads_q,
        query_mine,
        query_other,
        after(hidden_in, self_own_grad),
        grad_mid_low,
        attn_scale,
        size,
    )
    self_parts, _ = halves_end(self_held, size, [input_grad])
    weights_in = after((w_query, w_key, w_value), *layer_last)
    sum_query, sum_key, sum_value = [
        sum_heads[at * wide : (at + 1) * wide].T for at in range(3)
    ]
    gain_sums = jnp.stack(
        [
            gain_part(attn_gain, (weights_in[0], sum_query)),
            ffn_gain_sum,
            gain_part(kv_gain, (weights_in[1], sum_key), (weights_in[2], sum_value)),
        ]
    )
    self_grad = assemble(self_parts, after(place, gain_sums), F32)
    others = [
        lax.ppermute(gain_sums, "tensor", [(t, t ^ step) for t in range(size)])
        for step in range(1, size)
    ]
    for other in others:
        gain_sums = gain_sums + other

    return (
        layer_out,
        input_grad,
        self_grad,
        sum_query,
        sum_key,
        sum_value,
        sum_heads[3 * wide :],
        sum_gate,
        sum_up,
        sum_down,
        gain_sums[0],
        gain_sums[1],
        gain_sums[2],
    )


def solution(mesh):
    placed = (
        P("dp", None),
        P("dp", None),
        P("dp", None),
        P("dp"),
        P("dp", "tensor"),
        P("dp", "tensor"),
        P("dp", "tensor"),
        P("tensor", "dp"),
        P("dp", "tensor"),
        P("dp", "tensor"),
        P("tensor", "dp"),
        P("dp"),
        P("dp"),
        P("dp"),
    )
    return jax.shard_map(
        local,
        mesh=mesh,
        in_specs=placed,
        out_specs=(
            P("dp", None),
            P("dp", None),
            P("dp", None),
            P("dp", "tensor"),
            P("dp", "tensor"),
            P("dp", "tensor"),
            P("tensor", "dp"),
            P("dp", "tensor"),
            P("dp", "tensor"),
            P("tensor", "dp"),
            P("dp"),
            P("dp"),
            P("dp"),
        ),
        check_vma=False,
    )
```
